32 devices in a mesh: row: 4 (over z), col: 8 (over y, x, core).
Axes of the slice: x: 2, y: 2, z: 4, core: 2. Of those that a mesh axis runs over, the one named last changes fastest.
Arguments:
- block_in: bfloat16 [4, 1024, 2048], P(None, 'row', 'col'), may hold values from -6 to 6
- grad_out: bfloat16 [4, 1024, 2048], P(None, 'row', 'col'), may hold values from -6 to 6
- gain_attn: float32 [2048], replicated, may hold values from 0.25 to 1.75
- gain_ffn: float32 [2048], replicated, may hold values from 0.25 to 1.75
- router_attn: bfloat16 [2048, 8], replicated, may hold values from -0.125 to 0.125
- router_ffn: bfloat16 [2048, 8], replicated, may hold values from -0.125 to 0.125
- w_query: bfloat16 [8, 2048, 2048], P(None, 'row', 'col'), may hold values from -0.125 to 0.125
- key_weight: bfloat16 [2048, 2048], P('row', 'col'), may hold values from -0.125 to 0.125
- value_weight: bfloat16 [2048, 2048], P('row', 'col'), may hold values from -0.125 to 0.125
- w_out: bfloat16 [8, 2048, 2048], P(None, 'col', 'row'), may hold values from -0.75 to 0.75
- w_gate: bfloat16 [8, 2048, 5632], P(None, 'row', 'col'), may hold values from -0.125 to 0.125
- w_up: bfloat16 [8, 2048, 5632], P(None, 'row', 'col'), may hold values from -0.125 to 0.125
- w_down: bfloat16 [8, 5632, 2048], P(None, 'col', 'row'), may hold values from -0.078125 to 0.078125
- routes_attn: int32 [4, 1024, 2], P(None, 'row'), may hold values from 0 to 7, all different within a row
- routes_ffn: int32 [4, 1024, 2], P(None, 'row'), may hold values from 0 to 7, all different within a row
- order_attn: int32 [4, 4, 512], P(None, 'row'), may hold values from 0 to 511, each once within a row
- order_ffn: int32 [4, 4, 512], P(None, 'row'), may hold values from 0 to 511, each once within a row
- block_ids: int32 [4, 1024], replicated, may hold values from 0 to 9, never falling along the last dimension, each value on 1 to 256 neighbouring positions
Outputs:
- block_out: bfloat16 [4, 1024, 2048], P(None, 'row', 'col')
- grad_in: float32 [4, 1024, 2048], P(None, 'row', 'col')
- grad_gain_attn: float32 [2048], replicated
- grad_gain_ffn: float32 [2048], replicated
- grad_router_attn: float32 [2048, 8], replicated
- grad_router_ffn: float32 [2048, 8], replicated
- grad_w_query: float32 [8, 2048, 2048], P(None, 'row', 'col')
- grad_w_key: float32 [2048, 2048], P('row', 'col')
- grad_w_value: float32 [2048, 2048], P('row', 'col')
- grad_w_out: float32 [8, 2048, 2048], P(None, 'col', 'row')
- grad_w_gate: float32 [8, 2048, 5632], P(None, 'row', 'col')
- grad_w_up: float32 [8, 2048, 5632], P(None, 'row', 'col')
- grad_w_down: float32 [8, 5632, 2048], P(None, 'col', 'row')
The draws below stay inside these ranges and needn't reach their ends.
Inputs may be any that keep to these rules, and one draw needn't show every extreme that they name: `routes_attn`: each token names two different experts. `routes_ffn`: each token names two different experts. `order_attn`: each row along the last dimension is a permutation of the pair numbers of one routing block. `order_ffn`: each row along the last dimension is a permutation of the pair numbers of one routing block. `block_ids`: along a sequence the attention block ids never fall and start at 0; each id covers consecutive positions, at most 256 and at most half of a sequence.
All inputs are finite; a program needn't handle non-finite values.
Results may differ from the reference program's by a relative error of at most 0.02.
Values may be sent and summed in bfloat16 or wider, within the bound.
No kernel may reach another device: no remote copies, remote signals or barrier semaphores. Data moves between devices by JAX's collectives and lax.ppermute only.
A program may use at most 640 MiB of HBM per device.

```python
import math
from functools import partial
import jax
import jax.numpy as jnp
import numpy as np
from jax import lax

D = 2048
FF = 5632
HEADS = 16
HEAD_DIM = 128
EXPERTS = 8
SEQS = 4
SEQ_DEV = 256
SEQ_LEN = 1024
BLOCKS = 4
CAPACITY = 72


def levels(stream_key, shape, split, low, largest):
    level, own = 1.0, jax.random.fold_in(stream_key, 6)
    for axis_at, parts in split:
        draws = jnp.exp(jax.random.uniform(jax.random.fold_in(own, axis_at), (parts,), jnp.float32, low / len(split), largest / len(split)))
        level = level * jnp.repeat(draws, shape[axis_at] // parts).reshape([-1 if axis == axis_at else 1 for axis in range(len(shape))])
    return level


def choose_distinct(stream_key, rows, count, top, lift):
    order = jax.random.permutation(jax.random.fold_in(stream_key, 1), count)
    boost = order
    for power in range(3):
        boost = boost * boost // count
    boost = boost * lift // count
    tickets = jax.random.randint(jax.random.fold_in(stream_key, 2), (rows, count), 0, 4096) + boost
    holders = jax.random.permutation(jax.random.fold_in(stream_key, 3), rows)[jnp.arange(count) % rows]
    tickets = jnp.where(jnp.arange(rows)[:, None] == holders[None, :], 1 << 14, tickets)
    score = tickets * count + jnp.arange(count)
    return lax.top_k(score.astype(jnp.int32), top)[1].astype(jnp.int32)


def length_profile(number_of, total, reach, slope):
    weights = [(1 << 20) // math.isqrt(rank ** slope) + 1 for rank in range(2, number_of + 1)]
    surplus, holding = total - reach - (number_of - 1), [1] * (number_of - 1)
    while surplus > 0:
        candidates = [i for i in range(number_of - 1) if holding[i] < reach]
        pool, budget = sum([weights[i] for i in candidates]), surplus
        for i in candidates:
            more = min(reach - holding[i], max(1, budget * weights[i] // pool), surplus)
            holding[i] = holding[i] + more
            surplus = surplus - more
    return np.array([reach] + holding)


def ragged(rng, count, total, most, lean):
    if count == 2:
        one = jax.random.randint(rng, (), max(1, total - most), min(most, total - 1) + 1)
        return jnp.stack([one, total - one])
    sizes = jnp.asarray(length_profile(count, total, most, lean), jnp.int32)
    couples = (count - 1) // 2
    giver, sink = sizes[1:1 + 2 * couples:2], sizes[2:2 + 2 * couples:2]
    room = jnp.minimum(giver - 1, most - sink)
    passed = jax.random.randint(jax.random.fold_in(rng, 1), (couples,), 0, 1 << 20) % (room + 1)
    sizes = sizes.at[1:1 + 2 * couples:2].set(giver - passed).at[2:2 + 2 * couples:2].set(sink + passed)
    return sizes[jax.random.permutation(jax.random.fold_in(rng, 2), count)]


def normal_values(own_key, extent, scale, limit, cuts=(), kind=jnp.bfloat16):
    level = levels(own_key, extent, cuts, -0.22, 0.18) if cuts else 1.0
    drawn = jax.random.normal(own_key, extent, jnp.float32) * scale * level
    return jnp.minimum(jnp.maximum(drawn, -limit), limit).astype(kind)


def setup_inputs(seed: int = 0) -> dict:
    seeds = jax.random.split(jax.random.key(seed), 19)
    return {
        "block_in": normal_values(seeds[0], (SEQS, SEQ_LEN, D), 1.0, 6.0, ((1, 4), (2, 8))),
        "grad_out": normal_values(seeds[1], (SEQS, SEQ_LEN, D), 1.0, 6.0, ((1, 4), (2, 8))),
        "gain_attn": jnp.clip(1.0 + 0.15 * jax.random.normal(seeds[2], (D,), jnp.float32), 0.25, 1.75),
        "gain_ffn": jnp.clip(1.0 + 0.15 * jax.random.normal(seeds[3], (D,), jnp.float32), 0.25, 1.75),
        "router_attn": normal_values(seeds[4], (D, EXPERTS), D ** -0.5, 0.125),
        "router_ffn": normal_values(seeds[5], (D, EXPERTS), D ** -0.5, 0.125),
        "w_query": normal_values(seeds[6], (EXPERTS, D, HEADS * HEAD_DIM), D ** -0.5, 0.125, ((1, 4), (2, 8))),
        "key_weight": normal_values(seeds[7], (D, HEADS * HEAD_DIM), D ** -0.5, 0.125, ((0, 4), (1, 8))),
        "value_weight": normal_values(seeds[8], (D, HEADS * HEAD_DIM), D ** -0.5, 0.125, ((0, 4), (1, 8))),
        "w_out": normal_values(seeds[9], (EXPERTS, HEADS * HEAD_DIM, D), (HEADS * HEAD_DIM * 32 // SEQ_LEN) ** -0.5, 0.75, ((1, 8), (2, 4))),
        "w_gate": normal_values(seeds[10], (EXPERTS, D, FF), D ** -0.5, 0.125, ((1, 4), (2, 8))),
        "w_up": normal_values(seeds[11], (EXPERTS, D, FF), D ** -0.5, 0.125, ((1, 4), (2, 8))),
        "w_down": normal_values(seeds[12], (EXPERTS, FF, D), FF ** -0.5, 0.078125, ((1, 8), (2, 4))),
        "routes_attn": choose_distinct(seeds[13], SEQS * SEQ_LEN, EXPERTS, 2, 2048).reshape((SEQS, SEQ_LEN, 2)),
        "routes_ffn": choose_distinct(seeds[14], SEQS * SEQ_LEN, EXPERTS, 2, 2048).reshape((SEQS, SEQ_LEN, 2)),
        "order_attn": jax.vmap(lambda own: jax.random.permutation(own, 2 * SEQ_DEV))(jax.random.split(seeds[15], SEQS * BLOCKS)).reshape((SEQS, BLOCKS, 2 * SEQ_DEV)).astype(jnp.int32),
        "order_ffn": jax.vmap(lambda own: jax.random.permutation(own, 2 * SEQ_DEV))(jax.random.split(seeds[16], SEQS * BLOCKS)).reshape((SEQS, BLOCKS, 2 * SEQ_DEV)).astype(jnp.int32),
        "block_ids": jax.vmap(lambda own: jnp.searchsorted(jnp.cumsum(ragged(own, SEQ_LEN // 128 + 2, SEQ_LEN, min(256, SEQ_LEN // 2), 0)), jnp.arange(SEQ_LEN), side="right"))(jax.random.split(seeds[17], SEQS)).reshape((SEQS, SEQ_LEN)).astype(jnp.int32),
    }


EPSILON = 1e-05
ROPE_BASE = 10000.0
MASKED_SCORE = -1e+30
TOP_PRECISION = lax.Precision.HIGHEST

@jax.custom_vjp
def lower_precision(v):
    return lax.optimization_barrier(v.astype(jnp.bfloat16)).astype(jnp.float32)

@jax.custom_vjp
def lower_precision_backward(v):
    return v

def low_keep(v):
    return (lower_precision(v), None)

def low_pass(kept, grad):
    return (grad,)

def back_keep(v):
    return (v, None)

def back_low(kept, grad):
    return (lower_precision(grad),)
lower_precision.defvjp(low_keep, low_pass)
lower_precision_backward.defvjp(back_keep, back_low)

def rope_tables(positions, width):
    half_width = width // 2
    frequency = jnp.exp(-math.log(ROPE_BASE) * jnp.arange(half_width, dtype=jnp.float32) * (2.0 / width))
    angles = positions.astype(jnp.float32)[..., None] * frequency
    angles = jnp.concatenate([angles, angles], axis=-1)
    return (jnp.cos(angles), jnp.sin(angles))

def rotate(values, cosine, sine, sign):
    half_width = values.shape[-1] // 2
    turned = jnp.concatenate([-values[..., half_width:], values[..., :half_width]], axis=-1)
    return values * cosine[..., None, :] + sign * turned * sine[..., None, :]

def slot_table(pair_experts, pair_order, capacity, experts):
    pair_count = pair_experts.shape[0]
    same_expert = pair_experts[:, None] == pair_experts[None, :]
    earlier = pair_order[None, :] < pair_order[:, None]
    rank_count = lax.optimization_barrier(jnp.sum(jnp.logical_and(same_expert, earlier).astype(jnp.int32), axis=1))
    keep_mask = rank_count < capacity
    target = jnp.where(keep_mask, pair_experts * capacity + rank_count, -1)
    matches = target[:, None] == jnp.arange(experts * capacity, dtype=jnp.int32)[None, :]
    pair_ids = jnp.arange(pair_count, dtype=jnp.int32)
    source = lax.optimization_barrier(jnp.sum(jnp.where(matches, pair_ids[:, None], 0), axis=0))
    filled = jnp.any(matches, axis=0)
    return (target, keep_mask, source, filled)

def slot_tables(routes, order):
    seq_count = routes.shape[0]
    pairs = routes.reshape(seq_count, BLOCKS, 2 * SEQ_DEV)
    table_fn = jax.vmap(jax.vmap(partial(slot_table, capacity=CAPACITY, experts=EXPERTS)))
    target, keep_mask, source, filled = table_fn(pairs, order)
    blocks_at = jnp.arange(BLOCKS, dtype=jnp.int32)[None, :, None]
    target = jnp.where(keep_mask, target + blocks_at * (EXPERTS * CAPACITY), 0)
    source = source // 2 + blocks_at * SEQ_DEV
    return (target.reshape(seq_count, -1), keep_mask.reshape(seq_count, -1), source.reshape(seq_count, -1), filled.reshape(seq_count, -1))

def normalize(values, gain):
    return values * lax.rsqrt(lax.optimization_barrier(jnp.mean(values * values, axis=-1, keepdims=True)) + EPSILON) * gain

def routing(hidden_state, router_matrix, routes):
    router_logits = lower_precision_backward(jnp.einsum('mnq,qg->mng', hidden_state, router_matrix, precision=TOP_PRECISION))
    chosen = jnp.take_along_axis(router_logits, routes, axis=-1)
    return jax.nn.softmax(chosen, axis=-1)

def dispatch(hidden_state, tables):
    slot_rows = jnp.take_along_axis(hidden_state, tables[2][..., None], axis=1)
    return jnp.where(tables[3][..., None], slot_rows, 0.0)

def combine(slot_values, gate_probs, tables):
    target, keep_mask = (tables[0], tables[1])
    picked = jnp.take_along_axis(slot_values, target[..., None], axis=1)
    weights = jnp.where(keep_mask, gate_probs.reshape(keep_mask.shape), 0.0)
    summed = picked * weights[..., None]
    return lax.optimization_barrier(jnp.sum(summed.reshape(summed.shape[0], -1, 2, summed.shape[-1]), axis=2))

def attend_block(queries, query_blocks, key_rows, value_token_rows, key_blocks):
    raw = lower_precision_backward(jnp.einsum('qhd,khd->hqk', queries, key_rows, precision=TOP_PRECISION))
    allowed = key_blocks[None, None, :] <= query_blocks[None, :, None]
    scores = jnp.where(allowed, raw * HEAD_DIM ** (-0.5), MASKED_SCORE)
    probs = jax.nn.softmax(scores, axis=-1)
    return jnp.einsum('hqk,khd->qhd', lower_precision(probs), value_token_rows, precision=TOP_PRECISION)

def forward_layer(attn_tables, ffn_tables, routes_attn, routes_ffn, block_ids, block_in, gain_attn, gain_ffn, router_attn, router_ffn, w_query, key_weight, value_weight, w_out, w_gate, w_up, w_down):
    seq_count = block_in.shape[0]
    attention_hidden = lower_precision(normalize(block_in, gain_attn))
    gates_attn = routing(attention_hidden, router_attn, routes_attn)
    tok_cos, tok_sin = rope_tables(jnp.arange(SEQ_LEN, dtype=jnp.int32), HEAD_DIM)
    key_before_rotation = lower_precision_backward(jnp.einsum('pik,kq->piq', attention_hidden, key_weight, precision=TOP_PRECISION))
    key_rows = lower_precision(rotate(key_before_rotation.reshape(seq_count, SEQ_LEN, HEADS, HEAD_DIM), tok_cos, tok_sin, 1.0))
    value_token_rows = lower_precision(lower_precision_backward(jnp.einsum('pik,kq->piq', attention_hidden, value_weight, precision=TOP_PRECISION)))
    value_token_rows = value_token_rows.reshape(seq_count, SEQ_LEN, HEADS, HEAD_DIM)
    slot_in_attn = dispatch(attention_hidden, attn_tables).reshape(seq_count, BLOCKS, EXPERTS, CAPACITY, D)
    query_pre = lower_precision_backward(jnp.einsum('snecd,edf->snecf', slot_in_attn, w_query, precision=TOP_PRECISION))
    slot_cos, slot_sin = rope_tables(attn_tables[2], HEAD_DIM)
    queries = lower_precision(rotate(query_pre.reshape(seq_count, -1, HEADS, HEAD_DIM), slot_cos, slot_sin, 1.0))
    query_blocks = jnp.take_along_axis(block_ids, attn_tables[2], axis=1)
    attended_list = []
    for seq_index in range(seq_count):
        keys_here = key_rows[seq_index]
        values_here = value_token_rows[seq_index]
        blocks_here = block_ids[seq_index]

        def one_block(pieces):
            return attend_block(pieces[0], pieces[1], keys_here, values_here, blocks_here)
        outcome = lax.map(jax.checkpoint(one_block), (queries[seq_index].reshape(BLOCKS, -1, HEADS, HEAD_DIM), query_blocks[seq_index].reshape(BLOCKS, -1)))
        attended_list.append(outcome.reshape(-1, HEADS * HEAD_DIM))
    attended = lower_precision(lower_precision_backward(jnp.stack(attended_list)))
    attended = attended.reshape(seq_count, BLOCKS, EXPERTS, CAPACITY, HEADS * HEAD_DIM)
    out_slots = lower_precision_backward(jnp.einsum('snecf,efd->snecd', attended, w_out, precision=TOP_PRECISION)).reshape(seq_count, -1, D)
    mid = block_in + combine(out_slots, gates_attn, attn_tables)
    hidden_ffn = lower_precision(normalize(lower_precision(mid), gain_ffn))
    gates_ffn = routing(hidden_ffn, router_ffn, routes_ffn)
    slot_in_ffn = dispatch(hidden_ffn, ffn_tables).reshape(seq_count, BLOCKS, EXPERTS, CAPACITY, D)
    gate_pre = lower_precision_backward(jnp.einsum('snecd,edf->snecf', slot_in_ffn, w_gate, precision=TOP_PRECISION))
    up_pre = lower_precision_backward(jnp.einsum('snecd,edf->snecf', slot_in_ffn, w_up, precision=TOP_PRECISION))
    activated = lower_precision(jax.nn.silu(gate_pre) * up_pre)
    down_slots = lower_precision_backward(jnp.einsum('snecf,efd->snecd', activated, w_down, precision=TOP_PRECISION)).reshape(seq_count, -1, D)
    return mid + combine(down_slots, gates_ffn, ffn_tables)

def reference(block_in, grad_out, gain_attn, gain_ffn, router_attn, router_ffn, w_query, key_weight, value_weight, w_out, w_gate, w_up, w_down, routes_attn, routes_ffn, order_attn, order_ffn, block_ids):
    attn_tables = slot_tables(routes_attn, order_attn)
    ffn_tables = slot_tables(routes_ffn, order_ffn)

    def forward(*params):
        return forward_layer(attn_tables, ffn_tables, routes_attn, routes_ffn, block_ids, *params)
    params = tuple((argument.astype(jnp.float32) for argument in (block_in, gain_attn, gain_ffn, router_attn, router_ffn, w_query, key_weight, value_weight, w_out, w_gate, w_up, w_down)))
    result, pullback = jax.vjp(forward, *params)
    gradients = pullback(grad_out.astype(jnp.float32))
    return (result.astype(jnp.bfloat16), gradients[0], gradients[1], gradients[2], gradients[3], gradients[4], gradients[5], gradients[6], gradients[7], gradients[8], gradients[9], gradients[10], gradients[11])
```

```python
from functools import partial
import math

import jax
import jax.numpy as jnp
from jax import lax
from jax.experimental import pallas as pl
from jax.experimental.pallas import tpu as pltpu
from jax.sharding import PartitionSpec as P

HEAD_DIM = 128
EPSILON = 1e-05
ROPE_BASE = 10000.0
MASKED_SCORE = -1e30
BF16 = jnp.bfloat16
F32 = jnp.float32


def dot_f32(spec, left, right):
    return jnp.einsum(spec, left, right, preferred_element_type=F32)


def rope_tables(positions):
    half_width = HEAD_DIM // 2
    frequency = jnp.exp(
        -math.log(ROPE_BASE) * jnp.arange(half_width, dtype=F32) * (2.0 / HEAD_DIM)
    )
    angles = positions.astype(F32)[..., None] * frequency
    angles = jnp.concatenate([angles, angles], axis=-1)
    return (jnp.cos(angles), jnp.sin(angles))


def rotate(values, cosine, sine, sign):
    heads = values.reshape(*values.shape[:-1], -1, HEAD_DIM)
    half_width = HEAD_DIM // 2
    turned = jnp.concatenate([-heads[..., half_width:], heads[..., :half_width]], axis=-1)
    out = heads * cosine[..., None, :] + sign * turned * sine[..., None, :]
    return out.reshape(values.shape)


def pair_ranks(routes, order):
    pairs = routes.reshape(order.shape)
    earlier = (order[..., None, :] < order[..., :, None]).astype(BF16)
    same = (pairs[..., None, :] == pairs[..., :, None]).astype(BF16)
    ranks = jnp.sum((earlier * same).astype(F32), axis=-1).astype(jnp.int32)
    return ranks.reshape(routes.shape)


def slot_match(routes, ranks, expert, capacity):
    chosen = jnp.where(routes == expert, ranks, -1)
    rank_here = jnp.max(chosen, axis=-1)
    slots = jnp.arange(capacity, dtype=jnp.int32)[:, None]
    return rank_here[..., None, :] == slots


def gate_table(hidden, router, routes):
    experts = router.shape[1]
    logits = jnp.dot(hidden, router, preferred_element_type=F32)
    ids = jnp.arange(experts, dtype=jnp.int32)
    chosen = jnp.any(routes[..., None] == ids, axis=-2)
    masked = jnp.where(chosen, logits, MASKED_SCORE)
    top = jnp.max(masked, axis=-1, keepdims=True)
    exps = jnp.where(chosen, jnp.exp(masked - top), 0.0)
    return exps / jnp.sum(exps, axis=-1, keepdims=True)


def normalize_rows(wide):
    inverse = lax.rsqrt(jnp.mean(wide * wide, axis=-1, keepdims=True) + EPSILON)
    return (wide * inverse, inverse)


def pick(match, per_token):
    return jnp.sum(jnp.where(match, per_token[..., None, :], 0), axis=-1)


def scores_of(q, k, qblk, kblk):
    raw = lax.dot_general(q, k, (((1,), (1,)), ((), ())), preferred_element_type=F32)
    return jnp.where(kblk <= qblk, raw * HEAD_DIM ** (-0.5), MASKED_SCORE)


def attend_kernel(q_ref, k_ref, v_ref, qblk_ref, kblk_ref, out_ref, lse_ref):
    scores = scores_of(q_ref[0], k_ref[0], qblk_ref[0], kblk_ref[0])
    top = jnp.max(scores, axis=-1, keepdims=True)
    exps = jnp.exp(scores - top)
    total = jnp.sum(exps, axis=-1, keepdims=True)
    probs = (exps * (1.0 / total)).astype(BF16)
    out = jnp.dot(probs, v_ref[0], preferred_element_type=F32)
    out_ref[0] = out.astype(BF16)
    lse_ref[0, 0] = top + jnp.log(total)


def attend(q, k, v, qblk, kblk):
    seqs, rows, cols = q.shape
    keys = k.shape[1]
    heads = cols // HEAD_DIM
    q_spec = pl.BlockSpec((1, rows, HEAD_DIM), lambda s, h: (s, 0, h))
    k_spec = pl.BlockSpec((1, keys, HEAD_DIM), lambda s, h: (s, 0, h))
    return pl.pallas_call(
        attend_kernel,
        grid=(seqs, heads),
        in_specs=[
            q_spec,
            k_spec,
            k_spec,
            pl.BlockSpec((1, rows, 1), lambda s, h: (s, 0, 0)),
            pl.BlockSpec((1, 1, keys), lambda s, h: (s, 0, 0)),
        ],
        out_specs=[q_spec, pl.BlockSpec((1, 1, rows, 1), lambda s, h: (s, h, 0, 0))],
        out_shape=[
            jax.ShapeDtypeStruct(q.shape, BF16),
            jax.ShapeDtypeStruct((seqs, heads, rows, 1), F32),
        ],
        compiler_params=pltpu.CompilerParams(vmem_limit_bytes=48 * 1024 * 1024),
        cost_estimate=pl.CostEstimate(
            flops=4 * seqs * rows * keys * cols,
            bytes_accessed=4 * q.size + 4 * k.size,
            transcendentals=seqs * heads * rows * keys,
        ),
        name="attend",
    )(q, k, v, qblk, kblk)


def attend_back_kernel(
    q_ref, k_ref, v_ref, g_ref, lse_ref, qblk_ref, kblk_ref, dq_ref, dk_ref, dv_ref
):
    q, k, g = q_ref[0], k_ref[0], g_ref[0]
    probs = jnp.exp(scores_of(q, k, qblk_ref[0], kblk_ref[0]) - lse_ref[0, 0])
    grad = lax.dot_general(g, v_ref[0], (((1,), (1,)), ((), ())), preferred_element_type=F32)
    inner = jnp.sum(probs * grad, axis=-1, keepdims=True)
    grad_scores = (probs * (grad - inner) * HEAD_DIM ** (-0.5)).astype(BF16)
    first = (((0,), (0,)), ((), ()))
    dq_ref[0] = jnp.dot(grad_scores, k, preferred_element_type=F32)
    dk_ref[0] = lax.dot_general(grad_scores, q, first, preferred_element_type=F32)
    dv = lax.dot_general(probs.astype(BF16), g, first, preferred_element_type=F32)
    dv_ref[0] = dv.astype(BF16)


def attend_back(q, k, v, grad, lse, qblk, kblk):
    seqs, rows, cols = q.shape
    keys = k.shape[1]
    heads = cols // HEAD_DIM
    q_spec = pl.BlockSpec((1, rows, HEAD_DIM), lambda s, h: (s, 0, h))
    k_spec = pl.BlockSpec((1, keys, HEAD_DIM), lambda s, h: (s, 0, h))
    return pl.pallas_call(
        attend_back_kernel,
        grid=(seqs, heads),
        in_specs=[
            q_spec,
            k_spec,
            k_spec,
            q_spec,
            pl.BlockSpec((1, 1, rows, 1), lambda s, h: (s, h, 0, 0)),
            pl.BlockSpec((1, rows, 1), lambda s, h: (s, 0, 0)),
            pl.BlockSpec((1, 1, keys), lambda s, h: (s, 0, 0)),
        ],
        out_specs=[q_spec, k_spec, k_spec],
        out_shape=[
            jax.ShapeDtypeStruct(q.shape, F32),
            jax.ShapeDtypeStruct(k.shape, F32),
            jax.ShapeDtypeStruct(k.shape, BF16),
        ],
        compiler_params=pltpu.CompilerParams(vmem_limit_bytes=56 * 1024 * 1024),
        cost_estimate=pl.CostEstimate(
            flops=10 * seqs * rows * keys * cols,
            bytes_accessed=8 * q.size + 10 * k.size,
            transcendentals=seqs * heads * rows * keys,
        ),
        name="attend_back",
    )(q, k, v, grad, lse, qblk, kblk)


def all_tokens(own):
    rows = lax.all_gather(own, "row", axis=1, tiled=True)
    return lax.all_gather(rows, "col", axis=2, tiled=True)


def to_experts(weight, split):
    ranks = lax.axis_size("row")
    experts, height, width = weight.shape
    local = experts // ranks
    grouped = weight.reshape(ranks, local, height, width)
    whole = []
    for j in range(local):
        got = lax.all_to_all(grouped[:, j], "row", 0, 0)
        if split == 1:
            whole.append(got.reshape(ranks * height, width))
        else:
            whole.append(got.transpose(1, 0, 2).reshape(height, ranks * width))
    return whole


def to_owners(grads, split):
    ranks = lax.axis_size("row")
    got = []
    for grad in grads:
        height, width = grad.shape
        if split == 1:
            parts = grad.reshape(ranks, height // ranks, width)
        else:
            parts = grad.reshape(height, ranks, width // ranks).transpose(1, 0, 2)
        got.append(lax.all_to_all(parts, "row", 0, 0))
    stacked = jnp.stack(got, axis=1)
    return stacked.reshape(-1, *stacked.shape[2:]).astype(F32)


def slots_home(slot_rows, seqs, capacity):
    ranks = lax.axis_size("row")
    got = []
    for rows in slot_rows:
        own = lax.psum_scatter(rows, "col", scatter_dimension=1, tiled=True)
        own = own.reshape(seqs, ranks, capacity, -1)
        got.append(lax.all_to_all(own, "row", 1, 1))
    stacked = jnp.stack(got, axis=2)
    return stacked.reshape(seqs, -1, stacked.shape[-1])


def per_device(
    block_in,
    grad_out,
    gain_attn,
    gain_ffn,
    router_attn,
    router_ffn,
    w_query,
    key_weight,
    value_weight,
    w_out,
    w_gate,
    w_up,
    w_down,
    routes_attn,
    routes_ffn,
    order_attn,
    order_ffn,
    block_ids,
):
    seqs, seq_dev, share = block_in.shape
    experts = w_query.shape[0]
    capacity = 18 * seq_dev // (8 * experts)
    head_cols = key_weight.shape[1]
    width = gain_attn.shape[0]
    seq_len = block_ids.shape[1]
    ranks = lax.axis_size("row")
    local = experts // ranks
    row_at, col_at = lax.axis_index("row"), lax.axis_index("col")
    slot_rows = seqs * ranks * capacity

    def own_features(whole):
        return lax.dynamic_slice_in_dim(whole, col_at * share, share, whole.ndim - 1)

    def own_tokens(whole):
        return lax.dynamic_slice_in_dim(whole, row_at * seq_dev, seq_dev, 1)

    small = jnp.stack(
        [
            routes_attn.reshape(seqs, -1),
            order_attn.reshape(seqs, -1),
            routes_ffn.reshape(seqs, -1),
            order_ffn.reshape(seqs, -1),
        ]
    )
    small = lax.all_gather(small, "row", axis=2, tiled=False)
    routes_a = small[0].reshape(seqs, ranks, seq_dev, 2)
    routes_f = small[2].reshape(seqs, ranks, seq_dev, 2)
    ranks_a = pair_ranks(routes_a, small[1])
    ranks_f = pair_ranks(routes_f, small[3])
    mine = [row_at * local + j for j in range(local)]
    match_a = [slot_match(routes_a, ranks_a, e, capacity) for e in mine]
    match_f = [slot_match(routes_f, ranks_f, e, capacity) for e in mine]

    def home_match(routes, rank):
        at = lambda whole: lax.dynamic_index_in_dim(whole, row_at, 1, keepdims=False)
        routes_here, ranks_here = at(routes), at(rank)
        every = [slot_match(routes_here, ranks_here, e, capacity) for e in range(experts)]
        return jnp.concatenate(every, axis=1).astype(BF16)

    home_a = home_match(routes_a, ranks_a)
    home_f = home_match(routes_f, ranks_f)

    def dispatch(match, tokens):
        blocks = tokens.reshape(seqs, ranks, seq_dev, -1)
        return [
            jnp.einsum("snct,sntd->sncd", m.astype(BF16), blocks).reshape(slot_rows, -1)
            for m in match
        ]

    def come_home(match, rows):
        return dot_f32("sct,scf->stf", match, rows)

    def slot_gates(match, gates):
        blocks = gates.reshape(seqs, ranks, seq_dev, experts)
        out = []
        for m, e in zip(match, mine):
            one = lax.dynamic_index_in_dim(blocks, e, 3, keepdims=False)
            out.append(pick(m, one).reshape(slot_rows, 1))
        return out

    def gate_dots(match, dots):
        per_token = []
        for m, d in zip(match, dots):
            spread = jnp.where(m, d.reshape(seqs, ranks, capacity, 1), 0.0)
            per_token.append(jnp.sum(spread, axis=2))
        both = jnp.stack(per_token, axis=-1)
        both = lax.psum(both, "col")
        got = lax.all_to_all(both, "row", 1, 1)
        return got.transpose(0, 2, 1, 3).reshape(seqs, seq_dev, experts)

    in_all = all_tokens(block_in)
    normed_a, inverse_a = normalize_rows(in_all.astype(F32))
    hidden_a = (normed_a * gain_attn).astype(BF16)
    key_all = lax.all_gather(key_weight, "row", axis=0, tiled=True)
    value_all = lax.all_gather(value_weight, "row", axis=0, tiled=True)
    query_w = to_experts(w_query, 1)
    out_w = to_experts(w_out, 2)
    tok_cos, tok_sin = rope_tables(jnp.arange(seq_len, dtype=jnp.int32))
    keys = rotate(dot_f32("std,df->stf", hidden_a, key_all), tok_cos, tok_sin, 1.0).astype(BF16)
    values = dot_f32("std,df->stf", hidden_a, value_all).astype(BF16)
    gates_a = gate_table(hidden_a, router_attn, routes_a.reshape(seqs, seq_len, 2))
    weights_a = slot_gates(match_a, gates_a)
    slot_in_a = dispatch(match_a, hidden_a)
    token_at = jnp.arange(seq_len, dtype=jnp.int32).reshape(1, ranks, seq_dev)
    block_at = block_ids.reshape(seqs, ranks, seq_dev)
    tables = [rope_tables(pick(m, token_at).reshape(slot_rows)) for m in match_a]
    queries = [
        rotate(jnp.dot(x, w, preferred_element_type=F32), c, s, 1.0).astype(BF16)
        for x, w, (c, s) in zip(slot_in_a, query_w, tables)
    ]

    def by_seq(parts):
        return jnp.concatenate([p.reshape(seqs, -1, p.shape[-1]) for p in parts], axis=1)

    def by_expert(whole):
        split = whole.reshape(seqs, local, ranks * capacity, whole.shape[-1])
        return [split[:, j].reshape(slot_rows, -1) for j in range(local)]

    q_seq = by_seq(queries)
    qblk = by_seq([pick(m, block_at).reshape(slot_rows, 1) for m in match_a])
    kblk = block_ids.reshape(seqs, 1, seq_len)
    attended_seq, log_totals = attend(q_seq, keys, values, qblk, kblk)
    attended = by_expert(attended_seq)
    out_slots = [
        (jnp.dot(a, w, preferred_element_type=F32) * g).astype(BF16)
        for a, w, g in zip(attended, out_w, weights_a)
    ]
    mid = block_in.astype(F32) + come_home(home_a, slots_home(out_slots, seqs, capacity))

    mid_low = mid.astype(BF16)
    mid_all = all_tokens(mid_low)
    normed_f, inverse_f = normalize_rows(mid_all.astype(F32))
    hidden_f = (normed_f * gain_ffn).astype(BF16)
    gate_w = to_experts(w_gate, 1)
    up_w = to_experts(w_up, 1)
    down_w = to_experts(w_down, 2)
    gates_f = gate_table(hidden_f, router_ffn, routes_f.reshape(seqs, seq_len, 2))
    weights_f = slot_gates(match_f, gates_f)
    slot_in_f = dispatch(match_f, hidden_f)
    out_grad_all = all_tokens(grad_out)
    slot_grad_out = dispatch(match_f, out_grad_all)
    down_slots, slot_grads_f, dots_f = [], [], []
    grads_gate, grads_up, grads_down = [], [], []
    for j in range(local):
        gate_pre = jnp.dot(slot_in_f[j], gate_w[j], preferred_element_type=F32)
        up_pre = jnp.dot(slot_in_f[j], up_w[j], preferred_element_type=F32)
        gate_sig = jax.nn.sigmoid(gate_pre)
        gate_silu = gate_pre * gate_sig
        activated = gate_silu * up_pre
        scaled = (activated * weights_f[j]).astype(BF16)
        down = jnp.dot(scaled, down_w[j], preferred_element_type=F32)
        down_slots.append(down.astype(BF16))
        grad_raw = dot_f32("rd,fd->rf", slot_grad_out[j], down_w[j])
        dots_f.append(jnp.sum(grad_raw * activated, axis=-1))
        grad_act = grad_raw * weights_f[j]
        grad_gate = grad_act * up_pre * (gate_sig * (1.0 + gate_pre * (1.0 - gate_sig)))
        grad_gate = grad_gate.astype(BF16)
        grad_up = (grad_act * gate_silu).astype(BF16)
        grads_down.append(dot_f32("rf,rd->fd", scaled, slot_grad_out[j]).astype(BF16))
        grads_gate.append(dot_f32("rd,rf->df", slot_in_f[j], grad_gate).astype(BF16))
        grads_up.append(dot_f32("rd,rf->df", slot_in_f[j], grad_up).astype(BF16))
        slot_grad = dot_f32("rf,df->rd", grad_gate, gate_w[j])
        slot_grad = slot_grad + dot_f32("rf,df->rd", grad_up, up_w[j])
        slot_grads_f.append(slot_grad.astype(BF16))
    block_out = (mid + come_home(home_f, slots_home(down_slots, seqs, capacity))).astype(BF16)
    grad_down_own = to_owners(grads_down, 2)
    grad_gate_own = to_owners(grads_gate, 1)
    grad_up_own = to_owners(grads_up, 1)

    def sublayer_back(own_in, inverse_all, gain, router, gates_all, dots, dhidden):
        gates = own_tokens(gates_all)
        inverse = own_tokens(inverse_all)
        dlogits = gates * (dots - jnp.sum(gates * dots, axis=-1, keepdims=True))
        dlogits = dlogits.astype(BF16)
        gain_own = own_features(gain)
        router_own = lax.dynamic_slice_in_dim(router, col_at * share, share, 0)
        normed = own_in.astype(F32) * inverse
        hidden = (normed * gain_own).astype(BF16)
        dhidden = dhidden + dot_f32("ste,fe->stf", dlogits, router_own)
        grad_router = dot_f32("stf,ste->fe", hidden, dlogits)
        grad_gain = jnp.sum(dhidden * normed, axis=(0, 1))
        dn = dhidden * gain_own
        inner = lax.psum(jnp.sum(dn * normed, axis=-1, keepdims=True), "col") / width
        grad = inverse * (dn - normed * inner)
        grads = jnp.concatenate([grad_router, grad_gain[:, None]], axis=1)
        return grad, grads

    dhidden_f = come_home(home_f, slots_home(slot_grads_f, seqs, capacity))
    dots_home_f = gate_dots(match_f, dots_f)
    grad_mid, small_f = sublayer_back(
        mid_low, inverse_f, gain_ffn, router_ffn, gates_f, dots_home_f, dhidden_f
    )
    grad_mid = grad_out.astype(F32) + grad_mid

    mid_grad_all = all_tokens(grad_mid.astype(BF16))
    slot_grad_mid = dispatch(match_a, mid_grad_all)
    grad_att, dots_a, grads_out = [], [], []
    for j in range(local):
        grad_raw = dot_f32("rd,fd->rf", slot_grad_mid[j], out_w[j])
        dots_a.append(jnp.sum(grad_raw * attended[j].astype(F32), axis=-1))
        grad_att.append((grad_raw * weights_a[j]).astype(BF16))
        scaled = (attended[j].astype(F32) * weights_a[j]).astype(BF16)
        grads_out.append(dot_f32("rf,rd->fd", scaled, slot_grad_mid[j]).astype(BF16))
    dq, dk, dv = attend_back(q_seq, keys, values, by_seq(grad_att), log_totals, qblk, kblk)
    grad_key_pre = rotate(dk, tok_cos, tok_sin, -1.0).astype(BF16)
    grad_value_pre = dv
    grads_query, token_part = [], 0.0
    for j, dq_j in enumerate(by_expert(dq)):
        pre = rotate(dq_j, *tables[j], -1.0).astype(BF16)
        grads_query.append(dot_f32("rd,rf->df", slot_in_a[j], pre).astype(BF16))
        slot_grad = dot_f32("rf,df->rd", pre, query_w[j]).astype(BF16)
        slot_grad = slot_grad.reshape(seqs, ranks, capacity, width)
        token_part = token_part + dot_f32(
            "snct,sncd->sntd", match_a[j].astype(BF16), slot_grad
        )
    token_part = token_part.reshape(seqs, seq_len, width)
    token_part = token_part + dot_f32("stf,df->std", grad_key_pre, key_all)
    token_part = token_part + dot_f32("stf,df->std", grad_value_pre, value_all)
    part = lax.psum_scatter(token_part.astype(BF16), "col", scatter_dimension=2, tiled=True)
    dhidden_a = lax.psum_scatter(part, "row", scatter_dimension=1, tiled=True).astype(F32)
    grad_key = dot_f32("std,stf->df", hidden_a, grad_key_pre).astype(BF16)
    grad_value = dot_f32("std,stf->df", hidden_a, grad_value_pre).astype(BF16)
    grad_key_own = lax.psum_scatter(grad_key, "row", scatter_dimension=0, tiled=True).astype(F32)
    grad_value_own = lax.psum_scatter(
        grad_value, "row", scatter_dimension=0, tiled=True
    ).astype(F32)
    grad_query_own = to_owners(grads_query, 1)
    grad_out_own = to_owners(grads_out, 2)
    dots_home_a = gate_dots(match_a, dots_a)
    grad_in, small_a = sublayer_back(
        block_in, inverse_a, gain_attn, router_attn, gates_a, dots_home_a, dhidden_a
    )
    grad_in = grad_mid + grad_in

    def whole_small(grads):
        return lax.all_gather(lax.psum(grads, "row"), "col", axis=0, tiled=True)

    small_f, small_a = whole_small(small_f), whole_small(small_a)
    return (
        block_out,
        grad_in,
        small_a[:, experts],
        small_f[:, experts],
        small_a[:, :experts],
        small_f[:, :experts],
        grad_query_own,
        grad_key_own,
        grad_value_own,
        grad_out_own,
        grad_gate_own,
        grad_up_own,
        grad_down_own,
    )


def solution(mesh):
    in_specs = (
        P(None, "row", "col"),
        P(None, "row", "col"),
        P(),
        P(),
        P(),
        P(),
        P(None, "row", "col"),
        P("row", "col"),
        P("row", "col"),
        P(None, "col", "row"),
        P(None, "row", "col"),
        P(None, "row", "col"),
        P(None, "col", "row"),
        P(None, "row", None),
        P(None, "row", None),
        P(None, "row", None),
        P(None, "row", None),
        P(),
    )
    out_specs = (
        P(None, "row", "col"),
        P(None, "row", "col"),
        P(),
        P(),
        P(),
        P(),
        P(None, "row", "col"),
        P("row", "col"),
        P("row", "col"),
        P(None, "col", "row"),
        P(None, "row", "col"),
        P(None, "row", "col"),
        P(None, "col", "row"),
    )
    return jax.shard_map(
        per_device, mesh=mesh, in_specs=in_specs, out_specs=out_specs, check_vma=False
    )
```

```python
from functools import partial
import math

import jax
import jax.numpy as jnp
from jax import lax
from jax.experimental import pallas as pl
from jax.experimental.pallas import tpu as pltpu
from jax.sharding import PartitionSpec as P

HEAD_DIM = 128
EPSILON = 1e-05
ROPE_BASE = 10000.0
MASKED_SCORE = -1e30
BF16 = jnp.bfloat16
F32 = jnp.float32


def dot_f32(spec, left, right):
    return jnp.einsum(spec, left, right, preferred_element_type=F32)


def tie(value, *others):
    return lax.optimization_barrier((value, others))[0]


def rope_tables(length):
    half_width = HEAD_DIM // 2
    frequency = jnp.exp(
        -math.log(ROPE_BASE) * jnp.arange(half_width, dtype=F32) * (2.0 / HEAD_DIM)
    )
    angles = jnp.arange(length, dtype=jnp.int32).astype(F32)[:, None] * frequency
    cosine, sine = jnp.cos(angles), jnp.sin(angles)
    return (
        jnp.concatenate([cosine, cosine], axis=-1),
        jnp.concatenate([-sine, sine], axis=-1),
    )


def expert_ranks(pairs, order, expert):
    names, places = (jnp.concatenate([a[0], a[1]], axis=-1) for a in (pairs, order))
    ahead = jnp.logical_and(
        places[..., None, :] < places[..., :, None], names[..., None, :] == expert
    )
    rank = jnp.sum(ahead.astype(F32), axis=-1).astype(jnp.int32)
    chosen = jnp.where(names == expert, rank, -1)
    half = chosen.shape[-1] // 2
    return jnp.maximum(chosen[..., :half], chosen[..., half:])


def all_ranks(pairs, order):
    names, places = (jnp.concatenate([a[0], a[1]], axis=-1) for a in (pairs, order))
    ahead = jnp.logical_and(
        places[..., None, :] < places[..., :, None], names[..., None, :] == names[..., :, None]
    )
    rank = jnp.sum(ahead.astype(F32), axis=-1).astype(jnp.int32)
    half = rank.shape[-1] // 2
    return jnp.stack([rank[..., :half], rank[..., half:]])


def slot_match(pairs, ranks, expert, capacity):
    rank_here = jnp.max(jnp.where(pairs == expert, ranks, -1), axis=0)
    slots = jnp.arange(capacity, dtype=jnp.int32)[:, None]
    return rank_here[..., None, :] == slots


def gate_table(logits, routes):
    ids = jnp.arange(logits.shape[-1], dtype=jnp.int32)
    chosen = jnp.any(routes[..., None] == ids, axis=0)
    masked = jnp.where(chosen, logits, MASKED_SCORE)
    top = jnp.max(masked, axis=-1, keepdims=True)
    exps = jnp.where(chosen, jnp.exp(masked - top), 0.0)
    return exps / jnp.sum(exps, axis=-1, keepdims=True)


def normalize_rows(wide):
    inverse = lax.rsqrt(jnp.mean(wide * wide, axis=-1, keepdims=True) + EPSILON)
    return (wide * inverse, inverse)


def roll_half(values):
    return pltpu.roll(values, HEAD_DIM // 2, 1)


def project_kernel(
    rotated, x_ref, gain_ref, router_ref, weight_ref, cos_ref, sin_ref,
    hidden_ref, inverse_ref, logits_ref, out_ref,
):
    normed, inverse = normalize_rows(x_ref[...].astype(F32))
    hidden = (normed * gain_ref[...]).astype(BF16)
    hidden_ref[...] = hidden
    inverse_ref[...] = inverse
    logits_ref[...] = jnp.dot(hidden, router_ref[...], preferred_element_type=F32)
    made = jnp.dot(hidden, weight_ref[...], preferred_element_type=F32)
    cosine, sine = cos_ref[...], sin_ref[...]
    for at, turn in enumerate(rotated):
        columns = slice(at * HEAD_DIM, (at + 1) * HEAD_DIM)
        one = made[:, columns]
        if turn:
            one = one * cosine + roll_half(one) * sine
        out_ref[:, columns] = one.astype(BF16)


def project(x, gain, router, weight, cosine, sine, rotated):
    count, width = x.shape
    experts, cols = router.shape[1], weight.shape[1]
    length = cosine.shape[0]
    tile = 512
    row = lambda n: pl.BlockSpec((tile, n), lambda i: (i, 0))
    whole = lambda a: pl.BlockSpec(a.shape, lambda i: (0, 0))
    table = pl.BlockSpec((tile, HEAD_DIM), lambda i: (lax.rem(i, length // tile), 0))
    return pl.pallas_call(
        partial(project_kernel, rotated),
        grid=(count // tile,),
        in_specs=[row(width), pl.BlockSpec((1, width), lambda i: (0, 0)), whole(router),
                  whole(weight), table, table],
        out_specs=[row(width), row(1), row(experts), row(cols)],
        out_shape=[
            jax.ShapeDtypeStruct((count, width), BF16),
            jax.ShapeDtypeStruct((count, 1), F32),
            jax.ShapeDtypeStruct((count, experts), F32),
            jax.ShapeDtypeStruct((count, cols), BF16),
        ],
        compiler_params=pltpu.CompilerParams(vmem_limit_bytes=48 * 1024 * 1024),
        cost_estimate=pl.CostEstimate(
            flops=2 * count * width * cols,
            bytes_accessed=4 * count * width + 2 * count * cols,
            transcendentals=count,
        ),
        name="project",
    )(x, gain.reshape(1, width), router, weight, cosine, sine)


def scores_of(q, k, qblk, kblk):
    raw = lax.dot_general(q, k, (((1,), (1,)), ((), ())), preferred_element_type=F32)
    return jnp.where(kblk <= qblk, raw * HEAD_DIM ** (-0.5), MASKED_SCORE)


def head_part(ref, at):
    return ref[0, :, at * HEAD_DIM : (at + 1) * HEAD_DIM]


def pick_rows(match, tokens):
    return jnp.dot(match, tokens, preferred_element_type=F32).astype(BF16)


def put_rows(match, rows):
    first = (((0,), (0,)), ((), ()))
    return lax.dot_general(match, rows, first, preferred_element_type=F32)


def slot_rows_of(target_ref, kblk, rows):
    local, length = target_ref.shape[1:]
    at = lax.broadcasted_iota(jnp.int32, (rows, length), 0)
    found = [target_ref[0, j : j + 1] == at for j in range(local)]
    blocks = [
        jnp.sum(jnp.where(m, kblk.astype(F32), 0.0), axis=-1, keepdims=True) for m in found
    ]
    return found, [jnp.where(m, 1.0, 0.0).astype(BF16) for m in found], blocks


def attend_kernel(
    rows, qkv_ref, target_ref, gate_ref, kblk_ref, slot_ref, plain_ref, scaled_ref, lse_ref
):
    local = target_ref.shape[1]
    kblk = kblk_ref[0]
    found, match, blocks = slot_rows_of(target_ref, kblk, rows)
    q = jnp.concatenate([pick_rows(match[j], head_part(qkv_ref, j)) for j in range(local)], axis=0)
    k, v = head_part(qkv_ref, local), head_part(qkv_ref, local + 1)
    scores = scores_of(q, k, jnp.concatenate(blocks, axis=0), kblk.astype(F32))
    top = jnp.max(scores, axis=-1, keepdims=True)
    exps = jnp.exp(scores - top)
    total = jnp.sum(exps, axis=-1, keepdims=True)
    probs = (exps * (1.0 / total)).astype(BF16)
    out = jnp.dot(probs, v, preferred_element_type=F32).astype(BF16)
    lse_ref[0, 0] = top + jnp.log(total)
    for j in range(local):
        here = out[j * rows : (j + 1) * rows]
        gate = jnp.sum(jnp.where(found[j], gate_ref[0, j : j + 1], 0.0), axis=-1, keepdims=True)
        scaled = (here.astype(F32) * gate).astype(BF16)
        columns = slice(j * HEAD_DIM, (j + 1) * HEAD_DIM)
        slot_ref[j, 0] = scaled
        plain_ref[0, :, columns] = put_rows(match[j], here).astype(BF16)
        scaled_ref[0, :, columns] = put_rows(match[j], scaled).astype(BF16)


def attend(qkv, target, gates, kblk, rows, heads):
    seqs, length, cols = qkv.shape
    local = target.shape[1]
    token = lambda n: pl.BlockSpec((1, length, n * HEAD_DIM), lambda s, h: (s, 0, h))
    lane = lambda n: pl.BlockSpec((1, n, length), lambda s, h: (s, 0, 0))
    of_tokens = jax.ShapeDtypeStruct((seqs, length, heads * local * HEAD_DIM), BF16)
    total = local * rows
    return pl.pallas_call(
        partial(attend_kernel, rows),
        grid=(seqs, heads),
        in_specs=[token(local + 2), lane(local), lane(local), lane(1)],
        out_specs=[
            pl.BlockSpec((local, 1, rows, HEAD_DIM), lambda s, h: (0, s, 0, h)),
            token(local),
            token(local),
            pl.BlockSpec((1, 1, total, 1), lambda s, h: (s, h, 0, 0)),
        ],
        out_shape=[
            jax.ShapeDtypeStruct((local, seqs, rows, heads * HEAD_DIM), BF16),
            of_tokens,
            of_tokens,
            jax.ShapeDtypeStruct((seqs, heads, total, 1), F32),
        ],
        compiler_params=pltpu.CompilerParams(vmem_limit_bytes=56 * 1024 * 1024),
        cost_estimate=pl.CostEstimate(
            flops=12 * seqs * heads * total * length * HEAD_DIM,
            bytes_accessed=4 * qkv.size,
            transcendentals=seqs * heads * total * length,
        ),
        name="attend",
    )(qkv, target, gates, kblk)


def attend_back_kernel(
    rows, qkv_ref, target_ref, kblk_ref, lse_ref, plain_ref, raw_ref, gate_ref, cos_ref, sin_ref,
    out_ref, dots_ref,
):
    local = target_ref.shape[1]
    kblk = kblk_ref[0]
    _, match, blocks = slot_rows_of(target_ref, kblk, rows)
    q = jnp.concatenate([pick_rows(match[j], head_part(qkv_ref, j)) for j in range(local)], axis=0)
    k, v = head_part(qkv_ref, local), head_part(qkv_ref, local + 1)
    grads, dots = [], []
    for j in range(local):
        raw = head_part(raw_ref, j)
        gated = (raw * gate_ref[0, :, j : j + 1]).astype(BF16)
        grads.append(pick_rows(match[j], gated))
        dots.append(jnp.sum(raw * head_part(plain_ref, j).astype(F32), axis=-1, keepdims=True))
    g = jnp.concatenate(grads, axis=0)
    scores = scores_of(q, k, jnp.concatenate(blocks, axis=0), kblk.astype(F32))
    probs = jnp.exp(scores - lse_ref[0, 0])
    grad = lax.dot_general(g, v, (((1,), (1,)), ((), ())), preferred_element_type=F32)
    inner = jnp.sum(probs * grad, axis=-1, keepdims=True)
    grad_scores = (probs * (grad - inner) * HEAD_DIM ** (-0.5)).astype(BF16)
    dq = jnp.dot(grad_scores, k, preferred_element_type=F32)
    cosine, sine = cos_ref[...], sin_ref[...]
    inner_sum = 0.0
    turn = lambda value: (value * cosine - roll_half(value) * sine).astype(BF16)
    for j in range(local):
        here = dq[j * rows : (j + 1) * rows]
        high = here.astype(BF16)
        low = (here - high.astype(F32)).astype(BF16)
        placed = put_rows(match[j], high) + put_rows(match[j], low)
        out_ref[0, :, j * HEAD_DIM : (j + 1) * HEAD_DIM] = turn(placed)
        inner_sum = inner_sum + placed * head_part(qkv_ref, j).astype(F32)
    dk = put_rows(grad_scores, q)
    out_ref[0, :, local * HEAD_DIM : (local + 1) * HEAD_DIM] = turn(dk)
    dv = put_rows(probs.astype(BF16), g)
    out_ref[0, :, (local + 1) * HEAD_DIM : (local + 2) * HEAD_DIM] = dv.astype(BF16)
    inner_sum = inner_sum + dk * k.astype(F32) + dv * v.astype(F32)
    dots.append(jnp.sum(inner_sum, axis=-1, keepdims=True))
    for at in range(local + 1):

        @pl.when(pl.program_id(1) == 0)
        def _():
            dots_ref[0, :, at : at + 1] = dots[at]

        @pl.when(pl.program_id(1) > 0)
        def _():
            dots_ref[0, :, at : at + 1] = dots_ref[0, :, at : at + 1] + dots[at]


def attend_back(qkv, target, kblk, lse, plain, raw, gate_cols, cosine, sine, rows, heads):
    seqs, length, cols = qkv.shape
    local = target.shape[1]
    token = lambda n: pl.BlockSpec((1, length, n * HEAD_DIM), lambda s, h: (s, 0, h))
    lane = lambda n: pl.BlockSpec((1, n, length), lambda s, h: (s, 0, 0))
    total = local * rows
    column = pl.BlockSpec((1, length, local), lambda s, h: (s, 0, 0))
    table = pl.BlockSpec((length, HEAD_DIM), lambda s, h: (0, 0))
    return pl.pallas_call(
        partial(attend_back_kernel, rows),
        grid=(seqs, heads),
        in_specs=[
            token(local + 2),
            lane(local),
            lane(1),
            pl.BlockSpec((1, 1, total, 1), lambda s, h: (s, h, 0, 0)),
            token(local),
            token(local),
            column,
            table,
            table,
        ],
        out_specs=[
            token(local + 2),
            pl.BlockSpec((1, length, local + 1), lambda s, h: (s, 0, 0)),
        ],
        out_shape=[
            jax.ShapeDtypeStruct(qkv.shape, BF16),
            jax.ShapeDtypeStruct((seqs, length, local + 1), F32),
        ],
        compiler_params=pltpu.CompilerParams(vmem_limit_bytes=60 * 1024 * 1024),
        cost_estimate=pl.CostEstimate(
            flops=24 * seqs * heads * total * length * HEAD_DIM,
            bytes_accessed=8 * qkv.size,
            transcendentals=seqs * heads * total * length,
        ),
        name="attend_back",
    )(qkv, target, kblk, lse, plain, raw, gate_cols, cosine, sine)


def gather_rows(own):
    return lax.all_gather(own, "row", axis=1, tiled=True)


def gather_cols(rows):
    return lax.all_gather(rows, "col", axis=2, tiled=True)


def exchange(parts):
    return lax.all_to_all(parts, "row", 0, 0)


def exchange_pieces(piece_for):
    ranks, row = lax.axis_size("row"), lax.axis_index("row")
    got = [piece_for(row)]
    for m in range(1, ranks):
        steps = [(i, (i + m) % ranks) for i in range(ranks)]
        got.append(lax.ppermute(piece_for(lax.rem(row + m, ranks)), "row", steps))
    return got


def assemble(pieces, body, outs, name):
    ranks, each = len(pieces), len(pieces[0])

    def kernel(row_ref, *refs):
        for m in range(ranks):

            @pl.when(pl.program_id(0) == m)
            def _():
                body(m, refs[m * each : (m + 1) * each], refs[ranks * each :])

    def at(index):
        return lambda m, row: index(lax.rem(row[0] - m + ranks, ranks))

    flat = [a for piece in pieces for a in piece]
    whole = lambda a: pl.BlockSpec(a.shape, lambda m, row: (0,) * a.ndim)
    return pl.pallas_call(
        kernel,
        grid_spec=pltpu.PrefetchScalarGridSpec(
            num_scalar_prefetch=1,
            grid=(ranks,),
            in_specs=[whole(a) for a in flat],
            out_specs=[pl.BlockSpec(block, at(index)) for _, _, block, index in outs],
        ),
        out_shape=[jax.ShapeDtypeStruct(shape, dtype) for shape, dtype, _, _ in outs],
        compiler_params=pltpu.CompilerParams(vmem_limit_bytes=48 * 1024 * 1024),
        cost_estimate=pl.CostEstimate(
            flops=0, bytes_accessed=4 * sum(a.size for a in flat), transcendentals=0
        ),
        name=name,
    )(lax.axis_index("row").astype(jnp.int32).reshape(1), *flat)


def place_rows(outs, at, pieces, dtype):
    first = 0
    for piece in pieces:
        rows = slice(first, first + piece.shape[0])
        if at is None:
            outs[rows] = piece[...].astype(dtype)
        else:
            outs[at, rows] = piece[...].astype(dtype)
        first += piece.shape[0]


def spread_kernel(into_ref, weight_ref, extra_ref, out_ref):
    last = (((1,), (1,)), ((), ()))
    tokens, copies = into_ref.shape[1], out_ref.shape[2] // extra_ref.shape[2]
    rows = lax.dot_general(into_ref[0], weight_ref[...], last, preferred_element_type=F32)
    out_ref[0, :tokens] = rows.astype(BF16)
    share = extra_ref.shape[2]
    for at in range(copies):
        out_ref[0, tokens:, at * share : (at + 1) * share] = extra_ref[0]


def spread(into, weight, extra):
    blocks, tokens, depth = into.shape
    width = weight.shape[0]
    rows = tokens + extra.shape[1]
    block = lambda a: pl.BlockSpec((1, *a.shape[1:]), lambda i: (i, 0, 0))
    return pl.pallas_call(
        spread_kernel,
        grid=(blocks,),
        in_specs=[block(into), pl.BlockSpec(weight.shape, lambda i: (0, 0)), block(extra)],
        out_specs=pl.BlockSpec((1, rows, width), lambda i: (i, 0, 0)),
        out_shape=jax.ShapeDtypeStruct((blocks, rows, width), BF16),
        compiler_params=pltpu.CompilerParams(vmem_limit_bytes=48 * 1024 * 1024),
        cost_estimate=pl.CostEstimate(
            flops=2 * blocks * tokens * depth * width,
            bytes_accessed=2 * blocks * (tokens * depth + rows * width),
            transcendentals=0,
        ),
        name="spread",
    )(into, weight, extra)


def sum_cols(rows):
    return lax.psum_scatter(rows, "col", scatter_dimension=1, tiled=True)


def round_up(count, unit):
    return -(-count // unit) * unit


def rows_home(own, seqs, capacity, extra=None):
    ranks, share = lax.axis_size("row"), own.shape[-1]
    rows = own.reshape(-1, seqs, ranks, capacity, share).transpose(2, 1, 0, 3, 4)
    rows = rows.reshape(ranks, -1, share)
    count = rows.shape[1]
    if extra is not None:
        rows = jnp.concatenate([rows, extra], axis=1)
    got = exchange(rows)
    home = got[:, :count].reshape(ranks, seqs, -1, share).swapaxes(0, 1)
    return home.reshape(seqs, -1, share), got[:, count:]


def per_device(
    block_in,
    grad_out,
    gain_attn,
    gain_ffn,
    router_attn,
    router_ffn,
    w_query,
    key_weight,
    value_weight,
    w_out,
    w_gate,
    w_up,
    w_down,
    routes_attn,
    routes_ffn,
    order_attn,
    order_ffn,
    block_ids,
):
    seqs, seq_dev, share = block_in.shape
    experts, depth, head_cols = w_query.shape
    capacity = 18 * seq_dev // (8 * experts)
    heads = head_cols // HEAD_DIM
    hidden_units = w_gate.shape[2]
    width = gain_attn.shape[0]
    seq_len = block_ids.shape[1]
    ranks = lax.axis_size("row")
    local = experts // ranks
    row_at, col_at = lax.axis_index("row"), lax.axis_index("col")
    slot_rows = seqs * ranks * capacity
    count = seqs * seq_len

    def own_features(whole):
        return lax.dynamic_slice_in_dim(whole, col_at * share, share, whole.ndim - 1)

    def own_tokens(whole):
        return lax.dynamic_slice_in_dim(whole, row_at * seq_dev, seq_dev, 1)

    def by_pair(table):
        return table.reshape(seqs, seq_dev, 2).transpose(2, 0, 1)

    small = jnp.stack([by_pair(t) for t in (routes_attn, order_attn, routes_ffn, order_ffn)])
    split = jnp.concatenate([small % 256, small[1::2] // 256]).astype(BF16)
    split = split.transpose(2, 0, 1, 3).reshape(seqs, -1)
    held = split.shape[1]
    table_rows = round_up(held, 16 * share) // share
    split = jnp.pad(split, ((0, 0), (0, table_rows * share - held)))
    in_rows = gather_rows(
        jnp.concatenate([block_in, split.reshape(seqs, table_rows, share)], axis=1)
    ).reshape(seqs, ranks, -1, share)
    split = in_rows[:, :, seq_dev:].reshape(seqs, ranks, -1)[..., :held].astype(jnp.int32)
    split = split.reshape(seqs, ranks, 6, 2, seq_dev).transpose(2, 3, 0, 1, 4)
    small_all = [split[0], split[1] + 256 * split[4], split[2], split[3] + 256 * split[5]]
    in_rows = in_rows[:, :, :seq_dev].reshape(seqs, seq_len, share)

    def expert_in(weight, j, *after, half=None):
        weight = tie(weight, *after)
        _, height, columns = weight.shape
        first, rows = (0, height) if half is None else (half * (height // 2), height // 2)

        def piece_for(n):
            block = (1, rows, columns)
            return lax.dynamic_slice(weight, (n * local + j, first, 0), block)[0]

        return exchange_pieces(piece_for)

    def in_body(m, ins, outs):
        place_rows(outs[0], None, ins, BF16)

    def rows_in(*got):
        block = (hidden_units, depth)
        out = ((hidden_units, width), BF16, block, lambda b: (0, b))
        return assemble(list(zip(*got)), in_body, [out], "rows_in")[0]

    w_gate, w_up = w_gate.swapaxes(1, 2), w_up.swapaxes(1, 2)

    def group_in(weight, *after):
        grouped = tie(weight, *after).reshape(ranks, local, *weight.shape[1:])
        return lambda n: lax.dynamic_index_in_dim(grouped, n, 0, keepdims=False)

    parts = local + 2
    query_for = group_in(w_query)
    key_value = jnp.stack([key_weight, value_weight])
    query_got = exchange_pieces(lambda n: jnp.concatenate([query_for(n), key_value]))

    def query_body(m, ins, outs):
        for h in range(heads):
            for p in range(parts):
                at = (h * parts + p) * HEAD_DIM
                piece = ins[0][p, :, h * HEAD_DIM : (h + 1) * HEAD_DIM]
                outs[0][:, at : at + HEAD_DIM] = piece

    made = heads * parts * HEAD_DIM
    query_w = assemble(
        [(p,) for p in query_got],
        query_body,
        [((width, made), BF16, (depth, made), lambda b: (b, 0))],
        "query_in",
    )[0]

    mine = [row_at * local + j for j in range(local)]

    def tokens_to_slots(pairs, order):
        first = jnp.arange(ranks, dtype=jnp.int32)[:, None] * capacity
        out = []
        for e in mine:
            rank = expert_ranks(pairs, order, e)
            kept = jnp.logical_and(rank >= 0, rank < capacity)
            out.append(jnp.where(kept, first + rank, -1).reshape(seqs, seq_len))
        return jnp.stack(out, axis=1)

    target_a = tokens_to_slots(small_all[0], small_all[1])
    target_f = tokens_to_slots(small_all[2], small_all[3])
    routes_a = small_all[0].reshape(2, seqs, seq_len)
    routes_f = small_all[2].reshape(2, seqs, seq_len)
    out_for = group_in(w_out, *small_all)
    out_got = exchange_pieces(out_for)
    gate_first = expert_in(w_gate, 0, *query_got, half=0)

    def home_match(pairs, order):
        ranks_here = all_ranks(pairs, order)
        every = [slot_match(pairs, ranks_here, e, capacity) for e in range(experts)]
        return jnp.concatenate(every, axis=1).astype(BF16)

    home_a = home_match(small[0], small[1])
    home_f = home_match(small[2], small[3])

    def come_home(match, rows):
        return dot_f32("sct,scf->stf", match, rows)

    def my_gates(gates):
        return jnp.stack(
            [lax.dynamic_index_in_dim(gates, e, 2, keepdims=False) for e in mine], axis=1
        )

    in_all = gather_cols(in_rows).reshape(count, width)
    cosine, sine = rope_tables(seq_len)
    rotated = ([True] * (local + 1) + [False]) * heads
    hidden_a, inverse_a, logits_a, qkv = project(
        in_all, gain_attn, router_attn, query_w, cosine, sine, rotated
    )
    qkv = qkv.reshape(seqs, seq_len, -1)
    grad_rows = gather_rows(tie(grad_out, in_all))
    gates_a = gate_table(
        logits_a.reshape(seqs, seq_len, experts), routes_a
    )
    my_gates_a = my_gates(gates_a)
    kblk = block_ids.reshape(seqs, 1, seq_len)
    rows_each = ranks * capacity
    att_slot, att_plain, att_scaled, log_totals = attend(
        qkv, target_a, my_gates_a, kblk, rows_each, heads
    )
    def out_body(m, ins, outs):
        for j in range(local):
            outs[1][j] = ins[0][j]
            for h in range(heads):
                at = (h * local + j) * HEAD_DIM
                outs[0][at : at + HEAD_DIM] = ins[0][j, h * HEAD_DIM : (h + 1) * HEAD_DIM]

    rows_cat = heads * local * HEAD_DIM
    out_cat, out_w = assemble(
        [(p,) for p in tie(out_got, att_slot)],
        out_body,
        [
            ((rows_cat, width), BF16, (rows_cat, depth), lambda b: (0, b)),
            ((local, head_cols, width), BF16, (local, head_cols, depth), lambda b: (0, 0, b)),
        ],
        "out_in",
    )

    out_slots = dot_f32(
        "jrf,jfd->jrd", att_slot.reshape(local, slot_rows, head_cols), out_w
    ).astype(BF16)
    out_slots = tie(out_slots.reshape(-1, width), grad_rows, *gate_first)
    gate_got_in = [(gate_first, expert_in(w_gate, 0, *out_got, *gate_first, half=1))]
    up_first = expert_in(w_up, 0, *out_got, *gate_first, half=0)
    out_own = tie(sum_cols(out_slots), *gate_got_in[0][1], *up_first)
    out_home, _ = rows_home(out_own, seqs, capacity)
    mid = block_in.astype(F32) + come_home(home_a, out_home)

    mid_low = mid.astype(BF16)
    mid_rows = gather_rows(mid_low)
    mid_all = gather_cols(mid_rows).reshape(count, width)
    up_got_in = [(up_first, expert_in(w_up, 0, mid_rows, half=1))]
    down_got_in = [(expert_in(w_down, 0, mid_rows),)]
    mid_all = tie(mid_all, *up_got_in[0][1], *down_got_in[0][0])
    out_grad_all = gather_cols(tie(grad_rows, mid_all))
    normed_f, inverse_f = normalize_rows(mid_all.astype(F32))
    hidden_f = (normed_f * gain_ffn).astype(BF16)
    logits_f = jnp.dot(hidden_f, router_ffn, preferred_element_type=F32)
    gates_f = gate_table(
        logits_f.reshape(seqs, seq_len, experts), routes_f
    )
    my_gates_f = my_gates(gates_f)
    blocked = lambda a: a.reshape(seqs, ranks, seq_dev)
    slots_at = jnp.arange(capacity, dtype=jnp.int32)[:, None]
    first_at = jnp.arange(ranks, dtype=jnp.int32)[:, None, None] * capacity
    match_f = [blocked(target_f[:, j])[:, :, None, :] == first_at + slots_at for j in range(local)]
    weights_f = [
        jnp.sum(
            jnp.where(match_f[j], blocked(my_gates_f[:, j])[:, :, None, :], 0.0), axis=-1
        ).reshape(slot_rows, 1)
        for j in range(local)
    ]

    def dispatch(tokens, j):
        blocks = tokens.reshape(seqs, ranks, seq_dev, width)
        picked = jnp.einsum("snct,sntd->sncd", match_f[j].astype(BF16), blocks)
        return picked.reshape(slot_rows, width)

    down_slots, slot_grads_f, dots_f = [], [], []
    grads_gate, grads_up, grads_down = [], [], []
    for j in range(local):
        slot_in = dispatch(hidden_f, j)
        if j == 0 and local > 1:
            gate_got_in.append((expert_in(w_gate, 1, mid_all),))
            slot_in = tie(slot_in, *gate_got_in[1][0])
        if j + 1 < local:
            up_got_in.append((expert_in(w_up, j + 1, slot_in),))
        gate_w, up_w = rows_in(*gate_got_in[j]), rows_in(*up_got_in[j])
        gate_pre = dot_f32("rd,fd->rf", slot_in, gate_w)
        up_pre = dot_f32("rd,fd->rf", slot_in, up_w)
        down_w = rows_in(*down_got_in[j])
        gate_sig = jax.nn.sigmoid(gate_pre)
        gate_silu = gate_pre * gate_sig
        activated = gate_silu * up_pre
        scaled = (activated * weights_f[j]).astype(BF16)
        slot_grad_out = dispatch(out_grad_all, j)
        grads_down.append(dot_f32("rf,rd->fd", scaled, slot_grad_out).astype(BF16))
        down = jnp.dot(scaled, down_w, preferred_element_type=F32)
        down_slots.append(down.astype(BF16))
        grad_raw = dot_f32("rd,fd->rf", slot_grad_out, down_w)
        grad_act = grad_raw * weights_f[j]
        grad_gate = grad_act * up_pre * (gate_sig * (1.0 + gate_pre * (1.0 - gate_sig)))
        grad_gate = grad_gate.astype(BF16)
        grad_up = (grad_act * gate_silu).astype(BF16)
        grads_gate.append(dot_f32("rf,rd->fd", grad_gate, slot_in).astype(BF16))
        grads_up.append(dot_f32("rf,rd->fd", grad_up, slot_in).astype(BF16))
        slot_grad = dot_f32("rf,fd->rd", grad_gate, gate_w)
        slot_grad = slot_grad + dot_f32("rf,fd->rd", grad_up, up_w)
        slot_grad = slot_grad.astype(BF16)
        if j + 1 < local:
            slot_grad = tie(slot_grad, *up_got_in[-1][0])
            down_got_in.append((expert_in(w_down, j + 1, slot_grad),))
            if j + 2 < local:
                gate_got_in.append((expert_in(w_gate, j + 2, slot_grad),))
        slot_grads_f.append(slot_grad)
        inner = grad_gate.astype(F32) * gate_pre + grad_up.astype(F32) * up_pre
        dots = jnp.stack([jnp.sum(grad_raw * activated, axis=-1), jnp.sum(inner, axis=-1)])
        dots = dots.reshape(2, seqs, ranks, capacity).transpose(2, 0, 1, 3).reshape(ranks, -1)
        dots_f.append(dots.astype(BF16))

    def columns_out(grad, *after, half=None):
        grad = tie(grad, *after)
        size = grad.shape[0] // ranks
        first, rows = (0, size) if half is None else (half * (size // 2), size // 2)
        return exchange_pieces(lambda n: lax.dynamic_slice_in_dim(grad, n * size + first, rows, 0))

    def rows_out(grad, *after, half=None):
        grad = tie(grad, *after)
        height = grad.shape[0]
        first, rows = (0, height) if half is None else (half * (height // 2), height // 2)
        return exchange_pieces(
            lambda n: lax.dynamic_slice(grad, (first, n * depth), (rows, depth))
        )

    def whole_grad(got):
        counts = [len(parts) for parts in got]
        rows = sum(part[0].shape[0] for part in got[0])
        columns = got[0][0][0].shape[1]
        pieces = [tuple(part[m] for parts in got for part in parts) for m in range(ranks)]

        def body(m, ins, outs):
            first = 0
            for j, held in enumerate(counts):
                place_rows(outs[0], j, ins[first : first + held], F32)
                first += held

        out = ((experts, rows, columns), F32, (local, rows, columns), lambda b: (b, 0, 0))
        return assemble(pieces, body, [out], "whole_grad")[0]

    def sublayer_back(own_in, inverse_all, gain, router, gates_all, logits_all, dots, inner, dhidden):
        gates = own_tokens(gates_all)
        inverse = own_tokens(inverse_all)
        dlogits = gates * (dots - jnp.sum(gates * dots, axis=-1, keepdims=True))
        dlogits = dlogits.astype(BF16)
        gain_own = own_features(gain)
        router_own = lax.dynamic_slice_in_dim(router, col_at * share, share, 0)
        normed = own_in.astype(F32) * inverse
        hidden = (normed * gain_own).astype(BF16)
        dhidden = dhidden + dot_f32("ste,fe->stf", dlogits, router_own)
        grad_router = dot_f32("ste,stf->ef", dlogits, hidden)
        grad_gain = jnp.sum(dhidden * normed, axis=(0, 1))
        dn = dhidden * gain_own
        inner = inner + jnp.sum(dlogits.astype(F32) * own_tokens(logits_all), axis=-1)
        grad = inverse * (dn - normed * (inner / width)[..., None])
        return grad, jnp.concatenate([grad_router, grad_gain[None]], axis=0)

    seq3 = lambda a: a.reshape(seqs, seq_len, -1)
    last = down_got_in[-1][-1]
    down_got = [[rows_out(grads_down[0], *last)]]
    gate_first = rows_out(grads_gate[0], *last, half=0)
    per_row = dots_f[0].shape[1]
    dot_rows = round_up(per_row, share) // share
    under = round_up(ranks * dot_rows, 16)
    own_rows, own_dots = [], []
    for rows, dots in zip(slot_grads_f, dots_f):
        dots = jnp.pad(dots, ((0, 0), (0, dot_rows * share - per_row)))
        dots = jnp.pad(dots.reshape(-1, share), ((0, under - ranks * dot_rows), (0, 0)))
        dots = jnp.tile(dots, (1, width // share))
        own = sum_cols(jnp.concatenate([rows, dots], axis=0))
        own_rows.append(own[:slot_rows])
        own_dots.append(own[slot_rows : slot_rows + ranks * dot_rows].reshape(ranks, -1, share))
    own_rows = tie(
        jnp.concatenate(own_rows, axis=0),
        *down_got[0][0],
        *gate_first,
        *grads_gate,
        *grads_up,
        *grads_down,
        *down_slots,
    )
    grad_home, dots_home = rows_home(
        own_rows, seqs, capacity, jnp.concatenate(own_dots, axis=1)
    )
    dhidden_f = come_home(home_f, grad_home)
    dots_home = dots_home.reshape(ranks, local, -1)[..., :per_row].astype(F32)
    dots_home = dots_home.reshape(experts, 2, seqs, capacity, 1).transpose(1, 2, 0, 3, 4)
    match_home = home_f.reshape(seqs, experts, capacity, seq_dev).astype(F32)
    dots_home = jnp.sum(dots_home * match_home, axis=3).swapaxes(2, 3)
    logits_f = logits_f.reshape(seqs, seq_len, experts)
    grad_mid, small_f = sublayer_back(
        mid_low, seq3(inverse_f), gain_ffn, router_ffn, gates_f, logits_f,
        dots_home[0], jnp.sum(dots_home[1], axis=-1), dhidden_f,
    )
    grad_mid = grad_out.astype(F32) + grad_mid

    mid_grad_rows = gather_rows(grad_mid.astype(BF16))
    mid_grad_all = gather_cols(mid_grad_rows).reshape(count, width)
    gate_got = [[gate_first, rows_out(grads_gate[0], mid_grad_rows, half=1)]]
    up_got = [[rows_out(grads_up[0], mid_grad_rows)]]
    mid_grad_all = tie(mid_grad_all, *gate_got[0][1], *up_got[0][0])
    down_slots = tie(jnp.concatenate(down_slots, axis=0), mid_grad_all)
    down_own = sum_cols(down_slots)
    grad_raw = dot_f32("rd,fd->rf", mid_grad_all, out_cat)
    early = []
    for j in range(1, local):
        down_got.append([rows_out(grads_down[j], mid_grad_all)])
        gate_got.append([rows_out(grads_gate[j], mid_grad_all, half=0)])
        early += [*down_got[-1][0], *gate_got[-1][0]]
    into, dots_a = attend_back(
        qkv, target_a, kblk, log_totals, att_plain, seq3(grad_raw), my_gates_a.swapaxes(1, 2),
        cosine, sine, rows_each, heads,
    )
    last = ()
    for j in range(1, local):
        gate_got[j].append(rows_out(grads_gate[j], into, *early, half=1))
        up_got.append([rows_out(grads_up[j], into, *early)])
        last += (*gate_got[j][1], *up_got[-1][0])
    grad_out_cat = dot_f32("rf,rd->fd", att_scaled.reshape(count, -1), mid_grad_all).astype(BF16)
    placed = jnp.zeros((seqs, ranks, experts, seq_dev), F32)
    dots_a = dots_a.reshape(seqs, ranks, seq_dev, local + 1).swapaxes(2, 3)
    placed = lax.dynamic_update_slice_in_dim(placed, dots_a[:, :, :local], row_at * local, 2)
    extra = jnp.concatenate([placed, dots_a[:, :, local:]], axis=2).astype(BF16)
    extra = extra.reshape(seqs * ranks, -1)
    held = extra.shape[1]
    under = round_up(held, 16 * share) // share
    extra = jnp.pad(extra, ((0, 0), (0, under * share - held)))
    token_part = spread(
        into.reshape(seqs * ranks, seq_dev, -1), query_w, extra.reshape(-1, under, share)
    ).reshape(seqs, -1, width)
    token_part = tie(token_part, down_own, *early)
    down_home, _ = rows_home(tie(down_own, token_part), seqs, capacity)
    part = lax.psum_scatter(token_part, "col", scatter_dimension=2, tiled=True)
    out_pieces = rows_out(grad_out_cat, token_part, *last)
    part = tie(part, *last, *out_pieces, down_home)
    own = lax.psum_scatter(part, "row", scatter_dimension=1, tiled=True)
    dhidden_a = own[:, :seq_dev].astype(F32)
    dots_a = own[:, seq_dev:].reshape(seqs, -1)[:, :held].astype(F32)
    dots_a = dots_a.reshape(seqs, experts + 1, seq_dev).swapaxes(1, 2)

    def out_grad_body(m, ins, outs):
        for j in range(local):
            for h in range(heads):
                at = (h * local + j) * HEAD_DIM
                piece = ins[0][at : at + HEAD_DIM].astype(F32)
                outs[0][j, h * HEAD_DIM : (h + 1) * HEAD_DIM] = piece

    grad_out_own = assemble(
        [(p,) for p in out_pieces],
        out_grad_body,
        [((experts, head_cols, depth), F32, (local, head_cols, depth), lambda b: (b, 0, 0))],
        "out_grad",
    )[0]

    def query_grad_body(m, ins, outs):
        for h in range(heads):
            columns = slice(h * HEAD_DIM, (h + 1) * HEAD_DIM)
            for p in range(parts):
                at = (h * parts + p) * HEAD_DIM
                piece = ins[0][:, at : at + HEAD_DIM].astype(F32)
                if p < local:
                    outs[0][p, :, columns] = piece
                elif m == 0:
                    outs[1 + p - local][:, columns] = piece
                else:
                    outs[1 + p - local][:, columns] = outs[1 + p - local][:, columns] + piece

    grad_query_cat = dot_f32("rd,rf->df", hidden_a, into.reshape(count, -1)).astype(BF16)
    shared = ((depth, head_cols), F32, (depth, head_cols), lambda b: (0, 0))
    grad_query_own, grad_key_own, grad_value_own = assemble(
        [(p,) for p in columns_out(grad_query_cat, part)],
        query_grad_body,
        [
            ((experts, depth, head_cols), F32, (local, depth, head_cols), lambda b: (b, 0, 0)),
            shared,
            shared,
        ],
        "query_grad",
    )
    logits_a = logits_a.reshape(seqs, seq_len, experts)
    grad_in, small_a = sublayer_back(
        block_in, seq3(inverse_a), gain_attn, router_attn, gates_a, logits_a,
        dots_a[..., :experts], dots_a[..., experts], dhidden_a,
    )
    grad_in = grad_mid + grad_in
    block_out = (mid + come_home(home_f, down_home)).astype(BF16)

    smalls = jnp.concatenate([small_a, small_f], axis=0)
    smalls = lax.all_gather(smalls, ("row", "col"), axis=0, tiled=False)
    smalls = smalls.reshape(ranks, -1, 2 * experts + 2, share)
    smalls = jnp.sum(smalls, axis=0).transpose(1, 0, 2).reshape(-1, width)
    return (
        block_out,
        grad_in,
        smalls[experts],
        smalls[2 * experts + 1],
        smalls[:experts].T,
        smalls[experts + 1 : 2 * experts + 1].T,
        grad_query_own,
        grad_key_own,
        grad_value_own,
        grad_out_own,
        whole_grad(gate_got).swapaxes(1, 2),
        whole_grad(up_got).swapaxes(1, 2),
        whole_grad(down_got),
    )


def solution(mesh):
    in_specs = (
        P(None, "row", "col"),
        P(None, "row", "col"),
        P(),
        P(),
        P(),
        P(),
        P(None, "row", "col"),
        P("row", "col"),
        P("row", "col"),
        P(None, "col", "row"),
        P(None, "row", "col"),
        P(None, "row", "col"),
        P(None, "col", "row"),
        P(None, "row", None),
        P(None, "row", None),
        P(None, "row", None),
        P(None, "row", None),
        P(),
    )
    out_specs = (
        P(None, "row", "col"),
        P(None, "row", "col"),
        P(),
        P(),
        P(),
        P(),
        P(None, "row", "col"),
        P("row", "col"),
        P("row", "col"),
        P(None, "col", "row"),
        P(None, "row", "col"),
        P(None, "row", "col"),
        P(None, "col", "row"),
    )
    return jax.shard_map(
        per_device, mesh=mesh, in_specs=in_specs, out_specs=out_specs, check_vma=False
    )
```

```python
from functools import partial
import math

import jax
import jax.numpy as jnp
from jax import lax
from jax.experimental import pallas as pl
from jax.experimental.pallas import tpu as pltpu
from jax.sharding import PartitionSpec as P

HEAD_DIM = 128
EPSILON = 1e-05
ROPE_BASE = 10000.0
MASKED_SCORE = -1e30
BF16 = jnp.bfloat16
F32 = jnp.float32


def dot_f32(spec, left, right):
    return jnp.einsum(spec, left, right, preferred_element_type=F32)


def tie(value, *others):
    return lax.optimization_barrier((value, others))[0]


def rope_tables(length):
    half_width = HEAD_DIM // 2
    frequency = jnp.exp(
        -math.log(ROPE_BASE) * jnp.arange(half_width, dtype=F32) * (2.0 / HEAD_DIM)
    )
    angles = jnp.arange(length, dtype=jnp.int32).astype(F32)[:, None] * frequency
    cosine, sine = jnp.cos(angles), jnp.sin(angles)
    return (
        jnp.concatenate([cosine, cosine], axis=-1),
        jnp.concatenate([-sine, sine], axis=-1),
    )


def expert_ranks(pairs, order, expert):
    names, places = (jnp.concatenate([a[0], a[1]], axis=-1) for a in (pairs, order))
    ahead = jnp.logical_and(
        places[..., None, :] < places[..., :, None], names[..., None, :] == expert
    )
    rank = jnp.sum(ahead.astype(F32), axis=-1).astype(jnp.int32)
    chosen = jnp.where(names == expert, rank, -1)
    half = chosen.shape[-1] // 2
    return jnp.maximum(chosen[..., :half], chosen[..., half:])


def all_ranks(pairs, order):
    names, places = (jnp.concatenate([a[0], a[1]], axis=-1) for a in (pairs, order))
    ahead = jnp.logical_and(
        places[..., None, :] < places[..., :, None], names[..., None, :] == names[..., :, None]
    )
    rank = jnp.sum(ahead.astype(F32), axis=-1).astype(jnp.int32)
    half = rank.shape[-1] // 2
    return jnp.stack([rank[..., :half], rank[..., half:]])


def slot_match(pairs, ranks, expert, capacity):
    rank_here = jnp.max(jnp.where(pairs == expert, ranks, -1), axis=0)
    slots = jnp.arange(capacity, dtype=jnp.int32)[:, None]
    return rank_here[..., None, :] == slots


def gate_table(logits, routes):
    ids = jnp.arange(logits.shape[-1], dtype=jnp.int32)
    chosen = jnp.any(routes[..., None] == ids, axis=0)
    masked = jnp.where(chosen, logits, MASKED_SCORE)
    top = jnp.max(masked, axis=-1, keepdims=True)
    exps = jnp.where(chosen, jnp.exp(masked - top), 0.0)
    return exps / jnp.sum(exps, axis=-1, keepdims=True)


def normalize_rows(wide):
    inverse = lax.rsqrt(jnp.mean(wide * wide, axis=-1, keepdims=True) + EPSILON)
    return (wide * inverse, inverse)


def roll_half(values):
    return pltpu.roll(values, HEAD_DIM // 2, 1)


def project_kernel(
    rotated, x_ref, gain_ref, router_ref, weight_ref, cos_ref, sin_ref,
    hidden_ref, inverse_ref, logits_ref, out_ref,
):
    normed, inverse = normalize_rows(x_ref[...].astype(F32))
    hidden = (normed * gain_ref[...]).astype(BF16)
    hidden_ref[...] = hidden
    inverse_ref[...] = inverse
    logits_ref[...] = jnp.dot(hidden, router_ref[...], preferred_element_type=F32)
    made = jnp.dot(hidden, weight_ref[...], preferred_element_type=F32)
    cosine, sine = cos_ref[...], sin_ref[...]
    for at, turn in enumerate(rotated):
        columns = slice(at * HEAD_DIM, (at + 1) * HEAD_DIM)
        one = made[:, columns]
        if turn:
            one = one * cosine + roll_half(one) * sine
        out_ref[:, columns] = one.astype(BF16)


def project(x, gain, router, weight, cosine, sine, rotated):
    count, width = x.shape
    experts, cols = router.shape[1], weight.shape[1]
    length = cosine.shape[0]
    tile = 512
    row = lambda n: pl.BlockSpec((tile, n), lambda i: (i, 0))
    whole = lambda a: pl.BlockSpec(a.shape, lambda i: (0, 0))
    table = pl.BlockSpec((tile, HEAD_DIM), lambda i: (lax.rem(i, length // tile), 0))
    return pl.pallas_call(
        partial(project_kernel, rotated),
        grid=(count // tile,),
        in_specs=[row(width), pl.BlockSpec((1, width), lambda i: (0, 0)), whole(router),
                  whole(weight), table, table],
        out_specs=[row(width), row(1), row(experts), row(cols)],
        out_shape=[
            jax.ShapeDtypeStruct((count, width), BF16),
            jax.ShapeDtypeStruct((count, 1), F32),
            jax.ShapeDtypeStruct((count, experts), F32),
            jax.ShapeDtypeStruct((count, cols), BF16),
        ],
        compiler_params=pltpu.CompilerParams(vmem_limit_bytes=48 * 1024 * 1024),
        cost_estimate=pl.CostEstimate(
            flops=2 * count * width * cols,
            bytes_accessed=4 * count * width + 2 * count * cols,
            transcendentals=count,
        ),
        name="project",
    )(x, gain.reshape(1, width), router, weight, cosine, sine)


def scores_of(q, k, qblk, kblk):
    raw = lax.dot_general(q, k, (((1,), (1,)), ((), ())), preferred_element_type=F32)
    return jnp.where(kblk <= qblk, raw * HEAD_DIM ** (-0.5), MASKED_SCORE)


def head_part(ref, at):
    return ref[0, :, at * HEAD_DIM : (at + 1) * HEAD_DIM]


def pick_rows(match, tokens):
    return jnp.dot(match, tokens, preferred_element_type=F32).astype(BF16)


def put_rows(match, rows):
    first = (((0,), (0,)), ((), ()))
    return lax.dot_general(match, rows, first, preferred_element_type=F32)


def slot_rows_of(target_ref, kblk, rows):
    local, length = target_ref.shape[1:]
    at = lax.broadcasted_iota(jnp.int32, (rows, length), 0)
    found = [target_ref[0, j : j + 1] == at for j in range(local)]
    blocks = [
        jnp.sum(jnp.where(m, kblk.astype(F32), 0.0), axis=-1, keepdims=True) for m in found
    ]
    return found, [jnp.where(m, 1.0, 0.0).astype(BF16) for m in found], blocks


def attend_kernel(
    rows, qkv_ref, target_ref, gate_ref, kblk_ref, slot_ref, plain_ref, scaled_ref, lse_ref
):
    local = target_ref.shape[1]
    kblk = kblk_ref[0]
    found, match, blocks = slot_rows_of(target_ref, kblk, rows)
    q = jnp.concatenate([pick_rows(match[j], head_part(qkv_ref, j)) for j in range(local)], axis=0)
    k, v = head_part(qkv_ref, local), head_part(qkv_ref, local + 1)
    scores = scores_of(q, k, jnp.concatenate(blocks, axis=0), kblk.astype(F32))
    top = jnp.max(scores, axis=-1, keepdims=True)
    exps = jnp.exp(scores - top)
    total = jnp.sum(exps, axis=-1, keepdims=True)
    probs = (exps * (1.0 / total)).astype(BF16)
    out = jnp.dot(probs, v, preferred_element_type=F32).astype(BF16)
    lse_ref[0, 0] = top + jnp.log(total)
    for j in range(local):
        here = out[j * rows : (j + 1) * rows]
        gate = jnp.sum(jnp.where(found[j], gate_ref[0, j : j + 1], 0.0), axis=-1, keepdims=True)
        scaled = (here.astype(F32) * gate).astype(BF16)
        columns = slice(j * HEAD_DIM, (j + 1) * HEAD_DIM)
        slot_ref[j, 0] = scaled
        plain_ref[0, :, columns] = put_rows(match[j], here).astype(BF16)
        scaled_ref[0, :, columns] = put_rows(match[j], scaled).astype(BF16)


def attend(qkv, target, gates, kblk, rows, heads):
    seqs, length, cols = qkv.shape
    local = target.shape[1]
    token = lambda n: pl.BlockSpec((1, length, n * HEAD_DIM), lambda s, h: (s, 0, h))
    lane = lambda n: pl.BlockSpec((1, n, length), lambda s, h: (s, 0, 0))
    of_tokens = jax.ShapeDtypeStruct((seqs, length, heads * local * HEAD_DIM), BF16)
    total = local * rows
    return pl.pallas_call(
        partial(attend_kernel, rows),
        grid=(seqs, heads),
        in_specs=[token(local + 2), lane(local), lane(local), lane(1)],
        out_specs=[
            pl.BlockSpec((local, 1, rows, HEAD_DIM), lambda s, h: (0, s, 0, h)),
            token(local),
            token(local),
            pl.BlockSpec((1, 1, total, 1), lambda s, h: (s, h, 0, 0)),
        ],
        out_shape=[
            jax.ShapeDtypeStruct((local, seqs, rows, heads * HEAD_DIM), BF16),
            of_tokens,
            of_tokens,
            jax.ShapeDtypeStruct((seqs, heads, total, 1), F32),
        ],
        compiler_params=pltpu.CompilerParams(vmem_limit_bytes=56 * 1024 * 1024),
        cost_estimate=pl.CostEstimate(
            flops=12 * seqs * heads * total * length * HEAD_DIM,
            bytes_accessed=4 * qkv.size,
            transcendentals=seqs * heads * total * length,
        ),
        name="attend",
    )(qkv, target, gates, kblk)


def attend_back_kernel(
    rows, qkv_ref, target_ref, kblk_ref, lse_ref, plain_ref, raw_ref, gate_ref, cos_ref, sin_ref,
    out_ref, dots_ref,
):
    local = target_ref.shape[1]
    kblk = kblk_ref[0]
    _, match, blocks = slot_rows_of(target_ref, kblk, rows)
    q = jnp.concatenate([pick_rows(match[j], head_part(qkv_ref, j)) for j in range(local)], axis=0)
    k, v = head_part(qkv_ref, local), head_part(qkv_ref, local + 1)
    grads, dots = [], []
    for j in range(local):
        raw = head_part(raw_ref, j)
        gated = (raw * gate_ref[0, :, j : j + 1]).astype(BF16)
        grads.append(pick_rows(match[j], gated))
        dots.append(jnp.sum(raw * head_part(plain_ref, j).astype(F32), axis=-1, keepdims=True))
    g = jnp.concatenate(grads, axis=0)
    scores = scores_of(q, k, jnp.concatenate(blocks, axis=0), kblk.astype(F32))
    probs = jnp.exp(scores - lse_ref[0, 0])
    grad = lax.dot_general(g, v, (((1,), (1,)), ((), ())), preferred_element_type=F32)
    inner = jnp.sum(probs * grad, axis=-1, keepdims=True)
    grad_scores = (probs * (grad - inner) * HEAD_DIM ** (-0.5)).astype(BF16)
    dq = jnp.dot(grad_scores, k, preferred_element_type=F32)
    cosine, sine = cos_ref[...], sin_ref[...]
    inner_sum = 0.0
    turn = lambda value: (value * cosine - roll_half(value) * sine).astype(BF16)
    for j in range(local):
        here = dq[j * rows : (j + 1) * rows]
        high = here.astype(BF16)
        low = (here - high.astype(F32)).astype(BF16)
        placed = put_rows(match[j], high) + put_rows(match[j], low)
        out_ref[0, :, j * HEAD_DIM : (j + 1) * HEAD_DIM] = turn(placed)
        inner_sum = inner_sum + placed * head_part(qkv_ref, j).astype(F32)
    dk = put_rows(grad_scores, q)
    out_ref[0, :, local * HEAD_DIM : (local + 1) * HEAD_DIM] = turn(dk)
    dv = put_rows(probs.astype(BF16), g)
    out_ref[0, :, (local + 1) * HEAD_DIM : (local + 2) * HEAD_DIM] = dv.astype(BF16)
    inner_sum = inner_sum + dk * k.astype(F32) + dv * v.astype(F32)
    dots.append(jnp.sum(inner_sum, axis=-1, keepdims=True))
    for at in range(local + 1):

        @pl.when(pl.program_id(1) == 0)
        def _():
            dots_ref[0, :, at : at + 1] = dots[at]

        @pl.when(pl.program_id(1) > 0)
        def _():
            dots_ref[0, :, at : at + 1] = dots_ref[0, :, at : at + 1] + dots[at]


def attend_back(qkv, target, kblk, lse, plain, raw, gate_cols, cosine, sine, rows, heads):
    seqs, length, cols = qkv.shape
    local = target.shape[1]
    token = lambda n: pl.BlockSpec((1, length, n * HEAD_DIM), lambda s, h: (s, 0, h))
    lane = lambda n: pl.BlockSpec((1, n, length), lambda s, h: (s, 0, 0))
    total = local * rows
    column = pl.BlockSpec((1, length, local), lambda s, h: (s, 0, 0))
    table = pl.BlockSpec((length, HEAD_DIM), lambda s, h: (0, 0))
    return pl.pallas_call(
        partial(attend_back_kernel, rows),
        grid=(seqs, heads),
        in_specs=[
            token(local + 2),
            lane(local),
            lane(1),
            pl.BlockSpec((1, 1, total, 1), lambda s, h: (s, h, 0, 0)),
            token(local),
            token(local),
            column,
            table,
            table,
        ],
        out_specs=[
            token(local + 2),
            pl.BlockSpec((1, length, local + 1), lambda s, h: (s, 0, 0)),
        ],
        out_shape=[
            jax.ShapeDtypeStruct(qkv.shape, BF16),
            jax.ShapeDtypeStruct((seqs, length, local + 1), F32),
        ],
        compiler_params=pltpu.CompilerParams(vmem_limit_bytes=60 * 1024 * 1024),
        cost_estimate=pl.CostEstimate(
            flops=24 * seqs * heads * total * length * HEAD_DIM,
            bytes_accessed=8 * qkv.size,
            transcendentals=seqs * heads * total * length,
        ),
        name="attend_back",
    )(qkv, target, kblk, lse, plain, raw, gate_cols, cosine, sine)


def dispatch_body(target_ref, tokens, out_refs):
    rows = out_refs[0].shape[1]
    at = lax.broadcasted_iota(jnp.int32, (rows, tokens.shape[0]), 0)
    for j, out_ref in enumerate(out_refs):
        match = jnp.where(target_ref[0, j : j + 1] == at, 1.0, 0.0).astype(BF16)
        out_ref[0] = pick_rows(match, tokens[...])


def dispatch_kernel(x_ref, target_ref, *out_refs):
    dispatch_body(target_ref, x_ref.at[0], out_refs)


def norm_dispatch_kernel(step, x_ref, target_ref, gain_ref, router_ref, *refs):
    *out_refs, inverse_ref, logits_ref, hidden_ref = refs
    for first in range(0, x_ref.shape[1], step):
        rows = slice(first, first + step)
        normed, inverse = normalize_rows(x_ref[0, rows].astype(F32))
        hidden = (normed * gain_ref[...]).astype(BF16)
        hidden_ref[rows] = hidden
        inverse_ref[0, rows] = inverse
        logits_ref[0, rows] = jnp.dot(hidden, router_ref[...], preferred_element_type=F32)
    dispatch_body(target_ref, hidden_ref, out_refs)


def dispatch(x, target, rows, norm=None):
    seqs, length, width = x.shape
    local = target.shape[1]
    token = lambda n: pl.BlockSpec((1, length, n), lambda s: (s, 0, 0))
    in_specs = [token(width), pl.BlockSpec((1, local, length), lambda s: (s, 0, 0))]
    out_specs = [pl.BlockSpec((1, rows, width), lambda s: (s, 0, 0)) for _ in range(local)]
    out_shape = [jax.ShapeDtypeStruct((seqs, rows, width), BF16) for _ in range(local)]
    args, kernel, scratch = [x, target], dispatch_kernel, []
    if norm is not None:
        gain, router = norm
        experts = router.shape[1]
        in_specs += [
            pl.BlockSpec((1, width), lambda s: (0, 0)),
            pl.BlockSpec(router.shape, lambda s: (0, 0)),
        ]
        out_specs += [token(1), token(experts)]
        out_shape += [
            jax.ShapeDtypeStruct((seqs, length, 1), F32),
            jax.ShapeDtypeStruct((seqs, length, experts), F32),
        ]
        args += [gain.reshape(1, width), router]
        kernel = partial(norm_dispatch_kernel, 256)
        scratch = [pltpu.VMEM((length, width), BF16)]
    return pl.pallas_call(
        kernel,
        grid=(seqs,),
        in_specs=in_specs,
        out_specs=out_specs,
        out_shape=out_shape,
        scratch_shapes=scratch,
        compiler_params=pltpu.CompilerParams(vmem_limit_bytes=56 * 1024 * 1024),
        cost_estimate=pl.CostEstimate(
            flops=2 * local * seqs * rows * length * width,
            bytes_accessed=2 * x.size + 2 * local * seqs * rows * width,
            transcendentals=0,
        ),
        name="dispatch",
    )(*args)


def expert_kernel(
    x_ref, grad_ref, weight_ref, gate_ref, up_ref, down_ref,
    scaled_ref, grad_gate_ref, grad_up_ref, back_ref, dots_ref,
):
    last = (((1,), (1,)), ((), ()))
    x, weight = x_ref[...], weight_ref[...]
    gate_pre = lax.dot_general(x, gate_ref[...], last, preferred_element_type=F32)
    up_pre = lax.dot_general(x, up_ref[...], last, preferred_element_type=F32)
    raw = lax.dot_general(grad_ref[...], down_ref[...], last, preferred_element_type=F32)
    gate_sig = jax.nn.sigmoid(gate_pre)
    gate_silu = gate_pre * gate_sig
    activated = gate_silu * up_pre
    scaled_ref[...] = (activated * weight).astype(BF16)
    grad_act = raw * weight
    grad_gate = grad_act * up_pre * (gate_sig * (1.0 + gate_pre * (1.0 - gate_sig)))
    grad_gate = grad_gate.astype(BF16)
    grad_up = (grad_act * gate_silu).astype(BF16)
    grad_gate_ref[...] = grad_gate
    grad_up_ref[...] = grad_up
    back = jnp.dot(grad_gate, gate_ref[...], preferred_element_type=F32)
    back = back + jnp.dot(grad_up, up_ref[...], preferred_element_type=F32)
    back_ref[...] = back.astype(BF16)
    inner = grad_gate.astype(F32) * gate_pre + grad_up.astype(F32) * up_pre
    dots_ref[:, 0:1] = jnp.sum(raw * activated, axis=-1, keepdims=True)
    dots_ref[:, 1:2] = jnp.sum(inner, axis=-1, keepdims=True)


def expert_step(x, grad, weight, gate_w, up_w, down_w, tile):
    count, width = x.shape
    units = gate_w.shape[0]
    row = lambda n: pl.BlockSpec((tile, n), lambda i: (i, 0))
    whole = pl.BlockSpec((units, width), lambda i: (0, 0))
    shape = lambda n, dtype=BF16: jax.ShapeDtypeStruct((count, n), dtype)
    return pl.pallas_call(
        expert_kernel,
        grid=(count // tile,),
        in_specs=[row(width), row(width), row(1), whole, whole, whole],
        out_specs=[row(units), row(units), row(units), row(width), row(2)],
        out_shape=[shape(units), shape(units), shape(units), shape(width), shape(2, F32)],
        compiler_params=pltpu.CompilerParams(vmem_limit_bytes=56 * 1024 * 1024),
        cost_estimate=pl.CostEstimate(
            flops=10 * count * width * units,
            bytes_accessed=6 * count * (width + units) + 6 * width * units,
            transcendentals=count * units,
        ),
        name="expert_step",
    )(x, grad, weight, gate_w, up_w, down_w)


def gather_rows(own):
    return lax.all_gather(own, "row", axis=1, tiled=True)


def gather_cols(rows):
    return lax.all_gather(rows, "col", axis=2, tiled=True)


def exchange(parts):
    return lax.all_to_all(parts, "row", 0, 0)


def cut_pieces(piece_for):
    ranks, row = lax.axis_size("row"), lax.axis_index("row")
    return [piece_for(lax.rem(row + m, ranks)) for m in range(ranks)]


def exchange_pieces(pieces, *after):
    ranks = lax.axis_size("row")
    got = pieces[:1]
    for m in range(1, ranks):
        steps = [(i, (i + m) % ranks) for i in range(ranks)]
        got.append(lax.ppermute(tie(pieces[m], *after), "row", steps))
    return got


def cut_group(*parts):
    pieces = cut_pieces(lambda n: jnp.concatenate([piece_for(n) for piece_for, _ in parts], axis=0))
    return pieces, [rows for _, rows in parts]


def exchange_group(group, *after):
    pieces, counts = group
    got = exchange_pieces(pieces, *after)
    placed, first = [], 0
    for rows in counts:
        placed.append((got, first, rows))
        first += rows
    return got, placed


def assemble(pieces, body, outs, name):
    ranks, each = len(pieces), len(pieces[0])

    def kernel(row_ref, *refs):
        for m in range(ranks):

            @pl.when(pl.program_id(0) == m)
            def _():
                body(m, refs[m * each : (m + 1) * each], refs[ranks * each :])

    def at(index):
        return lambda m, row: index(lax.rem(row[0] - m + ranks, ranks))

    flat = [a for piece in pieces for a in piece]
    whole = lambda a: pl.BlockSpec(a.shape, lambda m, row: (0,) * a.ndim)
    return pl.pallas_call(
        kernel,
        grid_spec=pltpu.PrefetchScalarGridSpec(
            num_scalar_prefetch=1,
            grid=(ranks,),
            in_specs=[whole(a) for a in flat],
            out_specs=[pl.BlockSpec(block, at(index)) for _, _, block, index in outs],
        ),
        out_shape=[jax.ShapeDtypeStruct(shape, dtype) for shape, dtype, _, _ in outs],
        compiler_params=pltpu.CompilerParams(vmem_limit_bytes=48 * 1024 * 1024),
        cost_estimate=pl.CostEstimate(
            flops=0, bytes_accessed=4 * sum(a.size for a in flat), transcendentals=0
        ),
        name=name,
    )(lax.axis_index("row").astype(jnp.int32).reshape(1), *flat)


def place_rows(outs, at, refs, spans, dtype):
    to = 0
    for ref, (first, rows) in zip(refs, spans):
        piece = ref[first : first + rows].astype(dtype)
        if at is None:
            outs[to : to + rows] = piece
        else:
            outs[at, to : to + rows] = piece
        to += rows


def spread_kernel(into_ref, weight_ref, extra_ref, out_ref):
    last = (((1,), (1,)), ((), ()))
    tokens, copies = into_ref.shape[1], out_ref.shape[2] // extra_ref.shape[2]
    rows = lax.dot_general(into_ref[0], weight_ref[...], last, preferred_element_type=F32)
    out_ref[0, :tokens] = rows.astype(BF16)
    share = extra_ref.shape[2]
    for at in range(copies):
        out_ref[0, tokens:, at * share : (at + 1) * share] = extra_ref[0]


def spread(into, weight, extra):
    blocks, tokens, depth = into.shape
    width = weight.shape[0]
    rows = tokens + extra.shape[1]
    block = lambda a: pl.BlockSpec((1, *a.shape[1:]), lambda i: (i, 0, 0))
    return pl.pallas_call(
        spread_kernel,
        grid=(blocks,),
        in_specs=[block(into), pl.BlockSpec(weight.shape, lambda i: (0, 0)), block(extra)],
        out_specs=pl.BlockSpec((1, rows, width), lambda i: (i, 0, 0)),
        out_shape=jax.ShapeDtypeStruct((blocks, rows, width), BF16),
        compiler_params=pltpu.CompilerParams(vmem_limit_bytes=48 * 1024 * 1024),
        cost_estimate=pl.CostEstimate(
            flops=2 * blocks * tokens * depth * width,
            bytes_accessed=2 * blocks * (tokens * depth + rows * width),
            transcendentals=0,
        ),
        name="spread",
    )(into, weight, extra)


def sum_cols(rows):
    return lax.psum_scatter(rows, "col", scatter_dimension=1, tiled=True)


def round_up(count, unit):
    return -(-count // unit) * unit


def rows_home(own, seqs, capacity, extra=None):
    ranks, share = lax.axis_size("row"), own.shape[-1]
    rows = own.reshape(-1, seqs, ranks, capacity, share).transpose(2, 1, 0, 3, 4)
    rows = rows.reshape(ranks, -1, share)
    count = rows.shape[1]
    if extra is not None:
        rows = jnp.concatenate([rows, extra], axis=1)
    got = exchange(rows)
    home = got[:, :count].reshape(ranks, seqs, -1, share).swapaxes(0, 1)
    return home.reshape(seqs, -1, share), got[:, count:]


def per_device(
    block_in,
    grad_out,
    gain_attn,
    gain_ffn,
    router_attn,
    router_ffn,
    w_query,
    key_weight,
    value_weight,
    w_out,
    w_gate,
    w_up,
    w_down,
    routes_attn,
    routes_ffn,
    order_attn,
    order_ffn,
    block_ids,
):
    seqs, seq_dev, share = block_in.shape
    experts, depth, head_cols = w_query.shape
    capacity = 18 * seq_dev // (8 * experts)
    heads = head_cols // HEAD_DIM
    hidden_units = w_gate.shape[2]
    width = gain_attn.shape[0]
    seq_len = block_ids.shape[1]
    ranks = lax.axis_size("row")
    local = experts // ranks
    row_at, col_at = lax.axis_index("row"), lax.axis_index("col")
    slot_rows = seqs * ranks * capacity
    count = seqs * seq_len

    def own_features(whole):
        return lax.dynamic_slice_in_dim(whole, col_at * share, share, whole.ndim - 1)

    def own_tokens(whole):
        return lax.dynamic_slice_in_dim(whole, row_at * seq_dev, seq_dev, 1)

    def by_pair(table):
        return table.reshape(seqs, seq_dev, 2).transpose(2, 0, 1)

    small = jnp.stack([by_pair(t) for t in (routes_attn, order_attn, routes_ffn, order_ffn)])
    split = jnp.concatenate([small % 256, small[1::2] // 256]).astype(BF16)
    split = split.transpose(2, 0, 1, 3).reshape(seqs, -1)
    held = split.shape[1]
    table_rows = round_up(held, 16 * share) // share
    split = jnp.pad(split, ((0, 0), (0, table_rows * share - held)))
    in_rows = gather_rows(
        jnp.concatenate([block_in, split.reshape(seqs, table_rows, share)], axis=1)
    ).reshape(seqs, ranks, -1, share)
    split = in_rows[:, :, seq_dev:].reshape(seqs, ranks, -1)[..., :held].astype(jnp.int32)
    split = split.reshape(seqs, ranks, 6, 2, seq_dev).transpose(2, 3, 0, 1, 4)
    small_all = [split[0], split[1] + 256 * split[4], split[2], split[3] + 256 * split[5]]
    in_rows = in_rows[:, :, :seq_dev].reshape(seqs, seq_len, share)

    def halves(height, half):
        return (0, height) if half is None else (half * (height // 2), height // 2)

    def expert_part(weight, j, half=None):
        first, rows = halves(weight.shape[1], half)

        def piece_for(n):
            at = (n * local + j, first, 0)
            return lax.dynamic_slice(weight, at, (1, rows, weight.shape[2]))[0]

        return piece_for, rows

    def rows_in(placed):
        spans = [part[1:] for part in placed]
        pieces = [tuple(part[0][m] for part in placed) for m in range(ranks)]

        def body(m, ins, outs):
            place_rows(outs[0], None, ins, spans, BF16)

        out = ((hidden_units, width), BF16, (hidden_units, depth), lambda b: (0, b))
        return assemble(pieces, body, [out], "rows_in")[0]

    w_gate, w_up = w_gate.swapaxes(1, 2), w_up.swapaxes(1, 2)

    def group_in(weight):
        grouped = weight.reshape(ranks, local, *weight.shape[1:])
        return lambda n: lax.dynamic_index_in_dim(grouped, n, 0, keepdims=False)

    parts = local + 2
    key_value = jnp.stack([key_weight, value_weight])

    query_for = group_in(w_query)
    cosine, sine = rope_tables(seq_len)
    query_parts = cut_pieces(lambda n: jnp.concatenate([query_for(n), key_value]))
    in_rows = tie(in_rows, cosine, sine, *query_parts)
    query_got = exchange_pieces(query_parts, in_rows)

    def query_body(m, ins, outs):
        for h in range(heads):
            for p in range(parts):
                at = (h * parts + p) * HEAD_DIM
                piece = ins[0][p, :, h * HEAD_DIM : (h + 1) * HEAD_DIM]
                outs[0][:, at : at + HEAD_DIM] = piece

    made_cols = heads * parts * HEAD_DIM
    query_w = assemble(
        [(p,) for p in query_got],
        query_body,
        [((width, made_cols), BF16, (depth, made_cols), lambda b: (b, 0))],
        "query_in",
    )[0]

    mine = [row_at * local + j for j in range(local)]

    def tokens_to_slots(pairs, order):
        first = jnp.arange(ranks, dtype=jnp.int32)[:, None] * capacity
        out = []
        for e in mine:
            rank = expert_ranks(pairs, order, e)
            kept = jnp.logical_and(rank >= 0, rank < capacity)
            out.append(jnp.where(kept, first + rank, -1).reshape(seqs, seq_len))
        return jnp.stack(out, axis=1)

    target_a = tokens_to_slots(small_all[0], small_all[1])
    target_f = tokens_to_slots(small_all[2], small_all[3])
    routes_a = small_all[0].reshape(2, seqs, seq_len)
    routes_f = small_all[2].reshape(2, seqs, seq_len)
    w_out, w_gate, w_up, w_down = tie((w_out, w_gate, w_up, w_down), *query_got[1:2])
    out_parts = cut_pieces(group_in(w_out))
    group_a = cut_group(expert_part(w_gate, 0), expert_part(w_up, 0, 0))
    group_b = cut_group(expert_part(w_up, 0, 1), expert_part(w_down, 0))
    group_c = [cut_group(expert_part(w_gate, j), expert_part(w_up, j)) for j in range(1, local)]
    group_d = [
        [cut_group(expert_part(w_down, j, half)) for half in (0, 1)] for j in range(1, local)
    ]
    out_got = exchange_pieces(out_parts, *query_got)

    def home_match(pairs, order):
        ranks_here = all_ranks(pairs, order)
        every = [slot_match(pairs, ranks_here, e, capacity) for e in range(experts)]
        return jnp.concatenate(every, axis=1).astype(BF16)

    home_a = home_match(small[0], small[1])
    home_f = home_match(small[2], small[3])

    def come_home(match, rows):
        return dot_f32("sct,scf->stf", match, rows)

    def my_gates(gates):
        return jnp.stack(
            [lax.dynamic_index_in_dim(gates, e, 2, keepdims=False) for e in mine], axis=1
        )

    in_all = gather_cols(in_rows).reshape(count, width)
    in_all = tie(
        in_all, target_a, target_f, home_a, home_f, out_parts, group_a, group_b, group_c, group_d
    )
    rotated = ([True] * (local + 1) + [False]) * heads
    hidden_a, inverse_a, logits_a, qkv = project(
        in_all, gain_attn, router_attn, query_w, cosine, sine, rotated
    )
    qkv = qkv.reshape(seqs, seq_len, -1)
    grad_rows = gather_rows(tie(grad_out, in_all))
    gates_a = gate_table(
        logits_a.reshape(seqs, seq_len, experts), routes_a
    )
    my_gates_a = my_gates(gates_a)
    kblk = block_ids.reshape(seqs, 1, seq_len)
    rows_each = ranks * capacity
    att_slot, att_plain, att_scaled, log_totals = attend(
        qkv, target_a, my_gates_a, kblk, rows_each, heads
    )
    def out_body(m, ins, outs):
        for j in range(local):
            outs[1][j] = ins[0][j]
            for h in range(heads):
                at = (h * local + j) * HEAD_DIM
                outs[0][at : at + HEAD_DIM] = ins[0][j, h * HEAD_DIM : (h + 1) * HEAD_DIM]

    rows_cat = heads * local * HEAD_DIM
    out_cat, out_w = assemble(
        [(p,) for p in tie(out_got, att_slot)],
        out_body,
        [
            ((rows_cat, width), BF16, (rows_cat, depth), lambda b: (0, b)),
            ((local, head_cols, width), BF16, (local, head_cols, depth), lambda b: (0, 0, b)),
        ],
        "out_in",
    )

    out_slots = dot_f32(
        "jrf,jfd->jrd", att_slot.reshape(local, slot_rows, head_cols), out_w
    ).astype(BF16)
    out_slots = tie(out_slots.reshape(-1, width), grad_rows)
    got, (gate_in, up_first) = exchange_group(group_a, *out_got)
    out_own = tie(sum_cols(out_slots), *got)
    out_home, _ = rows_home(out_own, seqs, capacity)
    mid = block_in.astype(F32) + come_home(home_a, out_home)

    mid_low = mid.astype(BF16)
    mid_rows = gather_rows(mid_low)
    mid_all = gather_cols(mid_rows).reshape(count, width)
    got, (up_second, down_in) = exchange_group(group_b, mid_rows)
    mid_all = tie(mid_all, *got)
    arrived = [([gate_in], [up_first, up_second], [down_in])]
    out_grad_all = gather_cols(tie(grad_rows, mid_all))
    for j in range(1, local):
        got, (gate_in, up_in) = exchange_group(group_c[j - 1], mid_all)
        out_grad_all = tie(out_grad_all, *got)
        arrived.append(([gate_in], [up_in], []))
    seq3 = lambda a: a.reshape(seqs, seq_len, -1)
    *slot_in, inverse_f, logits_f = dispatch(
        seq3(mid_all), target_f, rows_each, (gain_ffn, router_ffn)
    )
    slot_in = [x.reshape(slot_rows, width) for x in slot_in]
    slot_grad_out = dispatch(out_grad_all, target_f, rows_each)
    slot_grad_out = [x.reshape(slot_rows, width) for x in slot_grad_out]
    gates_f = gate_table(logits_f, routes_f)
    my_gates_f = my_gates(gates_f)
    blocked = lambda a: a.reshape(seqs, ranks, seq_dev)
    slots_at = jnp.arange(capacity, dtype=jnp.int32)[:, None]
    first_at = jnp.arange(ranks, dtype=jnp.int32)[:, None, None] * capacity
    match_f = [blocked(target_f[:, j])[:, :, None, :] == first_at + slots_at for j in range(local)]
    weights_f = [
        jnp.sum(
            jnp.where(match_f[j], blocked(my_gates_f[:, j])[:, :, None, :], 0.0), axis=-1
        ).reshape(slot_rows, 1)
        for j in range(local)
    ]

    slot_grads_f, dots_f = [], []
    grads_gate, grads_up, grads_down, down_slots = [], [], [], []
    pieces = tie([[part[0] for part in placed] for placed in arrived[0]], slot_in[0])
    arrived[0] = [
        [(got, *part[1:]) for got, part in zip(held, placed)]
        for held, placed in zip(pieces, arrived[0])
    ]
    next_w = rows_in(arrived[0][0]), rows_in(arrived[0][1])
    for j in range(local):
        x = slot_in[j]
        if j > 0:
            x = tie(x, grads_gate[-1], grads_up[-1], grads_down[-1], down_slots[-1])
        gate_w, up_w = next_w
        down_w = rows_in(arrived[j][2])
        scaled, grad_gate, grad_up, slot_grad, dots = expert_step(
            x, slot_grad_out[j], weights_f[j], gate_w, up_w, down_w, rows_each
        )
        dots = dots.reshape(seqs, ranks, capacity, 2).transpose(1, 3, 0, 2).reshape(ranks, -1)
        dots_f.append(dots.astype(BF16))
        if j + 1 < local:
            got, (down_first,) = exchange_group(group_d[j][0], out_grad_all)
            slot_grad = tie(slot_grad, *got)
            got, (down_second,) = exchange_group(group_d[j][1], slot_grad)
            arrived[j + 1][2].extend([down_first, down_second])
            gate_in, up_in = arrived[j + 1][0][0], arrived[j + 1][1][0]
            held = tie(gate_in[0], got[1])
            next_w = rows_in([(held, *gate_in[1:])]), rows_in([(held, *up_in[1:])])
            made = tie((scaled, grad_gate, grad_up), got[1], next_w)
            grads_down.append(dot_f32("rf,rd->fd", made[0], slot_grad_out[j]).astype(BF16))
            grads_gate.append(dot_f32("rf,rd->fd", made[1], slot_in[j]).astype(BF16))
            grads_up.append(dot_f32("rf,rd->fd", made[2], slot_in[j]).astype(BF16))
            down = jnp.dot(made[0], down_w, preferred_element_type=F32)
            down_slots.append(down.astype(BF16))
        slot_grads_f.append(slot_grad)

    def grad_part(grad, half=None):
        first, rows = halves(grad.shape[0], half)

        def piece_for(n):
            return lax.dynamic_slice(grad, (first, n * depth), (rows, depth))

        return piece_for, rows

    def whole_grad(placed):
        flat = [part for parts in placed for part in parts]
        counts = [len(parts) for parts in placed]
        pieces = [tuple(part[0][m] for part in flat) for m in range(ranks)]

        def body(m, ins, outs):
            first = 0
            for j, held in enumerate(counts):
                spans = [part[1:] for part in placed[j]]
                place_rows(outs[0], j, ins[first : first + held], spans, F32)
                first += held

        rows = hidden_units
        out = ((experts, rows, depth), F32, (local, rows, depth), lambda b: (b, 0, 0))
        return assemble(pieces, body, [out], "whole_grad")[0]

    def sublayer_back(own_in, inverse_all, gain, router, gates_all, logits_all, dots, inner, dhidden):
        gates = own_tokens(gates_all)
        inverse = own_tokens(inverse_all)
        dlogits = gates * (dots - jnp.sum(gates * dots, axis=-1, keepdims=True))
        dlogits = dlogits.astype(BF16)
        gain_own = own_features(gain)
        router_own = lax.dynamic_slice_in_dim(router, col_at * share, share, 0)
        normed = own_in.astype(F32) * inverse
        hidden = (normed * gain_own).astype(BF16)
        dhidden = dhidden + dot_f32("ste,fe->stf", dlogits, router_own)
        grad_router = dot_f32("ste,stf->ef", dlogits, hidden)
        grad_gain = jnp.sum(dhidden * normed, axis=(0, 1))
        dn = dhidden * gain_own
        inner = inner + jnp.sum(dlogits.astype(F32) * own_tokens(logits_all), axis=-1)
        grad = inverse * (dn - normed * (inner / width)[..., None])
        return grad, jnp.concatenate([grad_router, grad_gain[None]], axis=0)

    first_grads = (grads_down, grads_gate, grads_up)
    if local == 1:
        first_grads = ([scaled], [grad_gate], [grad_up])
        for grads, rows in zip(first_grads, (slot_grad_out[0], slot_in[0], slot_in[0])):
            grads[0] = dot_f32("rf,rd->fd", grads[0], rows).astype(BF16)
    grads_down, grads_gate, grads_up = first_grads
    got, (down_first,) = exchange_group(
        cut_group(grad_part(grads_down[0], 0)), *[part[0][-1] for part in arrived[-1][2]]
    )
    slot_grads_f[-1] = tie(slot_grads_f[-1], *got)
    group_a = cut_group(grad_part(grads_down[0], 1), grad_part(grads_gate[0], 0))
    group_b = cut_group(grad_part(grads_gate[0], 1), grad_part(grads_up[0]))
    got, (down_second, gate_first) = exchange_group(group_a, slot_grads_f[-1])
    per_row = dots_f[0].shape[1]
    dot_rows = round_up(per_row, share) // share
    under = round_up(ranks * dot_rows, 16)
    own_rows, own_dots = [], []
    for rows, dots in zip(slot_grads_f, dots_f):
        dots = jnp.pad(dots, ((0, 0), (0, dot_rows * share - per_row)))
        dots = jnp.pad(dots.reshape(-1, share), ((0, under - ranks * dot_rows), (0, 0)))
        dots = jnp.tile(dots, (1, width // share))
        own = sum_cols(jnp.concatenate([rows, dots], axis=0))
        own_rows.append(own[:slot_rows])
        own_dots.append(own[slot_rows : slot_rows + ranks * dot_rows].reshape(ranks, -1, share))
    own_rows = tie(jnp.concatenate(own_rows, axis=0), *got)
    made = tie((scaled, grad_gate, grad_up), own_rows)
    if local > 1:
        grads_down.append(dot_f32("rf,rd->fd", made[0], slot_grad_out[-1]).astype(BF16))
        grads_gate.append(dot_f32("rf,rd->fd", made[1], slot_in[-1]).astype(BF16))
        grads_up.append(dot_f32("rf,rd->fd", made[2], slot_in[-1]).astype(BF16))
    down_slots.append(jnp.dot(made[0], down_w, preferred_element_type=F32).astype(BF16))
    grad_home, dots_home = rows_home(
        own_rows, seqs, capacity, jnp.concatenate(own_dots, axis=1)
    )
    dhidden_f = come_home(home_f, grad_home)
    dots_home = dots_home.reshape(ranks, local, -1)[..., :per_row].astype(F32)
    dots_home = dots_home.reshape(experts, 2, seqs, capacity, 1).transpose(1, 2, 0, 3, 4)
    match_home = home_f.reshape(seqs, experts, capacity, seq_dev).astype(F32)
    dots_home = jnp.sum(dots_home * match_home, axis=3).swapaxes(2, 3)
    grad_mid, small_f = sublayer_back(
        mid_low, inverse_f, gain_ffn, router_ffn, gates_f, logits_f,
        dots_home[0], jnp.sum(dots_home[1], axis=-1), dhidden_f,
    )
    grad_mid = grad_out.astype(F32) + grad_mid

    mid_grad_rows = gather_rows(grad_mid.astype(BF16))
    mid_grad_rows = tie(mid_grad_rows, group_b, *grads_down, *grads_gate, *grads_up, *down_slots)
    group_c = [
        cut_group(grad_part(grads_down[j]), grad_part(grads_gate[j], 0)) for j in range(1, local)
    ]
    group_d = [
        cut_group(grad_part(grads_gate[j], 1), grad_part(grads_up[j])) for j in range(1, local)
    ]
    mid_grad_all = gather_cols(mid_grad_rows).reshape(count, width)
    got, (gate_second, up_got) = exchange_group(group_b, mid_grad_rows)
    down_slots = jnp.concatenate(down_slots, axis=0)
    mid_grad_all = tie(mid_grad_all, down_slots, group_c, group_d, *got)
    down_parts, gate_parts = [[down_first, down_second]], [[gate_first, gate_second]]
    up_parts = [[up_got]]
    down_slots = tie(down_slots, mid_grad_all)
    down_own = sum_cols(down_slots)
    grad_raw = dot_f32("rd,fd->rf", mid_grad_all, out_cat)
    early = []
    for j in range(1, local):
        got, (down_got, gate_first) = exchange_group(group_c[j - 1], mid_grad_all)
        down_parts.append([down_got])
        gate_parts.append([gate_first])
        early += got
    into, dots_a = attend_back(
        qkv, target_a, kblk, log_totals, att_plain, seq3(grad_raw), my_gates_a.swapaxes(1, 2),
        cosine, sine, rows_each, heads,
    )
    placed = jnp.zeros((seqs, ranks, experts, seq_dev), F32)
    dots_a = dots_a.reshape(seqs, ranks, seq_dev, local + 1).swapaxes(2, 3)
    placed = lax.dynamic_update_slice_in_dim(placed, dots_a[:, :, :local], row_at * local, 2)
    extra = jnp.concatenate([placed, dots_a[:, :, local:]], axis=2).astype(BF16)
    extra = extra.reshape(seqs * ranks, -1)
    held = extra.shape[1]
    under = round_up(held, 16 * share) // share
    extra = jnp.pad(extra, ((0, 0), (0, under * share - held)))
    token_part = spread(
        into.reshape(seqs * ranks, seq_dev, -1), query_w, extra.reshape(-1, under, share)
    ).reshape(seqs, -1, width)
    token_part = tie(token_part, down_own, *early)
    last = []
    for j in range(1, local):
        got, (gate_second, up_got) = exchange_group(group_d[j - 1], token_part)
        gate_parts[j].append(gate_second)
        up_parts.append([up_got])
        last += got
    att_scaled = tie(att_scaled, *last[1:2]).reshape(count, -1)
    grad_out_cat = dot_f32("rf,rd->fd", att_scaled, mid_grad_all).astype(BF16)
    down_home, _ = rows_home(tie(down_own, token_part), seqs, capacity)
    part = lax.psum_scatter(token_part, "col", scatter_dimension=2, tiled=True)
    into = tie(into, *last[1:2]).reshape(count, -1)
    grad_query_cat = dot_f32("rd,rf->df", hidden_a, into).astype(BF16)
    out_pieces = exchange_pieces(cut_pieces(grad_part(grad_out_cat)[0]), *last[1:2])
    part = tie(part, *last, down_home, grad_query_cat, *out_pieces[1:2])
    own = lax.psum_scatter(part, "row", scatter_dimension=1, tiled=True)
    def out_grad_body(m, ins, outs):
        for j in range(local):
            for h in range(heads):
                at = (h * local + j) * HEAD_DIM
                piece = ins[0][at : at + HEAD_DIM].astype(F32)
                outs[0][j, h * HEAD_DIM : (h + 1) * HEAD_DIM] = piece

    grad_out_own = assemble(
        [(p,) for p in out_pieces],
        out_grad_body,
        [((experts, head_cols, depth), F32, (local, head_cols, depth), lambda b: (b, 0, 0))],
        "out_grad",
    )[0]
    gate_all, up_all, down_all = (whole_grad(p) for p in (gate_parts, up_parts, down_parts))
    own = tie(own, gate_all, up_all, down_all)
    dhidden_a = own[:, :seq_dev].astype(F32)
    dots_a = own[:, seq_dev:].reshape(seqs, -1)[:, :held].astype(F32)
    dots_a = dots_a.reshape(seqs, experts + 1, seq_dev).swapaxes(1, 2)

    def query_part(half):
        rows = depth // 2
        return cut_pieces(
            lambda n: lax.dynamic_slice_in_dim(grad_query_cat, n * depth + half * rows, rows, 0)
        )

    query_first = exchange_pieces(query_part(0), part)
    logits_a = logits_a.reshape(seqs, seq_len, experts)
    grad_in, small_a = sublayer_back(
        block_in, seq3(inverse_a), gain_attn, router_attn, gates_a, logits_a,
        dots_a[..., :experts], dots_a[..., experts], dhidden_a,
    )
    grad_in = grad_mid + grad_in
    block_out = (mid + come_home(home_f, down_home)).astype(BF16)

    smalls = jnp.concatenate([small_a, small_f], axis=0)
    high = smalls.astype(BF16)
    smalls = jnp.stack([high, (smalls - high.astype(F32)).astype(BF16)]).reshape(-1)
    held = smalls.shape[0]
    under = round_up(held, 16 * made_cols) // made_cols
    smalls = jnp.pad(smalls, (0, under * made_cols - held)).reshape(under, made_cols)
    query_second = exchange_pieces(
        [jnp.concatenate([piece, smalls], axis=0) for piece in query_part(1)]
    )
    smalls = sum(piece[depth // 2 :].astype(F32) for piece in query_second)
    smalls = jnp.sum(smalls.reshape(-1)[:held].reshape(2, -1, share), axis=0)
    smalls = lax.all_gather(smalls, "col", axis=1, tiled=True)
    def query_grad_body(m, ins, outs):
        for h in range(heads):
            columns = slice(h * HEAD_DIM, (h + 1) * HEAD_DIM)
            for p in range(parts):
                at = (h * parts + p) * HEAD_DIM
                for half in range(2):
                    rows = slice(half * (depth // 2), (half + 1) * (depth // 2))
                    piece = ins[half][: depth // 2, at : at + HEAD_DIM].astype(F32)
                    if p < local:
                        outs[0][p, rows, columns] = piece
                    elif m == 0:
                        outs[1 + p - local][rows, columns] = piece
                    else:
                        total = outs[1 + p - local][rows, columns] + piece
                        outs[1 + p - local][rows, columns] = total

    shared = ((depth, head_cols), F32, (depth, head_cols), lambda b: (0, 0))
    grad_query_own, grad_key_own, grad_value_own = assemble(
        list(zip(query_first, query_second)),
        query_grad_body,
        [
            ((experts, depth, head_cols), F32, (local, depth, head_cols), lambda b: (b, 0, 0)),
            shared,
            shared,
        ],
        "query_grad",
    )
    return (
        block_out,
        grad_in,
        smalls[experts],
        smalls[2 * experts + 1],
        smalls[:experts].T,
        smalls[experts + 1 : 2 * experts + 1].T,
        grad_query_own,
        grad_key_own,
        grad_value_own,
        grad_out_own,
        gate_all.swapaxes(1, 2),
        up_all.swapaxes(1, 2),
        down_all,
    )


def solution(mesh):
    in_specs = (
        P(None, "row", "col"),
        P(None, "row", "col"),
        P(),
        P(),
        P(),
        P(),
        P(None, "row", "col"),
        P("row", "col"),
        P("row", "col"),
        P(None, "col", "row"),
        P(None, "row", "col"),
        P(None, "row", "col"),
        P(None, "col", "row"),
        P(None, "row", None),
        P(None, "row", None),
        P(None, "row", None),
        P(None, "row", None),
        P(),
    )
    out_specs = (
        P(None, "row", "col"),
        P(None, "row", "col"),
        P(),
        P(),
        P(),
        P(),
        P(None, "row", "col"),
        P("row", "col"),
        P("row", "col"),
        P(None, "col", "row"),
        P(None, "row", "col"),
        P(None, "row", "col"),
        P(None, "col", "row"),
    )
    return jax.shard_map(
        per_device, mesh=mesh, in_specs=in_specs, out_specs=out_specs, check_vma=False
    )
```

```python
from functools import partial
import math

import jax
import jax.numpy as jnp
from jax import lax
from jax.experimental import pallas as pl
from jax.experimental.pallas import tpu as pltpu
from jax.sharding import PartitionSpec as P

HEAD_DIM = 128
EPSILON = 1e-05
ROPE_BASE = 10000.0
MASKED_SCORE = -1e30
BF16 = jnp.bfloat16
F32 = jnp.float32


def dot_f32(spec, left, right):
    return jnp.einsum(spec, left, right, preferred_element_type=F32)


def tie(value, *others):
    return lax.optimization_barrier((value, others))[0]


def rope_tables(length):
    half_width = HEAD_DIM // 2
    frequency = jnp.exp(
        -math.log(ROPE_BASE) * jnp.arange(half_width, dtype=F32) * (2.0 / HEAD_DIM)
    )
    angles = jnp.arange(length, dtype=jnp.int32).astype(F32)[:, None] * frequency
    cosine, sine = jnp.cos(angles), jnp.sin(angles)
    return (
        jnp.concatenate([cosine, cosine], axis=-1),
        jnp.concatenate([-sine, sine], axis=-1),
    )


def expert_ranks(pairs, order, expert):
    names, places = (jnp.concatenate([a[0], a[1]], axis=-1) for a in (pairs, order))
    ahead = jnp.logical_and(
        places[..., None, :] < places[..., :, None], names[..., None, :] == expert
    )
    rank = jnp.sum(ahead.astype(F32), axis=-1).astype(jnp.int32)
    chosen = jnp.where(names == expert, rank, -1)
    half = chosen.shape[-1] // 2
    return jnp.maximum(chosen[..., :half], chosen[..., half:])


def all_ranks(pairs, order):
    names, places = (jnp.concatenate([a[0], a[1]], axis=-1) for a in (pairs, order))
    ahead = jnp.logical_and(
        places[..., None, :] < places[..., :, None], names[..., None, :] == names[..., :, None]
    )
    rank = jnp.sum(ahead.astype(F32), axis=-1).astype(jnp.int32)
    half = rank.shape[-1] // 2
    return jnp.stack([rank[..., :half], rank[..., half:]])


def slot_match(pairs, ranks, expert, capacity):
    rank_here = jnp.max(jnp.where(pairs == expert, ranks, -1), axis=0)
    slots = jnp.arange(capacity, dtype=jnp.int32)[:, None]
    return rank_here[..., None, :] == slots


def gate_table(logits, routes):
    ids = jnp.arange(logits.shape[-1], dtype=jnp.int32)
    chosen = jnp.any(routes[..., None] == ids, axis=0)
    masked = jnp.where(chosen, logits, MASKED_SCORE)
    top = jnp.max(masked, axis=-1, keepdims=True)
    exps = jnp.where(chosen, jnp.exp(masked - top), 0.0)
    return exps / jnp.sum(exps, axis=-1, keepdims=True)


def normalize_rows(wide):
    inverse = lax.rsqrt(jnp.mean(wide * wide, axis=-1, keepdims=True) + EPSILON)
    return (wide * inverse, inverse)


def roll_half(values):
    return pltpu.roll(values, HEAD_DIM // 2, 1)


def project_kernel(
    rotated, x_ref, gain_ref, router_ref, weight_ref, cos_ref, sin_ref,
    hidden_ref, inverse_ref, logits_ref, out_ref,
):
    normed, inverse = normalize_rows(x_ref[...].astype(F32))
    hidden = (normed * gain_ref[...]).astype(BF16)
    hidden_ref[...] = hidden
    inverse_ref[...] = inverse
    logits_ref[...] = jnp.dot(hidden, router_ref[...], preferred_element_type=F32)
    made = jnp.dot(hidden, weight_ref[...], preferred_element_type=F32)
    cosine, sine = cos_ref[...], sin_ref[...]
    for at, turn in enumerate(rotated):
        columns = slice(at * HEAD_DIM, (at + 1) * HEAD_DIM)
        one = made[:, columns]
        if turn:
            one = one * cosine + roll_half(one) * sine
        out_ref[:, columns] = one.astype(BF16)


def project(x, gain, router, weight, cosine, sine, rotated):
    count, width = x.shape
    experts, cols = router.shape[1], weight.shape[1]
    length = cosine.shape[0]
    tile = 512
    row = lambda n: pl.BlockSpec((tile, n), lambda i: (i, 0))
    whole = lambda a: pl.BlockSpec(a.shape, lambda i: (0, 0))
    table = pl.BlockSpec((tile, HEAD_DIM), lambda i: (lax.rem(i, length // tile), 0))
    return pl.pallas_call(
        partial(project_kernel, rotated),
        grid=(count // tile,),
        in_specs=[row(width), pl.BlockSpec((1, width), lambda i: (0, 0)), whole(router),
                  whole(weight), table, table],
        out_specs=[row(width), row(1), row(experts), row(cols)],
        out_shape=[
            jax.ShapeDtypeStruct((count, width), BF16),
            jax.ShapeDtypeStruct((count, 1), F32),
            jax.ShapeDtypeStruct((count, experts), F32),
            jax.ShapeDtypeStruct((count, cols), BF16),
        ],
        compiler_params=pltpu.CompilerParams(vmem_limit_bytes=48 * 1024 * 1024),
        cost_estimate=pl.CostEstimate(
            flops=2 * count * width * cols,
            bytes_accessed=4 * count * width + 2 * count * cols,
            transcendentals=count,
        ),
        name="project",
    )(x, gain.reshape(1, width), router, weight, cosine, sine)


def scores_of(q, k, qblk, kblk):
    raw = lax.dot_general(q, k, (((1,), (1,)), ((), ())), preferred_element_type=F32)
    return jnp.where(kblk <= qblk, raw * HEAD_DIM ** (-0.5), MASKED_SCORE)


def head_part(ref, at):
    return ref[0, :, at * HEAD_DIM : (at + 1) * HEAD_DIM]


def pick_rows(match, tokens):
    return jnp.dot(match, tokens, preferred_element_type=F32).astype(BF16)


def put_rows(match, rows):
    first = (((0,), (0,)), ((), ()))
    return lax.dot_general(match, rows, first, preferred_element_type=F32)


def slot_rows_of(target_ref, kblk, rows):
    local, length = target_ref.shape[1:]
    at = lax.broadcasted_iota(jnp.int32, (rows, length), 0)
    found = [target_ref[0, j : j + 1] == at for j in range(local)]
    blocks = [
        jnp.sum(jnp.where(m, kblk.astype(F32), 0.0), axis=-1, keepdims=True) for m in found
    ]
    return found, [jnp.where(m, 1.0, 0.0).astype(BF16) for m in found], blocks


def attend_kernel(
    rows, qkv_ref, target_ref, gate_ref, kblk_ref, slot_ref, plain_ref, scaled_ref, lse_ref
):
    local = target_ref.shape[1]
    kblk = kblk_ref[0]
    found, match, blocks = slot_rows_of(target_ref, kblk, rows)
    q = jnp.concatenate([pick_rows(match[j], head_part(qkv_ref, j)) for j in range(local)], axis=0)
    k, v = head_part(qkv_ref, local), head_part(qkv_ref, local + 1)
    scores = scores_of(q, k, jnp.concatenate(blocks, axis=0), kblk.astype(F32))
    top = jnp.max(scores, axis=-1, keepdims=True)
    exps = jnp.exp(scores - top)
    total = jnp.sum(exps, axis=-1, keepdims=True)
    probs = (exps * (1.0 / total)).astype(BF16)
    out = jnp.dot(probs, v, preferred_element_type=F32).astype(BF16)
    lse_ref[0, 0] = top + jnp.log(total)
    for j in range(local):
        here = out[j * rows : (j + 1) * rows]
        gate = jnp.sum(jnp.where(found[j], gate_ref[0, j : j + 1], 0.0), axis=-1, keepdims=True)
        scaled = (here.astype(F32) * gate).astype(BF16)
        columns = slice(j * HEAD_DIM, (j + 1) * HEAD_DIM)
        slot_ref[j, 0] = scaled
        plain_ref[0, :, columns] = put_rows(match[j], here).astype(BF16)
        scaled_ref[0, :, columns] = put_rows(match[j], scaled).astype(BF16)


def attend(qkv, target, gates, kblk, rows, heads):
    seqs, length, cols = qkv.shape
    local = target.shape[1]
    token = lambda n: pl.BlockSpec((1, length, n * HEAD_DIM), lambda s, h: (s, 0, h))
    lane = lambda n: pl.BlockSpec((1, n, length), lambda s, h: (s, 0, 0))
    of_tokens = jax.ShapeDtypeStruct((seqs, length, heads * local * HEAD_DIM), BF16)
    total = local * rows
    return pl.pallas_call(
        partial(attend_kernel, rows),
        grid=(seqs, heads),
        in_specs=[token(local + 2), lane(local), lane(local), lane(1)],
        out_specs=[
            pl.BlockSpec((local, 1, rows, HEAD_DIM), lambda s, h: (0, s, 0, h)),
            token(local),
            token(local),
            pl.BlockSpec((1, 1, total, 1), lambda s, h: (s, h, 0, 0)),
        ],
        out_shape=[
            jax.ShapeDtypeStruct((local, seqs, rows, heads * HEAD_DIM), BF16),
            of_tokens,
            of_tokens,
            jax.ShapeDtypeStruct((seqs, heads, total, 1), F32),
        ],
        compiler_params=pltpu.CompilerParams(vmem_limit_bytes=56 * 1024 * 1024),
        cost_estimate=pl.CostEstimate(
            flops=12 * seqs * heads * total * length * HEAD_DIM,
            bytes_accessed=4 * qkv.size,
            transcendentals=seqs * heads * total * length,
        ),
        name="attend",
    )(qkv, target, gates, kblk)


def attend_back_kernel(
    rows, qkv_ref, target_ref, kblk_ref, lse_ref, plain_ref, raw_ref, gate_ref, cos_ref, sin_ref,
    out_ref, dots_ref,
):
    local = target_ref.shape[1]
    kblk = kblk_ref[0]
    _, match, blocks = slot_rows_of(target_ref, kblk, rows)
    q = jnp.concatenate([pick_rows(match[j], head_part(qkv_ref, j)) for j in range(local)], axis=0)
    k, v = head_part(qkv_ref, local), head_part(qkv_ref, local + 1)
    grads, dots = [], []
    for j in range(local):
        raw = head_part(raw_ref, j)
        gated = (raw * gate_ref[0, :, j : j + 1]).astype(BF16)
        grads.append(pick_rows(match[j], gated))
        dots.append(jnp.sum(raw * head_part(plain_ref, j).astype(F32), axis=-1, keepdims=True))
    g = jnp.concatenate(grads, axis=0)
    scores = scores_of(q, k, jnp.concatenate(blocks, axis=0), kblk.astype(F32))
    probs = jnp.exp(scores - lse_ref[0, 0])
    grad = lax.dot_general(g, v, (((1,), (1,)), ((), ())), preferred_element_type=F32)
    inner = jnp.sum(probs * grad, axis=-1, keepdims=True)
    grad_scores = (probs * (grad - inner) * HEAD_DIM ** (-0.5)).astype(BF16)
    dq = jnp.dot(grad_scores, k, preferred_element_type=F32)
    cosine, sine = cos_ref[...], sin_ref[...]
    inner_sum = 0.0
    turn = lambda value: (value * cosine - roll_half(value) * sine).astype(BF16)
    for j in range(local):
        here = dq[j * rows : (j + 1) * rows]
        high = here.astype(BF16)
        low = (here - high.astype(F32)).astype(BF16)
        placed = put_rows(match[j], high) + put_rows(match[j], low)
        out_ref[0, :, j * HEAD_DIM : (j + 1) * HEAD_DIM] = turn(placed)
        inner_sum = inner_sum + placed * head_part(qkv_ref, j).astype(F32)
    dk = put_rows(grad_scores, q)
    out_ref[0, :, local * HEAD_DIM : (local + 1) * HEAD_DIM] = turn(dk)
    dv = put_rows(probs.astype(BF16), g)
    out_ref[0, :, (local + 1) * HEAD_DIM : (local + 2) * HEAD_DIM] = dv.astype(BF16)
    inner_sum = inner_sum + dk * k.astype(F32) + dv * v.astype(F32)
    dots.append(jnp.sum(inner_sum, axis=-1, keepdims=True))
    for at in range(local + 1):

        @pl.when(pl.program_id(1) == 0)
        def _():
            dots_ref[0, :, at : at + 1] = dots[at]

        @pl.when(pl.program_id(1) > 0)
        def _():
            dots_ref[0, :, at : at + 1] = dots_ref[0, :, at : at + 1] + dots[at]


def attend_back(qkv, target, kblk, lse, plain, raw, gate_cols, cosine, sine, rows, heads):
    seqs, length, cols = qkv.shape
    local = target.shape[1]
    token = lambda n: pl.BlockSpec((1, length, n * HEAD_DIM), lambda s, h: (s, 0, h))
    lane = lambda n: pl.BlockSpec((1, n, length), lambda s, h: (s, 0, 0))
    total = local * rows
    column = pl.BlockSpec((1, length, local), lambda s, h: (s, 0, 0))
    table = pl.BlockSpec((length, HEAD_DIM), lambda s, h: (0, 0))
    return pl.pallas_call(
        partial(attend_back_kernel, rows),
        grid=(seqs, heads),
        in_specs=[
            token(local + 2),
            lane(local),
            lane(1),
            pl.BlockSpec((1, 1, total, 1), lambda s, h: (s, h, 0, 0)),
            token(local),
            token(local),
            column,
            table,
            table,
        ],
        out_specs=[
            token(local + 2),
            pl.BlockSpec((1, length, local + 1), lambda s, h: (s, 0, 0)),
        ],
        out_shape=[
            jax.ShapeDtypeStruct(qkv.shape, BF16),
            jax.ShapeDtypeStruct((seqs, length, local + 1), F32),
        ],
        compiler_params=pltpu.CompilerParams(vmem_limit_bytes=60 * 1024 * 1024),
        cost_estimate=pl.CostEstimate(
            flops=0,
            bytes_accessed=4 * qkv.size,
            transcendentals=0,
        ),
        name="attend_back",
    )(qkv, target, kblk, lse, plain, raw, gate_cols, cosine, sine)


def dispatch_body(target_ref, tokens, out_refs):
    rows = out_refs[0].shape[1]
    at = lax.broadcasted_iota(jnp.int32, (rows, tokens.shape[0]), 0)
    for j, out_ref in enumerate(out_refs):
        match = jnp.where(target_ref[0, j : j + 1] == at, 1.0, 0.0).astype(BF16)
        out_ref[0] = pick_rows(match, tokens[...])


def dispatch_kernel(x_ref, target_ref, *out_refs):
    dispatch_body(target_ref, x_ref.at[0], out_refs)


def norm_dispatch_kernel(step, x_ref, target_ref, gain_ref, router_ref, *refs):
    *out_refs, inverse_ref, logits_ref, hidden_ref = refs
    for first in range(0, x_ref.shape[1], step):
        rows = slice(first, first + step)
        normed, inverse = normalize_rows(x_ref[0, rows].astype(F32))
        hidden = (normed * gain_ref[...]).astype(BF16)
        hidden_ref[rows] = hidden
        inverse_ref[0, rows] = inverse
        logits_ref[0, rows] = jnp.dot(hidden, router_ref[...], preferred_element_type=F32)
    dispatch_body(target_ref, hidden_ref, out_refs)


def dispatch(x, target, rows, norm=None):
    seqs, length, width = x.shape
    local = target.shape[1]
    token = lambda n: pl.BlockSpec((1, length, n), lambda s: (s, 0, 0))
    in_specs = [token(width), pl.BlockSpec((1, local, length), lambda s: (s, 0, 0))]
    out_specs = [pl.BlockSpec((1, rows, width), lambda s: (s, 0, 0)) for _ in range(local)]
    out_shape = [jax.ShapeDtypeStruct((seqs, rows, width), BF16) for _ in range(local)]
    args, kernel, scratch = [x, target], dispatch_kernel, []
    if norm is not None:
        gain, router = norm
        experts = router.shape[1]
        in_specs += [
            pl.BlockSpec((1, width), lambda s: (0, 0)),
            pl.BlockSpec(router.shape, lambda s: (0, 0)),
        ]
        out_specs += [token(1), token(experts)]
        out_shape += [
            jax.ShapeDtypeStruct((seqs, length, 1), F32),
            jax.ShapeDtypeStruct((seqs, length, experts), F32),
        ]
        args += [gain.reshape(1, width), router]
        kernel = partial(norm_dispatch_kernel, 256)
        scratch = [pltpu.VMEM((length, width), BF16)]
    return pl.pallas_call(
        kernel,
        grid=(seqs,),
        in_specs=in_specs,
        out_specs=out_specs,
        out_shape=out_shape,
        scratch_shapes=scratch,
        compiler_params=pltpu.CompilerParams(vmem_limit_bytes=56 * 1024 * 1024),
        cost_estimate=pl.CostEstimate(
            flops=0,
            bytes_accessed=2 * x.size,
            transcendentals=0,
        ),
        name="dispatch",
    )(*args)


def expert_kernel(
    x_ref, grad_ref, weight_ref, gate_ref, up_ref, down_ref,
    scaled_ref, grad_gate_ref, grad_up_ref, back_ref, dots_ref,
):
    last = (((1,), (1,)), ((), ()))
    x, weight = x_ref[...], weight_ref[...]
    gate_pre = lax.dot_general(x, gate_ref[...], last, preferred_element_type=F32)
    up_pre = lax.dot_general(x, up_ref[...], last, preferred_element_type=F32)
    raw = lax.dot_general(grad_ref[...], down_ref[...], last, preferred_element_type=F32)
    gate_sig = jax.nn.sigmoid(gate_pre)
    gate_silu = gate_pre * gate_sig
    activated = gate_silu * up_pre
    scaled_ref[...] = (activated * weight).astype(BF16)
    grad_act = raw * weight
    grad_gate = grad_act * up_pre * (gate_sig * (1.0 + gate_pre * (1.0 - gate_sig)))
    grad_gate = grad_gate.astype(BF16)
    grad_up = (grad_act * gate_silu).astype(BF16)
    grad_gate_ref[...] = grad_gate
    grad_up_ref[...] = grad_up
    back = jnp.dot(grad_gate, gate_ref[...], preferred_element_type=F32)
    back = back + jnp.dot(grad_up, up_ref[...], preferred_element_type=F32)
    back_ref[...] = back.astype(BF16)
    inner = grad_gate.astype(F32) * gate_pre + grad_up.astype(F32) * up_pre
    dots_ref[:, 0:1] = jnp.sum(raw * activated, axis=-1, keepdims=True)
    dots_ref[:, 1:2] = jnp.sum(inner, axis=-1, keepdims=True)


def expert_step(x, grad, weight, gate_w, up_w, down_w, tile):
    count, width = x.shape
    units = gate_w.shape[0]
    row = lambda n: pl.BlockSpec((tile, n), lambda i: (i, 0))
    whole = pl.BlockSpec((units, width), lambda i: (0, 0))
    shape = lambda n, dtype=BF16: jax.ShapeDtypeStruct((count, n), dtype)
    return pl.pallas_call(
        expert_kernel,
        grid=(count // tile,),
        in_specs=[row(width), row(width), row(1), whole, whole, whole],
        out_specs=[row(units), row(units), row(units), row(width), row(2)],
        out_shape=[shape(units), shape(units), shape(units), shape(width), shape(2, F32)],
        compiler_params=pltpu.CompilerParams(vmem_limit_bytes=56 * 1024 * 1024),
        cost_estimate=pl.CostEstimate(
            flops=0,
            bytes_accessed=6 * width * units,
            transcendentals=0,
        ),
        name="expert_step",
    )(x, grad, weight, gate_w, up_w, down_w)


def gather_rows(own):
    return lax.all_gather(own, "row", axis=1, tiled=True)


def gather_cols(rows):
    return lax.all_gather(rows, "col", axis=2, tiled=True)


def exchange(parts):
    return lax.all_to_all(parts, "row", 0, 0)


def cut_pieces(piece_for):
    ranks, row = lax.axis_size("row"), lax.axis_index("row")
    return [piece_for(lax.rem(row + m, ranks)) for m in range(ranks)]


def exchange_pieces(pieces, *after):
    ranks = lax.axis_size("row")
    got = pieces[:1]
    for m in range(1, ranks):
        steps = [(i, (i + m) % ranks) for i in range(ranks)]
        got.append(lax.ppermute(tie(pieces[m], *after), "row", steps))
    return got


def cut_group(*parts):
    pieces = cut_pieces(lambda n: jnp.concatenate([piece_for(n) for piece_for, _ in parts], axis=0))
    return pieces, [rows for _, rows in parts]


def exchange_group(group, *after):
    pieces, counts = group
    got = exchange_pieces(pieces, *after)
    placed, first = [], 0
    for rows in counts:
        placed.append((got, first, rows))
        first += rows
    return got, placed


def assemble(pieces, body, outs, name):
    ranks, each = len(pieces), len(pieces[0])

    def kernel(row_ref, *refs):
        for m in range(ranks):

            @pl.when(pl.program_id(0) == m)
            def _():
                body(m, refs[m * each : (m + 1) * each], refs[ranks * each :])

    def at(index):
        return lambda m, row: index(lax.rem(row[0] - m + ranks, ranks))

    flat = [a for piece in pieces for a in piece]
    whole = lambda a: pl.BlockSpec(a.shape, lambda m, row: (0,) * a.ndim)
    return pl.pallas_call(
        kernel,
        grid_spec=pltpu.PrefetchScalarGridSpec(
            num_scalar_prefetch=1,
            grid=(ranks,),
            in_specs=[whole(a) for a in flat],
            out_specs=[pl.BlockSpec(block, at(index)) for _, _, block, index in outs],
        ),
        out_shape=[jax.ShapeDtypeStruct(shape, dtype) for shape, dtype, _, _ in outs],
        compiler_params=pltpu.CompilerParams(vmem_limit_bytes=48 * 1024 * 1024),
        cost_estimate=pl.CostEstimate(
            flops=0, bytes_accessed=4 * sum(a.size for a in flat), transcendentals=0
        ),
        name=name,
    )(lax.axis_index("row").astype(jnp.int32).reshape(1), *flat)


def place_rows(outs, at, refs, spans, dtype):
    to = 0
    for ref, (first, rows) in zip(refs, spans):
        piece = ref[first : first + rows].astype(dtype)
        if at is None:
            outs[to : to + rows] = piece
        else:
            outs[at, to : to + rows] = piece
        to += rows


def spread_kernel(into_ref, weight_ref, extra_ref, out_ref):
    last = (((1,), (1,)), ((), ()))
    tokens, copies = into_ref.shape[1], out_ref.shape[2] // extra_ref.shape[2]
    rows = lax.dot_general(into_ref[0], weight_ref[...], last, preferred_element_type=F32)
    out_ref[0, :tokens] = rows.astype(BF16)
    share = extra_ref.shape[2]
    for at in range(copies):
        out_ref[0, tokens:, at * share : (at + 1) * share] = extra_ref[0]


def spread(into, weight, extra):
    blocks, tokens, depth = into.shape
    width = weight.shape[0]
    rows = tokens + extra.shape[1]
    block = lambda a: pl.BlockSpec((1, *a.shape[1:]), lambda i: (i, 0, 0))
    return pl.pallas_call(
        spread_kernel,
        grid=(blocks,),
        in_specs=[block(into), pl.BlockSpec(weight.shape, lambda i: (0, 0)), block(extra)],
        out_specs=pl.BlockSpec((1, rows, width), lambda i: (i, 0, 0)),
        out_shape=jax.ShapeDtypeStruct((blocks, rows, width), BF16),
        compiler_params=pltpu.CompilerParams(vmem_limit_bytes=48 * 1024 * 1024),
        cost_estimate=pl.CostEstimate(
            flops=0,
            bytes_accessed=2 * blocks * rows * width,
            transcendentals=0,
        ),
        name="spread",
    )(into, weight, extra)


def sum_cols(rows):
    return lax.psum_scatter(rows, "col", scatter_dimension=1, tiled=True)


def round_up(count, unit):
    return -(-count // unit) * unit


def rows_home(own, seqs, capacity, extra=None):
    ranks, share = lax.axis_size("row"), own.shape[-1]
    rows = own.reshape(-1, seqs, ranks, capacity, share).transpose(2, 1, 0, 3, 4)
    rows = rows.reshape(ranks, -1, share)
    count = rows.shape[1]
    if extra is not None:
        rows = jnp.concatenate([rows, extra], axis=1)
    got = exchange(rows)
    home = got[:, :count].reshape(ranks, seqs, -1, share).swapaxes(0, 1)
    return home.reshape(seqs, -1, share), got[:, count:]


def per_device(
    block_in,
    grad_out,
    gain_attn,
    gain_ffn,
    router_attn,
    router_ffn,
    w_query,
    key_weight,
    value_weight,
    w_out,
    w_gate,
    w_up,
    w_down,
    routes_attn,
    routes_ffn,
    order_attn,
    order_ffn,
    block_ids,
):
    seqs, seq_dev, share = block_in.shape
    experts, depth, head_cols = w_query.shape
    capacity = 18 * seq_dev // (8 * experts)
    heads = head_cols // HEAD_DIM
    hidden_units = w_gate.shape[2]
    width = gain_attn.shape[0]
    seq_len = block_ids.shape[1]
    ranks = lax.axis_size("row")
    local = experts // ranks
    row_at, col_at = lax.axis_index("row"), lax.axis_index("col")
    slot_rows = seqs * ranks * capacity
    count = seqs * seq_len

    def own_features(whole):
        return lax.dynamic_slice_in_dim(whole, col_at * share, share, whole.ndim - 1)

    def own_tokens(whole):
        return lax.dynamic_slice_in_dim(whole, row_at * seq_dev, seq_dev, 1)

    def by_pair(table):
        return table.reshape(seqs, seq_dev, 2).transpose(2, 0, 1)

    small = jnp.stack([by_pair(t) for t in (routes_attn, order_attn, routes_ffn, order_ffn)])
    split = jnp.concatenate([small % 256, small[1::2] // 256]).astype(BF16)
    split = split.transpose(2, 0, 1, 3).reshape(seqs, -1)
    held = split.shape[1]
    table_rows = round_up(held, 16 * share) // share
    split = jnp.pad(split, ((0, 0), (0, table_rows * share - held)))
    in_rows = gather_rows(
        jnp.concatenate([block_in, split.reshape(seqs, table_rows, share)], axis=1)
    ).reshape(seqs, ranks, -1, share)
    split = in_rows[:, :, seq_dev:].reshape(seqs, ranks, -1)[..., :held].astype(jnp.int32)
    split = split.reshape(seqs, ranks, 6, 2, seq_dev).transpose(2, 3, 0, 1, 4)
    small_all = [split[0], split[1] + 256 * split[4], split[2], split[3] + 256 * split[5]]
    in_rows = in_rows[:, :, :seq_dev].reshape(seqs, seq_len, share)

    def halves(height, half):
        return (0, height) if half is None else (half * (height // 2), height // 2)

    def expert_part(weight, j, half=None):
        first, rows = halves(weight.shape[1], half)

        def piece_for(n):
            at = (n * local + j, first, 0)
            return lax.dynamic_slice(weight, at, (1, rows, weight.shape[2]))[0]

        return piece_for, rows

    def rows_in(placed):
        spans = [part[1:] for part in placed]
        pieces = [tuple(part[0][m] for part in placed) for m in range(ranks)]

        def body(m, ins, outs):
            place_rows(outs[0], None, ins, spans, BF16)

        out = ((hidden_units, width), BF16, (hidden_units, depth), lambda b: (0, b))
        return assemble(pieces, body, [out], "rows_in")[0]

    w_gate, w_up = w_gate.swapaxes(1, 2), w_up.swapaxes(1, 2)

    def group_in(weight):
        grouped = weight.reshape(ranks, local, *weight.shape[1:])
        return lambda n: lax.dynamic_index_in_dim(grouped, n, 0, keepdims=False)

    parts = local + 2
    key_value = jnp.stack([key_weight, value_weight])

    query_for = group_in(w_query)
    cosine, sine = rope_tables(seq_len)
    query_parts = cut_pieces(lambda n: jnp.concatenate([query_for(n), key_value]))
    out_parts = cut_pieces(group_in(w_out))
    group_a = cut_group(expert_part(w_gate, 0), expert_part(w_up, 0, 0))
    group_b = cut_group(expert_part(w_up, 0, 1), expert_part(w_down, 0))
    group_c = [cut_group(expert_part(w_gate, j), expert_part(w_up, j)) for j in range(1, local)]
    group_d = [cut_group(expert_part(w_down, j)) for j in range(1, local)]
    in_rows = tie(
        in_rows, cosine, sine, query_parts, out_parts, group_a, group_b, group_c, group_d
    )
    query_got = exchange_pieces(query_parts, in_rows)

    def query_body(m, ins, outs):
        for h in range(heads):
            for p in range(parts):
                at = (h * parts + p) * HEAD_DIM
                piece = ins[0][p, :, h * HEAD_DIM : (h + 1) * HEAD_DIM]
                outs[0][:, at : at + HEAD_DIM] = piece

    made_cols = heads * parts * HEAD_DIM
    query_w = assemble(
        [(p,) for p in query_got],
        query_body,
        [((width, made_cols), BF16, (depth, made_cols), lambda b: (b, 0))],
        "query_in",
    )[0]

    mine = [row_at * local + j for j in range(local)]

    def tokens_to_slots(pairs, order):
        first = jnp.arange(ranks, dtype=jnp.int32)[:, None] * capacity
        out = []
        for e in mine:
            rank = expert_ranks(pairs, order, e)
            kept = jnp.logical_and(rank >= 0, rank < capacity)
            out.append(jnp.where(kept, first + rank, -1).reshape(seqs, seq_len))
        return jnp.stack(out, axis=1)

    target_a = tokens_to_slots(small_all[0], small_all[1])
    target_f = tokens_to_slots(small_all[2], small_all[3])
    routes_a = small_all[0].reshape(2, seqs, seq_len)
    routes_f = small_all[2].reshape(2, seqs, seq_len)

    def home_match(pairs, order):
        ranks_here = all_ranks(pairs, order)
        every = [slot_match(pairs, ranks_here, e, capacity) for e in range(experts)]
        return jnp.concatenate(every, axis=1).astype(BF16)

    home_a = home_match(small[0], small[1])
    home_f = home_match(small[2], small[3])

    def come_home(match, rows):
        return dot_f32("sct,scf->stf", match, rows)

    def my_gates(gates):
        return jnp.stack(
            [lax.dynamic_index_in_dim(gates, e, 2, keepdims=False) for e in mine], axis=1
        )

    in_all = gather_cols(in_rows).reshape(count, width)
    grad_sent = jnp.einsum("sct,stf->scf", home_f, grad_out)
    grad_sent = grad_sent.reshape(seqs, ranks, local, capacity, share).transpose(1, 2, 0, 3, 4)
    in_all = tie(
        in_all, target_a, target_f, home_a, home_f, grad_sent
    )
    rotated = ([True] * (local + 1) + [False]) * heads
    hidden_a, inverse_a, logits_a, qkv = project(
        in_all, gain_attn, router_attn, query_w, cosine, sine, rotated
    )
    qkv = qkv.reshape(seqs, seq_len, -1)
    out_got = exchange_pieces(out_parts, in_all)
    qkv = tie(qkv, *out_got)
    grad_rows = exchange(tie(grad_sent, qkv))
    gates_a = gate_table(
        logits_a.reshape(seqs, seq_len, experts), routes_a
    )
    my_gates_a = my_gates(gates_a)
    kblk = block_ids.reshape(seqs, 1, seq_len)
    rows_each = ranks * capacity
    att_slot, att_plain, att_scaled, log_totals = attend(
        qkv, target_a, my_gates_a, kblk, rows_each, heads
    )
    def out_body(m, ins, outs):
        for j in range(local):
            outs[1][j] = ins[0][j]
            for h in range(heads):
                at = (h * local + j) * HEAD_DIM
                outs[0][at : at + HEAD_DIM] = ins[0][j, h * HEAD_DIM : (h + 1) * HEAD_DIM]

    rows_cat = heads * local * HEAD_DIM
    out_cat, out_w = assemble(
        [(p,) for p in tie(out_got, att_slot)],
        out_body,
        [
            ((rows_cat, width), BF16, (rows_cat, depth), lambda b: (0, b)),
            ((local, head_cols, width), BF16, (local, head_cols, depth), lambda b: (0, 0, b)),
        ],
        "out_in",
    )

    out_slots = dot_f32(
        "jrf,jfd->jrd", att_slot.reshape(local, slot_rows, head_cols), out_w
    ).astype(BF16)
    out_slots = tie(out_slots.reshape(-1, width), grad_rows)
    got, (gate_in, up_first) = exchange_group(group_a, *out_got)
    out_own = tie(sum_cols(out_slots), *got)
    out_home, _ = rows_home(out_own, seqs, capacity)
    mid = block_in.astype(F32) + come_home(home_a, out_home)

    mid_low = mid.astype(BF16)
    mid_rows = gather_rows(mid_low)
    mid_all = gather_cols(mid_rows).reshape(count, width)
    got, (up_second, down_in) = exchange_group(group_b, mid_rows)
    mid_all = tie(mid_all, *got)
    arrived = [([gate_in], [up_first, up_second], [down_in])]
    grad_rows = tie(grad_rows, mid_all).transpose(1, 2, 0, 3, 4)
    grad_rows = grad_rows.reshape(local, slot_rows, share)
    slot_grad_out = [
        lax.all_gather(grad_rows[j], "col", axis=1, tiled=True) for j in range(local)
    ]
    held_back = []
    for j in range(1, local):
        got, (gate_in, up_in) = exchange_group(group_c[j - 1], mid_all)
        held_back += got
        arrived.append(([gate_in], [up_in], []))
    seq3 = lambda a: a.reshape(seqs, seq_len, -1)
    *slot_in, inverse_f, logits_f = dispatch(
        seq3(mid_all), target_f, rows_each, (gain_ffn, router_ffn)
    )
    slot_in = [x.reshape(slot_rows, width) for x in slot_in]
    gates_f = gate_table(logits_f, routes_f)
    my_gates_f = my_gates(gates_f)
    blocked = lambda a: a.reshape(seqs, ranks, seq_dev)
    slots_at = jnp.arange(capacity, dtype=jnp.int32)[:, None]
    first_at = jnp.arange(ranks, dtype=jnp.int32)[:, None, None] * capacity
    match_f = [blocked(target_f[:, j])[:, :, None, :] == first_at + slots_at for j in range(local)]
    weights_f = [
        jnp.sum(
            jnp.where(match_f[j], blocked(my_gates_f[:, j])[:, :, None, :], 0.0), axis=-1
        ).reshape(slot_rows, 1)
        for j in range(local)
    ]

    slot_grads_f, dots_f = [], []
    grads_gate, grads_up, grads_down, down_slots = [], [], [], []
    pieces = tie([[part[0] for part in placed] for placed in arrived[0]], slot_in[0])
    arrived[0] = [
        [(got, *part[1:]) for got, part in zip(held, placed)]
        for held, placed in zip(pieces, arrived[0])
    ]
    next_w = rows_in(arrived[0][0]), rows_in(arrived[0][1])
    for j in range(local):
        x = slot_in[j]
        gate_w, up_w = next_w
        down_w = rows_in(arrived[j][2])
        scaled, grad_gate, grad_up, slot_grad, dots = expert_step(
            x, slot_grad_out[j], weights_f[j], gate_w, up_w, down_w, rows_each
        )
        dots = dots.reshape(seqs, ranks, capacity, 2).transpose(1, 3, 0, 2).reshape(ranks, -1)
        dots_f.append(dots.astype(BF16))
        if j + 1 < local:
            slot_grad = tie(slot_grad, *held_back)
            got, (down_in,) = exchange_group(group_d[j], *held_back)
            gate_in, up_in = arrived[j + 1][0][0], arrived[j + 1][1][0]
            next_w = rows_in([gate_in]), rows_in([up_in])
            made = tie((scaled, grad_gate, grad_up), *held_back)
            grads_down.append(dot_f32("rf,rd->fd", made[0], slot_grad_out[j]).astype(BF16))
            grads_gate.append(dot_f32("rf,rd->fd", made[1], slot_in[j]).astype(BF16))
            grads_up.append(dot_f32("rf,rd->fd", made[2], slot_in[j]).astype(BF16))
            down = jnp.dot(made[0], down_w, preferred_element_type=F32).astype(BF16)
            down_slots.append(down)
            done = (grads_down[-1], grads_gate[-1], grads_up[-1], down, next_w)
            arrived[j + 1][2].append((tie(got, done), *down_in[1:]))
        slot_grads_f.append(slot_grad)

    def grad_part(grad, half=None):
        first, rows = halves(grad.shape[0], half)

        def piece_for(n):
            return lax.dynamic_slice(grad, (first, n * depth), (rows, depth))

        return piece_for, rows

    def whole_grad(placed):
        flat = [part for parts in placed for part in parts]
        counts = [len(parts) for parts in placed]
        pieces = [tuple(part[0][m] for part in flat) for m in range(ranks)]

        def body(m, ins, outs):
            first = 0
            for j, held in enumerate(counts):
                spans = [part[1:] for part in placed[j]]
                place_rows(outs[0], j, ins[first : first + held], spans, F32)
                first += held

        rows = hidden_units
        out = ((experts, rows, depth), F32, (local, rows, depth), lambda b: (b, 0, 0))
        return assemble(pieces, body, [out], "whole_grad")[0]

    def sublayer_back(own_in, inverse_all, gain, router, gates_all, logits_all, dots, inner, dhidden):
        gates = own_tokens(gates_all)
        inverse = own_tokens(inverse_all)
        dlogits = gates * (dots - jnp.sum(gates * dots, axis=-1, keepdims=True))
        dlogits = dlogits.astype(BF16)
        gain_own = own_features(gain)
        router_own = lax.dynamic_slice_in_dim(router, col_at * share, share, 0)
        normed = own_in.astype(F32) * inverse
        hidden = (normed * gain_own).astype(BF16)
        dhidden = dhidden + dot_f32("ste,fe->stf", dlogits, router_own)
        grad_router = dot_f32("ste,stf->ef", dlogits, hidden)
        grad_gain = jnp.sum(dhidden * normed, axis=(0, 1))
        dn = dhidden * gain_own
        inner = inner + jnp.sum(dlogits.astype(F32) * own_tokens(logits_all), axis=-1)
        grad = inverse * (dn - normed * (inner / width)[..., None])
        return grad, jnp.concatenate([grad_router, grad_gain[None]], axis=0)

    first_grads = (grads_down, grads_gate, grads_up)
    if local == 1:
        first_grads = ([scaled], [grad_gate], [grad_up])
        for grads, rows in zip(first_grads, (slot_grad_out[0], slot_in[0], slot_in[0])):
            grads[0] = dot_f32("rf,rd->fd", grads[0], rows).astype(BF16)
    grads_down, grads_gate, grads_up = first_grads
    got, (down_first,) = exchange_group(
        cut_group(grad_part(grads_down[0], 0)), *[part[0][-1] for part in arrived[-1][2]]
    )
    slot_grads_f[-1] = tie(slot_grads_f[-1], *got)
    group_a = cut_group(grad_part(grads_down[0], 1), grad_part(grads_gate[0], 0))
    group_b = cut_group(grad_part(grads_gate[0], 1), grad_part(grads_up[0]))
    got, (down_second, gate_first) = exchange_group(group_a, slot_grads_f[-1])
    per_row = dots_f[0].shape[1]
    dot_rows = round_up(per_row, share) // share
    under = round_up(ranks * dot_rows, 16)
    own_rows, own_dots = [], []
    for rows, dots in zip(slot_grads_f, dots_f):
        dots = jnp.pad(dots, ((0, 0), (0, dot_rows * share - per_row)))
        dots = jnp.pad(dots.reshape(-1, share), ((0, under - ranks * dot_rows), (0, 0)))
        dots = jnp.tile(dots, (1, width // share))
        own = sum_cols(jnp.concatenate([rows, dots], axis=0))
        own_rows.append(own[:slot_rows])
        own_dots.append(own[slot_rows : slot_rows + ranks * dot_rows].reshape(ranks, -1, share))
    own_rows = tie(jnp.concatenate(own_rows, axis=0), *got)
    made = tie((scaled, grad_gate, grad_up), own_rows)
    if local > 1:
        grads_down.append(dot_f32("rf,rd->fd", made[0], slot_grad_out[-1]).astype(BF16))
        grads_gate.append(dot_f32("rf,rd->fd", made[1], slot_in[-1]).astype(BF16))
        grads_up.append(dot_f32("rf,rd->fd", made[2], slot_in[-1]).astype(BF16))
    down_slots.append(jnp.dot(made[0], down_w, preferred_element_type=F32).astype(BF16))
    grad_home, dots_home = rows_home(
        own_rows, seqs, capacity, jnp.concatenate(own_dots, axis=1)
    )
    dhidden_f = come_home(home_f, grad_home)
    dots_home = dots_home.reshape(ranks, local, -1)[..., :per_row].astype(F32)
    dots_home = dots_home.reshape(experts, 2, seqs, capacity, 1).transpose(1, 2, 0, 3, 4)
    match_home = home_f.reshape(seqs, experts, capacity, seq_dev).astype(F32)
    dots_home = jnp.sum(dots_home * match_home, axis=3).swapaxes(2, 3)
    grad_mid, small_f = sublayer_back(
        mid_low, inverse_f, gain_ffn, router_ffn, gates_f, logits_f,
        dots_home[0], jnp.sum(dots_home[1], axis=-1), dhidden_f,
    )
    grad_mid = grad_out.astype(F32) + grad_mid

    mid_grad_rows = gather_rows(grad_mid.astype(BF16))
    mid_grad_rows = tie(mid_grad_rows, group_b, *grads_down, *grads_gate, *grads_up, *down_slots)
    group_c = [
        cut_group(grad_part(grads_down[j]), grad_part(grads_gate[j], 0)) for j in range(1, local)
    ]
    group_d = [
        cut_group(grad_part(grads_gate[j], 1), grad_part(grads_up[j])) for j in range(1, local)
    ]
    mid_grad_all = gather_cols(mid_grad_rows).reshape(count, width)
    got, (gate_second, up_got) = exchange_group(group_b, mid_grad_rows)
    down_slots = jnp.concatenate(down_slots, axis=0)
    mid_grad_all = tie(mid_grad_all, down_slots, group_c, group_d, *got)
    down_parts, gate_parts = [[down_first, down_second]], [[gate_first, gate_second]]
    up_parts = [[up_got]]
    down_slots = tie(down_slots, mid_grad_all)
    down_own = sum_cols(down_slots)
    grad_raw = dot_f32("rd,fd->rf", mid_grad_all, out_cat)
    early = []
    for j in range(1, local):
        got, (down_got, gate_first) = exchange_group(group_c[j - 1], mid_grad_all)
        down_parts.append([down_got])
        gate_parts.append([gate_first])
        early += got
    into, dots_a = attend_back(
        qkv, target_a, kblk, log_totals, att_plain, seq3(grad_raw), my_gates_a.swapaxes(1, 2),
        cosine, sine, rows_each, heads,
    )
    placed = jnp.zeros((seqs, ranks, experts, seq_dev), F32)
    dots_a = dots_a.reshape(seqs, ranks, seq_dev, local + 1).swapaxes(2, 3)
    placed = lax.dynamic_update_slice_in_dim(placed, dots_a[:, :, :local], row_at * local, 2)
    extra = jnp.concatenate([placed, dots_a[:, :, local:]], axis=2).astype(BF16)
    extra = extra.reshape(seqs * ranks, -1)
    held = extra.shape[1]
    under = round_up(held, 16 * share) // share
    extra = jnp.pad(extra, ((0, 0), (0, under * share - held)))
    token_part = spread(
        into.reshape(seqs * ranks, seq_dev, -1), query_w, extra.reshape(-1, under, share)
    ).reshape(seqs, -1, width)
    token_part = tie(token_part, down_own, *early)
    last = []
    for j in range(1, local):
        got, (gate_second, up_got) = exchange_group(group_d[j - 1], token_part)
        gate_parts[j].append(gate_second)
        up_parts.append([up_got])
        last += got
    att_scaled = tie(att_scaled, *last[1:2]).reshape(count, -1)
    grad_out_cat = dot_f32("rf,rd->fd", att_scaled, mid_grad_all).astype(BF16)
    down_home, _ = rows_home(tie(down_own, token_part), seqs, capacity)
    part = lax.psum_scatter(token_part, "col", scatter_dimension=2, tiled=True)
    into = tie(into, *last[1:2]).reshape(count, -1)
    grad_query_cat = dot_f32("rd,rf->df", hidden_a, into).astype(BF16)
    out_pieces = exchange_pieces(cut_pieces(grad_part(grad_out_cat)[0]), *last[1:2])
    part = tie(part, *last, down_home, grad_query_cat, *out_pieces[1:2])
    own = lax.psum_scatter(part, "row", scatter_dimension=1, tiled=True)
    def out_grad_body(m, ins, outs):
        for j in range(local):
            for h in range(heads):
                at = (h * local + j) * HEAD_DIM
                piece = ins[0][at : at + HEAD_DIM].astype(F32)
                outs[0][j, h * HEAD_DIM : (h + 1) * HEAD_DIM] = piece

    grad_out_own = assemble(
        [(p,) for p in out_pieces],
        out_grad_body,
        [((experts, head_cols, depth), F32, (local, head_cols, depth), lambda b: (b, 0, 0))],
        "out_grad",
    )[0]
    gate_all, up_all, down_all = (whole_grad(p) for p in (gate_parts, up_parts, down_parts))
    own = tie(own, gate_all, up_all, down_all)
    dhidden_a = own[:, :seq_dev].astype(F32)
    dots_a = own[:, seq_dev:].reshape(seqs, -1)[:, :held].astype(F32)
    dots_a = dots_a.reshape(seqs, experts + 1, seq_dev).swapaxes(1, 2)

    def query_part(half):
        rows = depth // 2
        return cut_pieces(
            lambda n: lax.dynamic_slice_in_dim(grad_query_cat, n * depth + half * rows, rows, 0)
        )

    query_first = exchange_pieces(query_part(0), part)
    logits_a = logits_a.reshape(seqs, seq_len, experts)
    grad_in, small_a = sublayer_back(
        block_in, seq3(inverse_a), gain_attn, router_attn, gates_a, logits_a,
        dots_a[..., :experts], dots_a[..., experts], dhidden_a,
    )
    grad_in = grad_mid + grad_in
    block_out = (mid + come_home(home_f, down_home)).astype(BF16)

    smalls = jnp.concatenate([small_a, small_f], axis=0)
    high = smalls.astype(BF16)
    smalls = jnp.stack([high, (smalls - high.astype(F32)).astype(BF16)]).reshape(-1)
    held = smalls.shape[0]
    under = round_up(held, 16 * made_cols) // made_cols
    smalls = jnp.pad(smalls, (0, under * made_cols - held)).reshape(under, made_cols)
    query_second = exchange_pieces(
        [jnp.concatenate([piece, smalls], axis=0) for piece in query_part(1)]
    )
    smalls = sum(piece[depth // 2 :].astype(F32) for piece in query_second)
    smalls = jnp.sum(smalls.reshape(-1)[:held].reshape(2, -1, share), axis=0)
    smalls = lax.all_gather(smalls, "col", axis=1, tiled=True)
    def query_grad_body(m, ins, outs):
        for h in range(heads):
            columns = slice(h * HEAD_DIM, (h + 1) * HEAD_DIM)
            for p in range(parts):
                at = (h * parts + p) * HEAD_DIM
                for half in range(2):
                    rows = slice(half * (depth // 2), (half + 1) * (depth // 2))
                    piece = ins[half][: depth // 2, at : at + HEAD_DIM].astype(F32)
                    if p < local:
                        outs[0][p, rows, columns] = piece
                    elif m == 0:
                        outs[1 + p - local][rows, columns] = piece
                    else:
                        total = outs[1 + p - local][rows, columns] + piece
                        outs[1 + p - local][rows, columns] = total

    shared = ((depth, head_cols), F32, (depth, head_cols), lambda b: (0, 0))
    grad_query_own, grad_key_own, grad_value_own = assemble(
        list(zip(query_first, query_second)),
        query_grad_body,
        [
            ((experts, depth, head_cols), F32, (local, depth, head_cols), lambda b: (b, 0, 0)),
            shared,
            shared,
        ],
        "query_grad",
    )
    return (
        block_out,
        grad_in,
        smalls[experts],
        smalls[2 * experts + 1],
        smalls[:experts].T,
        smalls[experts + 1 : 2 * experts + 1].T,
        grad_query_own,
        grad_key_own,
        grad_value_own,
        grad_out_own,
        gate_all.swapaxes(1, 2),
        up_all.swapaxes(1, 2),
        down_all,
    )


def solution(mesh):
    in_specs = (
        P(None, "row", "col"),
        P(None, "row", "col"),
        P(),
        P(),
        P(),
        P(),
        P(None, "row", "col"),
        P("row", "col"),
        P("row", "col"),
        P(None, "col", "row"),
        P(None, "row", "col"),
        P(None, "row", "col"),
        P(None, "col", "row"),
        P(None, "row", None),
        P(None, "row", None),
        P(None, "row", None),
        P(None, "row", None),
        P(),
    )
    out_specs = (
        P(None, "row", "col"),
        P(None, "row", "col"),
        P(),
        P(),
        P(),
        P(),
        P(None, "row", "col"),
        P("row", "col"),
        P("row", "col"),
        P(None, "col", "row"),
        P(None, "row", "col"),
        P(None, "row", "col"),
        P(None, "col", "row"),
    )
    return jax.shard_map(
        per_device, mesh=mesh, in_specs=in_specs, out_specs=out_specs, check_vma=False
    )
```

```python
from functools import partial
import math

import jax
import jax.numpy as jnp
from jax import lax
from jax.experimental import pallas as pl
from jax.experimental.pallas import tpu as pltpu
from jax.sharding import PartitionSpec as P

HEAD_DIM = 128
EPSILON = 1e-05
ROPE_BASE = 10000.0
MASKED_SCORE = -1e30
BF16 = jnp.bfloat16
F32 = jnp.float32


def dot_f32(spec, left, right):
    return jnp.einsum(spec, left, right, preferred_element_type=F32)


def tie(value, *others):
    return lax.optimization_barrier((value, others))[0]


def rope_tables(length):
    half_width = HEAD_DIM // 2
    frequency = jnp.exp(
        -math.log(ROPE_BASE) * jnp.arange(half_width, dtype=F32) * (2.0 / HEAD_DIM)
    )
    angles = jnp.arange(length, dtype=jnp.int32).astype(F32)[:, None] * frequency
    cosine, sine = jnp.cos(angles), jnp.sin(angles)
    return (
        jnp.concatenate([cosine, cosine], axis=-1),
        jnp.concatenate([-sine, sine], axis=-1),
    )


def expert_ranks(pairs, order, expert):
    names, places = (jnp.concatenate([a[0], a[1]], axis=-1) for a in (pairs, order))
    ahead = jnp.logical_and(
        places[..., None, :] < places[..., :, None], names[..., None, :] == expert
    )
    rank = jnp.sum(ahead.astype(F32), axis=-1).astype(jnp.int32)
    chosen = jnp.where(names == expert, rank, -1)
    half = chosen.shape[-1] // 2
    return jnp.maximum(chosen[..., :half], chosen[..., half:])


def all_ranks(pairs, order):
    names, places = (jnp.concatenate([a[0], a[1]], axis=-1) for a in (pairs, order))
    ahead = jnp.logical_and(
        places[..., None, :] < places[..., :, None], names[..., None, :] == names[..., :, None]
    )
    rank = jnp.sum(ahead.astype(F32), axis=-1).astype(jnp.int32)
    half = rank.shape[-1] // 2
    return jnp.stack([rank[..., :half], rank[..., half:]])


def slot_match(pairs, ranks, expert, capacity):
    rank_here = jnp.max(jnp.where(pairs == expert, ranks, -1), axis=0)
    slots = jnp.arange(capacity, dtype=jnp.int32)[:, None]
    return rank_here[..., None, :] == slots


def gate_table(logits, routes):
    ids = jnp.arange(logits.shape[-1], dtype=jnp.int32)
    chosen = jnp.any(routes[..., None] == ids, axis=0)
    masked = jnp.where(chosen, logits, MASKED_SCORE)
    top = jnp.max(masked, axis=-1, keepdims=True)
    exps = jnp.where(chosen, jnp.exp(masked - top), 0.0)
    return exps / jnp.sum(exps, axis=-1, keepdims=True)


def normalize_rows(wide):
    inverse = lax.rsqrt(jnp.mean(wide * wide, axis=-1, keepdims=True) + EPSILON)
    return (wide * inverse, inverse)


def roll_half(values):
    return pltpu.roll(values, HEAD_DIM // 2, 1)


def project_kernel(
    rotated, x_ref, chosen_ref, gain_ref, router_ref, weight_ref, cos_ref, sin_ref,
    hidden_ref, inverse_ref, logits_ref, gates_ref, out_ref,
):
    normed, inverse = normalize_rows(x_ref[...].astype(F32))
    hidden = (normed * gain_ref[...]).astype(BF16)
    hidden_ref[...] = hidden
    inverse_ref[...] = inverse
    logits = jnp.dot(hidden, router_ref[...], preferred_element_type=F32)
    logits_ref[...] = logits
    chosen = chosen_ref[...] > 0.0
    top = jnp.max(jnp.where(chosen, logits, MASKED_SCORE), axis=-1, keepdims=True)
    exps = jnp.where(chosen, jnp.exp(jnp.where(chosen, logits - top, 0.0)), 0.0)
    gates_ref[...] = exps / jnp.sum(exps, axis=-1, keepdims=True)
    made = jnp.dot(hidden, weight_ref[...], preferred_element_type=F32)
    cosine, sine = cos_ref[...], sin_ref[...]
    for at, turn in enumerate(rotated):
        columns = slice(at * HEAD_DIM, (at + 1) * HEAD_DIM)
        one = made[:, columns]
        if turn:
            one = one * cosine + roll_half(one) * sine
        out_ref[:, columns] = one.astype(BF16)


def project(x, chosen, gain, router, weight, cosine, sine, rotated):
    count, width = x.shape
    experts, cols = router.shape[1], weight.shape[1]
    length = cosine.shape[0]
    tile = 512
    row = lambda n: pl.BlockSpec((tile, n), lambda i: (i, 0))
    whole = lambda a: pl.BlockSpec(a.shape, lambda i: (0, 0))
    table = pl.BlockSpec((tile, HEAD_DIM), lambda i: (lax.rem(i, length // tile), 0))
    return pl.pallas_call(
        partial(project_kernel, rotated),
        grid=(count // tile,),
        in_specs=[row(width), row(experts), pl.BlockSpec((1, width), lambda i: (0, 0)),
                  whole(router), whole(weight), table, table],
        out_specs=[row(width), row(1), row(experts), row(experts), row(cols)],
        out_shape=[
            jax.ShapeDtypeStruct((count, width), BF16),
            jax.ShapeDtypeStruct((count, 1), F32),
            jax.ShapeDtypeStruct((count, experts), F32),
            jax.ShapeDtypeStruct((count, experts), F32),
            jax.ShapeDtypeStruct((count, cols), BF16),
        ],
        compiler_params=pltpu.CompilerParams(vmem_limit_bytes=48 * 1024 * 1024),
        cost_estimate=pl.CostEstimate(
            flops=2 * count * width * cols,
            bytes_accessed=4 * count * width + 2 * count * cols,
            transcendentals=count,
        ),
        name="project",
    )(x, chosen, gain.reshape(1, width), router, weight, cosine, sine)


def scores_of(q, k, qblk, kblk):
    raw = lax.dot_general(q, k, (((1,), (1,)), ((), ())), preferred_element_type=F32)
    return jnp.where(kblk <= qblk, raw * HEAD_DIM ** (-0.5), MASKED_SCORE)


def head_part(ref, at):
    return ref[0, :, at * HEAD_DIM : (at + 1) * HEAD_DIM]


def pick_rows(match, tokens):
    return jnp.dot(match, tokens, preferred_element_type=F32).astype(BF16)


def put_rows(match, rows):
    first = (((0,), (0,)), ((), ()))
    return lax.dot_general(match, rows, first, preferred_element_type=F32)


def slot_rows_of(target_ref, kblk, rows):
    local, length = target_ref.shape[1:]
    at = lax.broadcasted_iota(jnp.int32, (rows, length), 0)
    found = [target_ref[0, j : j + 1] == at for j in range(local)]
    blocks = [
        jnp.sum(jnp.where(m, kblk.astype(F32), 0.0), axis=-1, keepdims=True) for m in found
    ]
    return found, [jnp.where(m, 1.0, 0.0).astype(BF16) for m in found], blocks


def attend_kernel(
    rows, qkv_ref, target_ref, gate_ref, kblk_ref, slot_ref, plain_ref, scaled_ref, lse_ref
):
    local = target_ref.shape[1]
    kblk = kblk_ref[0]
    found, match, blocks = slot_rows_of(target_ref, kblk, rows)
    q = jnp.concatenate([pick_rows(match[j], head_part(qkv_ref, j)) for j in range(local)], axis=0)
    k, v = head_part(qkv_ref, local), head_part(qkv_ref, local + 1)
    scores = scores_of(q, k, jnp.concatenate(blocks, axis=0), kblk.astype(F32))
    top = jnp.max(scores, axis=-1, keepdims=True)
    exps = jnp.exp(scores - top)
    total = jnp.sum(exps, axis=-1, keepdims=True)
    probs = (exps * (1.0 / total)).astype(BF16)
    out = jnp.dot(probs, v, preferred_element_type=F32).astype(BF16)
    lse_ref[0, 0] = top + jnp.log(total)
    for j in range(local):
        here = out[j * rows : (j + 1) * rows]
        gate = jnp.sum(jnp.where(found[j], gate_ref[0, j : j + 1], 0.0), axis=-1, keepdims=True)
        scaled = (here.astype(F32) * gate).astype(BF16)
        columns = slice(j * HEAD_DIM, (j + 1) * HEAD_DIM)
        slot_ref[j, 0] = scaled
        plain_ref[0, :, columns] = put_rows(match[j], here).astype(BF16)
        scaled_ref[0, :, columns] = put_rows(match[j], scaled).astype(BF16)


def attend(qkv, target, gates, kblk, rows, heads):
    seqs, length, cols = qkv.shape
    local = target.shape[1]
    token = lambda n: pl.BlockSpec((1, length, n * HEAD_DIM), lambda s, h: (s, 0, h))
    lane = lambda n: pl.BlockSpec((1, n, length), lambda s, h: (s, 0, 0))
    of_tokens = jax.ShapeDtypeStruct((seqs, length, heads * local * HEAD_DIM), BF16)
    total = local * rows
    return pl.pallas_call(
        partial(attend_kernel, rows),
        grid=(seqs, heads),
        in_specs=[token(local + 2), lane(local), lane(local), lane(1)],
        out_specs=[
            pl.BlockSpec((local, 1, rows, HEAD_DIM), lambda s, h: (0, s, 0, h)),
            token(local),
            token(local),
            pl.BlockSpec((1, 1, total, 1), lambda s, h: (s, h, 0, 0)),
        ],
        out_shape=[
            jax.ShapeDtypeStruct((local, seqs, rows, heads * HEAD_DIM), BF16),
            of_tokens,
            of_tokens,
            jax.ShapeDtypeStruct((seqs, heads, total, 1), F32),
        ],
        compiler_params=pltpu.CompilerParams(vmem_limit_bytes=56 * 1024 * 1024),
        cost_estimate=pl.CostEstimate(
            flops=12 * seqs * heads * total * length * HEAD_DIM,
            bytes_accessed=4 * qkv.size,
            transcendentals=seqs * heads * total * length,
        ),
        name="attend",
    )(qkv, target, gates, kblk)


def attend_back_kernel(
    rows, qkv_ref, target_ref, kblk_ref, lse_ref, plain_ref, raw_ref, gate_ref, cos_ref, sin_ref,
    out_ref, dots_ref,
):
    local = target_ref.shape[1]
    kblk = kblk_ref[0]
    _, match, blocks = slot_rows_of(target_ref, kblk, rows)
    q = jnp.concatenate([pick_rows(match[j], head_part(qkv_ref, j)) for j in range(local)], axis=0)
    k, v = head_part(qkv_ref, local), head_part(qkv_ref, local + 1)
    grads, dots = [], []
    for j in range(local):
        raw = head_part(raw_ref, j)
        gated = (raw * gate_ref[0, :, j : j + 1]).astype(BF16)
        grads.append(pick_rows(match[j], gated))
        dots.append(jnp.sum(raw * head_part(plain_ref, j).astype(F32), axis=-1, keepdims=True))
    g = jnp.concatenate(grads, axis=0)
    scores = scores_of(q, k, jnp.concatenate(blocks, axis=0), kblk.astype(F32))
    probs = jnp.exp(scores - lse_ref[0, 0])
    grad = lax.dot_general(g, v, (((1,), (1,)), ((), ())), preferred_element_type=F32)
    inner = jnp.sum(probs * grad, axis=-1, keepdims=True)
    grad_scores = (probs * (grad - inner) * HEAD_DIM ** (-0.5)).astype(BF16)
    dq = jnp.dot(grad_scores, k, preferred_element_type=F32)
    cosine, sine = cos_ref[...], sin_ref[...]
    inner_sum = 0.0
    turn = lambda value: (value * cosine - roll_half(value) * sine).astype(BF16)
    for j in range(local):
        here = dq[j * rows : (j + 1) * rows]
        high = here.astype(BF16)
        low = (here - high.astype(F32)).astype(BF16)
        placed = put_rows(match[j], high) + put_rows(match[j], low)
        out_ref[0, :, j * HEAD_DIM : (j + 1) * HEAD_DIM] = turn(placed)
        inner_sum = inner_sum + placed * head_part(qkv_ref, j).astype(F32)
    dk = put_rows(grad_scores, q)
    out_ref[0, :, local * HEAD_DIM : (local + 1) * HEAD_DIM] = turn(dk)
    dv = put_rows(probs.astype(BF16), g)
    out_ref[0, :, (local + 1) * HEAD_DIM : (local + 2) * HEAD_DIM] = dv.astype(BF16)
    inner_sum = inner_sum + dk * k.astype(F32) + dv * v.astype(F32)
    dots.append(jnp.sum(inner_sum, axis=-1, keepdims=True))
    for at in range(local + 1):

        @pl.when(pl.program_id(1) == 0)
        def _():
            dots_ref[0, :, at : at + 1] = dots[at]

        @pl.when(pl.program_id(1) > 0)
        def _():
            dots_ref[0, :, at : at + 1] = dots_ref[0, :, at : at + 1] + dots[at]


def attend_back(qkv, target, kblk, lse, plain, raw, gate_cols, cosine, sine, rows, heads):
    seqs, length, cols = qkv.shape
    local = target.shape[1]
    token = lambda n: pl.BlockSpec((1, length, n * HEAD_DIM), lambda s, h: (s, 0, h))
    lane = lambda n: pl.BlockSpec((1, n, length), lambda s, h: (s, 0, 0))
    total = local * rows
    column = pl.BlockSpec((1, length, local), lambda s, h: (s, 0, 0))
    table = pl.BlockSpec((length, HEAD_DIM), lambda s, h: (0, 0))
    return pl.pallas_call(
        partial(attend_back_kernel, rows),
        grid=(seqs, heads),
        in_specs=[
            token(local + 2),
            lane(local),
            lane(1),
            pl.BlockSpec((1, 1, total, 1), lambda s, h: (s, h, 0, 0)),
            token(local),
            token(local),
            column,
            table,
            table,
        ],
        out_specs=[
            token(local + 2),
            pl.BlockSpec((1, length, local + 1), lambda s, h: (s, 0, 0)),
        ],
        out_shape=[
            jax.ShapeDtypeStruct(qkv.shape, BF16),
            jax.ShapeDtypeStruct((seqs, length, local + 1), F32),
        ],
        compiler_params=pltpu.CompilerParams(vmem_limit_bytes=60 * 1024 * 1024),
        cost_estimate=pl.CostEstimate(
            flops=0,
            bytes_accessed=4 * qkv.size,
            transcendentals=0,
        ),
        name="attend_back",
    )(qkv, target, kblk, lse, plain, raw, gate_cols, cosine, sine)


def dispatch_body(target_ref, tokens, out_refs):
    rows = out_refs[0].shape[1]
    at = lax.broadcasted_iota(jnp.int32, (rows, tokens.shape[0]), 0)
    for j, out_ref in enumerate(out_refs):
        match = jnp.where(target_ref[0, j : j + 1] == at, 1.0, 0.0).astype(BF16)
        out_ref[0] = pick_rows(match, tokens[...])


def dispatch_kernel(x_ref, target_ref, *out_refs):
    dispatch_body(target_ref, x_ref.at[0], out_refs)


def norm_dispatch_kernel(step, x_ref, target_ref, gain_ref, router_ref, *refs):
    *out_refs, inverse_ref, logits_ref, hidden_ref = refs
    for first in range(0, x_ref.shape[1], step):
        rows = slice(first, first + step)
        normed, inverse = normalize_rows(x_ref[0, rows].astype(F32))
        hidden = (normed * gain_ref[...]).astype(BF16)
        hidden_ref[rows] = hidden
        inverse_ref[0, rows] = inverse
        logits_ref[0, rows] = jnp.dot(hidden, router_ref[...], preferred_element_type=F32)
    dispatch_body(target_ref, hidden_ref, out_refs)


def dispatch(x, target, rows, norm=None):
    seqs, length, width = x.shape
    local = target.shape[1]
    token = lambda n: pl.BlockSpec((1, length, n), lambda s: (s, 0, 0))
    in_specs = [token(width), pl.BlockSpec((1, local, length), lambda s: (s, 0, 0))]
    out_specs = [pl.BlockSpec((1, rows, width), lambda s: (s, 0, 0)) for _ in range(local)]
    out_shape = [jax.ShapeDtypeStruct((seqs, rows, width), BF16) for _ in range(local)]
    args, kernel, scratch = [x, target], dispatch_kernel, []
    if norm is not None:
        gain, router = norm
        experts = router.shape[1]
        in_specs += [
            pl.BlockSpec((1, width), lambda s: (0, 0)),
            pl.BlockSpec(router.shape, lambda s: (0, 0)),
        ]
        out_specs += [token(1), token(experts)]
        out_shape += [
            jax.ShapeDtypeStruct((seqs, length, 1), F32),
            jax.ShapeDtypeStruct((seqs, length, experts), F32),
        ]
        args += [gain.reshape(1, width), router]
        kernel = partial(norm_dispatch_kernel, 256)
        scratch = [pltpu.VMEM((length, width), BF16)]
    return pl.pallas_call(
        kernel,
        grid=(seqs,),
        in_specs=in_specs,
        out_specs=out_specs,
        out_shape=out_shape,
        scratch_shapes=scratch,
        compiler_params=pltpu.CompilerParams(vmem_limit_bytes=56 * 1024 * 1024),
        cost_estimate=pl.CostEstimate(
            flops=0,
            bytes_accessed=2 * x.size,
            transcendentals=0,
        ),
        name="dispatch",
    )(*args)


def expert_kernel(
    x_ref, grad_ref, weight_ref, gate_ref, up_ref, down_ref,
    scaled_ref, grad_gate_ref, grad_up_ref, back_ref, dots_ref,
):
    last = (((1,), (1,)), ((), ()))
    x, weight = x_ref[...], weight_ref[...]
    gate_pre = lax.dot_general(x, gate_ref[...], last, preferred_element_type=F32)
    up_pre = lax.dot_general(x, up_ref[...], last, preferred_element_type=F32)
    raw = lax.dot_general(grad_ref[...], down_ref[...], last, preferred_element_type=F32)
    gate_sig = jax.nn.sigmoid(gate_pre)
    gate_silu = gate_pre * gate_sig
    activated = gate_silu * up_pre
    scaled_ref[...] = (activated * weight).astype(BF16)
    grad_act = raw * weight
    grad_gate = grad_act * up_pre * (gate_sig * (1.0 + gate_pre * (1.0 - gate_sig)))
    grad_gate = grad_gate.astype(BF16)
    grad_up = (grad_act * gate_silu).astype(BF16)
    grad_gate_ref[...] = grad_gate
    grad_up_ref[...] = grad_up
    back = jnp.dot(grad_gate, gate_ref[...], preferred_element_type=F32)
    back = back + jnp.dot(grad_up, up_ref[...], preferred_element_type=F32)
    back_ref[...] = back.astype(BF16)
    inner = grad_gate.astype(F32) * gate_pre + grad_up.astype(F32) * up_pre
    dots_ref[:, 0:1] = jnp.sum(raw * activated, axis=-1, keepdims=True)
    dots_ref[:, 1:2] = jnp.sum(inner, axis=-1, keepdims=True)


def expert_step(x, grad, weight, gate_w, up_w, down_w, tile):
    count, width = x.shape
    units = gate_w.shape[0]
    row = lambda n: pl.BlockSpec((tile, n), lambda i: (i, 0))
    whole = pl.BlockSpec((units, width), lambda i: (0, 0))
    shape = lambda n, dtype=BF16: jax.ShapeDtypeStruct((count, n), dtype)
    return pl.pallas_call(
        expert_kernel,
        grid=(count // tile,),
        in_specs=[row(width), row(width), row(1), whole, whole, whole],
        out_specs=[row(units), row(units), row(units), row(width), row(2)],
        out_shape=[shape(units), shape(units), shape(units), shape(width), shape(2, F32)],
        compiler_params=pltpu.CompilerParams(vmem_limit_bytes=56 * 1024 * 1024),
        cost_estimate=pl.CostEstimate(
            flops=0,
            bytes_accessed=6 * width * units,
            transcendentals=0,
        ),
        name="expert_step",
    )(x, grad, weight, gate_w, up_w, down_w)


def gather_rows(own):
    return lax.all_gather(own, "row", axis=1, tiled=True)


def gather_cols(rows):
    return lax.all_gather(rows, "col", axis=2, tiled=True)


def exchange(parts):
    return lax.all_to_all(parts, "row", 0, 0)


def cut_pieces(piece_for):
    ranks, row = lax.axis_size("row"), lax.axis_index("row")
    return [piece_for(lax.rem(row + m, ranks)) for m in range(ranks)]


def exchange_pieces(pieces, *after):
    ranks = lax.axis_size("row")
    got = pieces[:1]
    for m in range(1, ranks):
        steps = [(i, (i + m) % ranks) for i in range(ranks)]
        got.append(lax.ppermute(tie(pieces[m], *after), "row", steps))
    return got


def cut_group(*parts):
    pieces = cut_pieces(lambda n: jnp.concatenate([piece_for(n) for piece_for, _ in parts], axis=0))
    return pieces, [rows for _, rows in parts]


def exchange_group(group, *after):
    pieces, counts = group
    got = exchange_pieces(pieces, *after)
    placed, first = [], 0
    for rows in counts:
        placed.append((got, first, rows))
        first += rows
    return got, placed


def assemble(pieces, body, outs, name):
    ranks, each = len(pieces), len(pieces[0])

    def kernel(row_ref, *refs):
        for m in range(ranks):

            @pl.when(pl.program_id(0) == m)
            def _():
                body(m, refs[m * each : (m + 1) * each], refs[ranks * each :])

    def at(index):
        return lambda m, row: index(lax.rem(row[0] - m + ranks, ranks))

    flat = [a for piece in pieces for a in piece]
    whole = lambda a: pl.BlockSpec(a.shape, lambda m, row: (0,) * a.ndim)
    return pl.pallas_call(
        kernel,
        grid_spec=pltpu.PrefetchScalarGridSpec(
            num_scalar_prefetch=1,
            grid=(ranks,),
            in_specs=[whole(a) for a in flat],
            out_specs=[pl.BlockSpec(block, at(index)) for _, _, block, index in outs],
        ),
        out_shape=[jax.ShapeDtypeStruct(shape, dtype) for shape, dtype, _, _ in outs],
        compiler_params=pltpu.CompilerParams(vmem_limit_bytes=48 * 1024 * 1024),
        cost_estimate=pl.CostEstimate(
            flops=0, bytes_accessed=4 * sum(a.size for a in flat), transcendentals=0
        ),
        name=name,
    )(lax.axis_index("row").astype(jnp.int32).reshape(1), *flat)


def place_rows(outs, at, refs, spans, dtype):
    to = 0
    for ref, (first, rows) in zip(refs, spans):
        piece = ref[first : first + rows].astype(dtype)
        if at is None:
            outs[to : to + rows] = piece
        else:
            outs[at, to : to + rows] = piece
        to += rows


def spread_kernel(into_ref, weight_ref, extra_ref, out_ref):
    last = (((1,), (1,)), ((), ()))
    tokens, copies = into_ref.shape[1], out_ref.shape[2] // extra_ref.shape[2]
    rows = lax.dot_general(into_ref[0], weight_ref[...], last, preferred_element_type=F32)
    out_ref[0, :tokens] = rows.astype(BF16)
    share = extra_ref.shape[2]
    for at in range(copies):
        out_ref[0, tokens:, at * share : (at + 1) * share] = extra_ref[0]


def spread(into, weight, extra):
    blocks, tokens, depth = into.shape
    width = weight.shape[0]
    rows = tokens + extra.shape[1]
    block = lambda a: pl.BlockSpec((1, *a.shape[1:]), lambda i: (i, 0, 0))
    return pl.pallas_call(
        spread_kernel,
        grid=(blocks,),
        in_specs=[block(into), pl.BlockSpec(weight.shape, lambda i: (0, 0)), block(extra)],
        out_specs=pl.BlockSpec((1, rows, width), lambda i: (i, 0, 0)),
        out_shape=jax.ShapeDtypeStruct((blocks, rows, width), BF16),
        compiler_params=pltpu.CompilerParams(vmem_limit_bytes=48 * 1024 * 1024),
        cost_estimate=pl.CostEstimate(
            flops=0,
            bytes_accessed=2 * blocks * rows * width,
            transcendentals=0,
        ),
        name="spread",
    )(into, weight, extra)


def sum_cols(rows):
    return lax.psum_scatter(rows, "col", scatter_dimension=1, tiled=True)


def round_up(count, unit):
    return -(-count // unit) * unit


def rows_home(own, seqs, capacity, extra=None):
    ranks, share = lax.axis_size("row"), own.shape[-1]
    rows = own.reshape(-1, seqs, ranks, capacity, share).transpose(2, 1, 0, 3, 4)
    rows = rows.reshape(ranks, -1, share)
    count = rows.shape[1]
    if extra is not None:
        rows = jnp.concatenate([rows, extra], axis=1)
    got = exchange(rows)
    home = got[:, :count].reshape(ranks, seqs, -1, share).swapaxes(0, 1)
    return home.reshape(seqs, -1, share), got[:, count:]


def per_device(
    block_in,
    grad_out,
    gain_attn,
    gain_ffn,
    router_attn,
    router_ffn,
    w_query,
    key_weight,
    value_weight,
    w_out,
    w_gate,
    w_up,
    w_down,
    routes_attn,
    routes_ffn,
    order_attn,
    order_ffn,
    block_ids,
):
    seqs, seq_dev, share = block_in.shape
    experts, depth, head_cols = w_query.shape
    capacity = 18 * seq_dev // (8 * experts)
    heads = head_cols // HEAD_DIM
    hidden_units = w_gate.shape[2]
    width = gain_attn.shape[0]
    seq_len = block_ids.shape[1]
    ranks = lax.axis_size("row")
    local = experts // ranks
    row_at, col_at = lax.axis_index("row"), lax.axis_index("col")
    slot_rows = seqs * ranks * capacity
    count = seqs * seq_len

    def own_features(whole):
        return lax.dynamic_slice_in_dim(whole, col_at * share, share, whole.ndim - 1)

    def own_tokens(whole):
        return lax.dynamic_slice_in_dim(whole, row_at * seq_dev, seq_dev, 1)

    def by_pair(table):
        return table.reshape(seqs, seq_dev, 2).transpose(2, 0, 1)

    small = jnp.stack([by_pair(t) for t in (routes_attn, order_attn, routes_ffn, order_ffn)])
    split = jnp.concatenate([small % 256, small[1::2] // 256]).astype(BF16)
    split = split.transpose(2, 0, 1, 3).reshape(seqs, -1)
    held = split.shape[1]
    table_rows = round_up(held, 16 * share) // share
    split = jnp.pad(split, ((0, 0), (0, table_rows * share - held)))
    in_rows = gather_rows(
        jnp.concatenate([block_in, split.reshape(seqs, table_rows, share)], axis=1)
    ).reshape(seqs, ranks, -1, share)
    split = in_rows[:, :, seq_dev:].reshape(seqs, ranks, -1)[..., :held].astype(jnp.int32)
    split = split.reshape(seqs, ranks, 6, 2, seq_dev).transpose(2, 3, 0, 1, 4)
    small_all = [split[0], split[1] + 256 * split[4], split[2], split[3] + 256 * split[5]]
    in_rows = in_rows[:, :, :seq_dev].reshape(seqs, seq_len, share)

    def halves(height, half):
        return (0, height) if half is None else (half * (height // 2), height // 2)

    def expert_part(weight, j, half=None):
        first, rows = halves(weight.shape[1], half)

        def piece_for(n):
            at = (n * local + j, first, 0)
            return lax.dynamic_slice(weight, at, (1, rows, weight.shape[2]))[0]

        return piece_for, rows

    def rows_in(placed):
        spans = [part[1:] for part in placed]
        pieces = [tuple(part[0][m] for part in placed) for m in range(ranks)]

        def body(m, ins, outs):
            place_rows(outs[0], None, ins, spans, BF16)

        out = ((hidden_units, width), BF16, (hidden_units, depth), lambda b: (0, b))
        return assemble(pieces, body, [out], "rows_in")[0]

    w_gate, w_up = w_gate.swapaxes(1, 2), w_up.swapaxes(1, 2)

    def group_in(weight):
        grouped = weight.reshape(ranks, local, *weight.shape[1:])
        return lambda n: lax.dynamic_index_in_dim(grouped, n, 0, keepdims=False)

    parts = local + 2
    key_value = jnp.stack([key_weight, value_weight])

    query_for = group_in(w_query)
    cosine, sine = rope_tables(seq_len)
    query_parts = cut_pieces(lambda n: jnp.concatenate([query_for(n), key_value]))
    out_parts = cut_pieces(group_in(w_out))
    group_a = cut_group(expert_part(w_gate, 0), expert_part(w_up, 0, 0))
    group_b = cut_group(expert_part(w_up, 0, 1), expert_part(w_down, 0))
    group_c = [cut_group(expert_part(w_gate, j), expert_part(w_up, j)) for j in range(1, local)]
    group_d = [cut_group(expert_part(w_down, j)) for j in range(1, local)]
    in_rows = tie(
        in_rows, cosine, sine, query_parts, out_parts, group_a, group_b, group_c, group_d
    )
    query_got = exchange_pieces(query_parts, in_rows)

    def query_body(m, ins, outs):
        for h in range(heads):
            for p in range(parts):
                at = (h * parts + p) * HEAD_DIM
                piece = ins[0][p, :, h * HEAD_DIM : (h + 1) * HEAD_DIM]
                outs[0][:, at : at + HEAD_DIM] = piece

    made_cols = heads * parts * HEAD_DIM
    query_w = assemble(
        [(p,) for p in query_got],
        query_body,
        [((width, made_cols), BF16, (depth, made_cols), lambda b: (b, 0))],
        "query_in",
    )[0]

    mine = [row_at * local + j for j in range(local)]

    def tokens_to_slots(pairs, order):
        first = jnp.arange(ranks, dtype=jnp.int32)[:, None] * capacity
        out = []
        for e in mine:
            rank = expert_ranks(pairs, order, e)
            kept = jnp.logical_and(rank >= 0, rank < capacity)
            out.append(jnp.where(kept, first + rank, -1).reshape(seqs, seq_len))
        return jnp.stack(out, axis=1)

    target_a = tokens_to_slots(small_all[0], small_all[1])
    target_f = tokens_to_slots(small_all[2], small_all[3])
    routes_a = small_all[0].reshape(2, seqs, seq_len)
    routes_f = small_all[2].reshape(2, seqs, seq_len)

    def home_match(pairs, order):
        ranks_here = all_ranks(pairs, order)
        every = [slot_match(pairs, ranks_here, e, capacity) for e in range(experts)]
        return jnp.concatenate(every, axis=1).astype(BF16)

    home_a = home_match(small[0], small[1])
    home_f = home_match(small[2], small[3])

    def come_home(match, rows):
        return dot_f32("sct,scf->stf", match, rows)

    def my_gates(gates):
        return jnp.stack(
            [lax.dynamic_index_in_dim(gates, e, 2, keepdims=False) for e in mine], axis=1
        )

    in_all = gather_cols(in_rows).reshape(count, width)
    grad_sent = jnp.einsum("sct,stf->scf", home_f, grad_out)
    grad_sent = grad_sent.reshape(seqs, ranks, local, capacity, share).transpose(1, 2, 0, 3, 4)
    chosen_a = jnp.any(routes_a[..., None] == jnp.arange(experts, dtype=jnp.int32), axis=0)
    chosen_a = chosen_a.astype(F32).reshape(count, experts)
    in_all = tie(in_all, target_a, target_f, home_a, home_f, grad_sent, chosen_a)
    rotated = ([True] * (local + 1) + [False]) * heads
    hidden_a, inverse_a, logits_a, gates_a, qkv = project(
        in_all, chosen_a, gain_attn, router_attn, query_w, cosine, sine, rotated
    )
    qkv = qkv.reshape(seqs, seq_len, -1)
    out_got = exchange_pieces(out_parts, in_all)
    qkv = tie(qkv, *out_got)
    grad_rows = exchange(tie(grad_sent, qkv))
    gates_a = gates_a.reshape(seqs, seq_len, experts)
    my_gates_a = my_gates(gates_a)
    kblk = block_ids.reshape(seqs, 1, seq_len)
    rows_each = ranks * capacity
    att_slot, att_plain, att_scaled, log_totals = attend(
        qkv, target_a, my_gates_a, kblk, rows_each, heads
    )
    def out_body(m, ins, outs):
        for j in range(local):
            outs[1][j] = ins[0][j]
            for h in range(heads):
                at = (h * local + j) * HEAD_DIM
                outs[0][at : at + HEAD_DIM] = ins[0][j, h * HEAD_DIM : (h + 1) * HEAD_DIM]

    rows_cat = heads * local * HEAD_DIM
    out_cat, out_w = assemble(
        [(p,) for p in tie(out_got, att_slot)],
        out_body,
        [
            ((rows_cat, width), BF16, (rows_cat, depth), lambda b: (0, b)),
            ((local, head_cols, width), BF16, (local, head_cols, depth), lambda b: (0, 0, b)),
        ],
        "out_in",
    )

    out_slots = dot_f32(
        "jrf,jfd->jrd", att_slot.reshape(local, slot_rows, head_cols), out_w
    ).astype(BF16)
    out_slots = tie(out_slots.reshape(-1, width), grad_rows)
    got, (gate_in, up_first) = exchange_group(group_a, *out_got)
    out_own = tie(sum_cols(out_slots), *got)
    out_home, _ = rows_home(out_own, seqs, capacity)
    mid = block_in.astype(F32) + come_home(home_a, out_home)

    mid_low = mid.astype(BF16)
    mid_rows = gather_rows(mid_low)
    mid_all = gather_cols(mid_rows).reshape(count, width)
    got, (up_second, down_in) = exchange_group(group_b, mid_rows)
    mid_all = tie(mid_all, *got)
    arrived = [([gate_in], [up_first, up_second], [down_in])]
    grad_rows = tie(grad_rows, mid_all).transpose(1, 2, 0, 3, 4)
    grad_rows = grad_rows.reshape(local, slot_rows, share)
    slot_grad_out = [
        lax.all_gather(grad_rows[j], "col", axis=1, tiled=True) for j in range(local)
    ]
    held_back = []
    for j in range(1, local):
        got, (gate_in, up_in) = exchange_group(group_c[j - 1], mid_all)
        held_back += got
        arrived.append(([gate_in], [up_in], []))
    seq3 = lambda a: a.reshape(seqs, seq_len, -1)
    *slot_in, inverse_f, logits_f = dispatch(
        seq3(mid_all), target_f, rows_each, (gain_ffn, router_ffn)
    )
    slot_in = [x.reshape(slot_rows, width) for x in slot_in]
    gates_f = gate_table(logits_f, routes_f)
    my_gates_f = my_gates(gates_f)
    blocked = lambda a: a.reshape(seqs, ranks, seq_dev)
    slots_at = jnp.arange(capacity, dtype=jnp.int32)[:, None]
    first_at = jnp.arange(ranks, dtype=jnp.int32)[:, None, None] * capacity
    match_f = [blocked(target_f[:, j])[:, :, None, :] == first_at + slots_at for j in range(local)]
    weights_f = [
        jnp.sum(
            jnp.where(match_f[j], blocked(my_gates_f[:, j])[:, :, None, :], 0.0), axis=-1
        ).reshape(slot_rows, 1)
        for j in range(local)
    ]

    slot_grads_f, dots_f = [], []
    grads_gate, grads_up, grads_down, down_slots = [], [], [], []
    pieces = tie([[part[0] for part in placed] for placed in arrived[0]], slot_in[0])
    arrived[0] = [
        [(got, *part[1:]) for got, part in zip(held, placed)]
        for held, placed in zip(pieces, arrived[0])
    ]
    next_w = rows_in(arrived[0][0]), rows_in(arrived[0][1])
    for j in range(local):
        x = slot_in[j]
        gate_w, up_w = next_w
        down_w = rows_in(arrived[j][2])
        scaled, grad_gate, grad_up, slot_grad, dots = expert_step(
            x, slot_grad_out[j], weights_f[j], gate_w, up_w, down_w, rows_each
        )
        dots = dots.reshape(seqs, ranks, capacity, 2).transpose(1, 3, 0, 2).reshape(ranks, -1)
        dots_f.append(dots.astype(BF16))
        if j + 1 < local:
            slot_grad = tie(slot_grad, *held_back)
            got, (down_in,) = exchange_group(group_d[j], *held_back)
            gate_in, up_in = arrived[j + 1][0][0], arrived[j + 1][1][0]
            next_w = rows_in([gate_in]), rows_in([up_in])
            made = tie((scaled, grad_gate, grad_up), *held_back)
            grads_down.append(dot_f32("rf,rd->fd", made[0], slot_grad_out[j]).astype(BF16))
            grads_gate.append(dot_f32("rf,rd->fd", made[1], slot_in[j]).astype(BF16))
            grads_up.append(dot_f32("rf,rd->fd", made[2], slot_in[j]).astype(BF16))
            down = jnp.dot(made[0], down_w, preferred_element_type=F32).astype(BF16)
            down_slots.append(down)
            done = (grads_down[-1], grads_gate[-1], grads_up[-1], down, next_w)
            arrived[j + 1][2].append((tie(got, done), *down_in[1:]))
        slot_grads_f.append(slot_grad)

    def grad_part(grad, half=None):
        first, rows = halves(grad.shape[0], half)

        def piece_for(n):
            return lax.dynamic_slice(grad, (first, n * depth), (rows, depth))

        return piece_for, rows

    def whole_grad(placed):
        flat = [part for parts in placed for part in parts]
        counts = [len(parts) for parts in placed]
        pieces = [tuple(part[0][m] for part in flat) for m in range(ranks)]

        def body(m, ins, outs):
            first = 0
            for j, held in enumerate(counts):
                spans = [part[1:] for part in placed[j]]
                place_rows(outs[0], j, ins[first : first + held], spans, F32)
                first += held

        rows = hidden_units
        out = ((experts, rows, depth), F32, (local, rows, depth), lambda b: (b, 0, 0))
        return assemble(pieces, body, [out], "whole_grad")[0]

    def sublayer_back(own_in, inverse_all, gain, router, gates_all, logits_all, dots, inner, dhidden):
        gates = own_tokens(gates_all)
        inverse = own_tokens(inverse_all)
        dlogits = gates * (dots - jnp.sum(gates * dots, axis=-1, keepdims=True))
        dlogits = dlogits.astype(BF16)
        gain_own = own_features(gain)
        router_own = lax.dynamic_slice_in_dim(router, col_at * share, share, 0)
        normed = own_in.astype(F32) * inverse
        hidden = (normed * gain_own).astype(BF16)
        dhidden = dhidden + dot_f32("ste,fe->stf", dlogits, router_own)
        grad_router = dot_f32("ste,stf->ef", dlogits, hidden)
        grad_gain = jnp.sum(dhidden * normed, axis=(0, 1))
        dn = dhidden * gain_own
        inner = inner + jnp.sum(dlogits.astype(F32) * own_tokens(logits_all), axis=-1)
        grad = inverse * (dn - normed * (inner / width)[..., None])
        return grad, jnp.concatenate([grad_router, grad_gain[None]], axis=0)

    first_grads = (grads_down, grads_gate, grads_up)
    if local == 1:
        first_grads = ([scaled], [grad_gate], [grad_up])
        for grads, rows in zip(first_grads, (slot_grad_out[0], slot_in[0], slot_in[0])):
            grads[0] = dot_f32("rf,rd->fd", grads[0], rows).astype(BF16)
    grads_down, grads_gate, grads_up = first_grads
    got, (down_first,) = exchange_group(
        cut_group(grad_part(grads_down[0], 0)), *[part[0][-1] for part in arrived[-1][2]]
    )
    slot_grads_f[-1] = tie(slot_grads_f[-1], *got)
    group_a = cut_group(grad_part(grads_down[0], 1), grad_part(grads_gate[0], 0))
    group_b = cut_group(grad_part(grads_gate[0], 1), grad_part(grads_up[0]))
    got, (down_second, gate_first) = exchange_group(group_a, slot_grads_f[-1])
    per_row = dots_f[0].shape[1]
    dot_rows = round_up(per_row, share) // share
    under = round_up(ranks * dot_rows, 16)
    own_rows, own_dots = [], []
    for rows, dots in zip(slot_grads_f, dots_f):
        dots = jnp.pad(dots, ((0, 0), (0, dot_rows * share - per_row)))
        dots = jnp.pad(dots.reshape(-1, share), ((0, under - ranks * dot_rows), (0, 0)))
        dots = jnp.tile(dots, (1, width // share))
        own = sum_cols(jnp.concatenate([rows, dots], axis=0))
        own_rows.append(own[:slot_rows])
        own_dots.append(own[slot_rows : slot_rows + ranks * dot_rows].reshape(ranks, -1, share))
    own_rows = tie(jnp.concatenate(own_rows, axis=0), *got)
    made = tie((scaled, grad_gate, grad_up), own_rows)
    if local > 1:
        grads_down.append(dot_f32("rf,rd->fd", made[0], slot_grad_out[-1]).astype(BF16))
        grads_gate.append(dot_f32("rf,rd->fd", made[1], slot_in[-1]).astype(BF16))
        grads_up.append(dot_f32("rf,rd->fd", made[2], slot_in[-1]).astype(BF16))
    down_slots.append(jnp.dot(made[0], down_w, preferred_element_type=F32).astype(BF16))
    grad_home, dots_home = rows_home(
        own_rows, seqs, capacity, jnp.concatenate(own_dots, axis=1)
    )
    dhidden_f = come_home(home_f, grad_home)
    dots_home = dots_home.reshape(ranks, local, -1)[..., :per_row].astype(F32)
    dots_home = dots_home.reshape(experts, 2, seqs, capacity, 1).transpose(1, 2, 0, 3, 4)
    match_home = home_f.reshape(seqs, experts, capacity, seq_dev).astype(F32)
    dots_home = jnp.sum(dots_home * match_home, axis=3).swapaxes(2, 3)
    grad_mid, small_f = sublayer_back(
        mid_low, inverse_f, gain_ffn, router_ffn, gates_f, logits_f,
        dots_home[0], jnp.sum(dots_home[1], axis=-1), dhidden_f,
    )
    grad_mid = grad_out.astype(F32) + grad_mid

    mid_grad_rows = gather_rows(grad_mid.astype(BF16))
    mid_grad_rows = tie(mid_grad_rows, group_b, *grads_down, *grads_gate, *grads_up, *down_slots)
    group_c = [
        cut_group(grad_part(grads_down[j]), grad_part(grads_gate[j], 0)) for j in range(1, local)
    ]
    group_d = [
        cut_group(grad_part(grads_gate[j], 1), grad_part(grads_up[j])) for j in range(1, local)
    ]
    mid_grad_all = gather_cols(mid_grad_rows).reshape(count, width)
    got, (gate_second, up_got) = exchange_group(group_b, mid_grad_rows)
    down_slots = jnp.concatenate(down_slots, axis=0)
    mid_grad_all = tie(mid_grad_all, down_slots, group_c, group_d, *got)
    down_parts, gate_parts = [[down_first, down_second]], [[gate_first, gate_second]]
    up_parts = [[up_got]]
    down_slots = tie(down_slots, mid_grad_all)
    down_own = sum_cols(down_slots)
    grad_raw = dot_f32("rd,fd->rf", mid_grad_all, out_cat)
    early = []
    for j in range(1, local):
        got, (down_got, gate_first) = exchange_group(group_c[j - 1], mid_grad_all)
        down_parts.append([down_got])
        gate_parts.append([gate_first])
        early += got
    into, dots_a = attend_back(
        qkv, target_a, kblk, log_totals, att_plain, seq3(grad_raw), my_gates_a.swapaxes(1, 2),
        cosine, sine, rows_each, heads,
    )
    placed = jnp.zeros((seqs, ranks, experts, seq_dev), F32)
    dots_a = dots_a.reshape(seqs, ranks, seq_dev, local + 1).swapaxes(2, 3)
    placed = lax.dynamic_update_slice_in_dim(placed, dots_a[:, :, :local], row_at * local, 2)
    extra = jnp.concatenate([placed, dots_a[:, :, local:]], axis=2).astype(BF16)
    extra = extra.reshape(seqs * ranks, -1)
    held = extra.shape[1]
    under = round_up(held, 16 * share) // share
    extra = jnp.pad(extra, ((0, 0), (0, under * share - held)))
    token_part = spread(
        into.reshape(seqs * ranks, seq_dev, -1), query_w, extra.reshape(-1, under, share)
    ).reshape(seqs, -1, width)
    token_part = tie(token_part, down_own, *early)
    last = []
    for j in range(1, local):
        got, (gate_second, up_got) = exchange_group(group_d[j - 1], token_part)
        gate_parts[j].append(gate_second)
        up_parts.append([up_got])
        last += got
    att_scaled = tie(att_scaled, *last[1:2]).reshape(count, -1)
    grad_out_cat = dot_f32("rf,rd->fd", att_scaled, mid_grad_all).astype(BF16)
    down_home, _ = rows_home(tie(down_own, token_part), seqs, capacity)
    part = lax.psum_scatter(token_part, "col", scatter_dimension=2, tiled=True)
    into = tie(into, *last[1:2]).reshape(count, -1)
    grad_query_cat = dot_f32("rd,rf->df", hidden_a, into).astype(BF16)
    out_pieces = exchange_pieces(cut_pieces(grad_part(grad_out_cat)[0]), *last[1:2])
    part = tie(part, *last, down_home, grad_query_cat, *out_pieces[1:2])
    own = lax.psum_scatter(part, "row", scatter_dimension=1, tiled=True)
    def out_grad_body(m, ins, outs):
        for j in range(local):
            for h in range(heads):
                at = (h * local + j) * HEAD_DIM
                piece = ins[0][at : at + HEAD_DIM].astype(F32)
                outs[0][j, h * HEAD_DIM : (h + 1) * HEAD_DIM] = piece

    grad_out_own = assemble(
        [(p,) for p in out_pieces],
        out_grad_body,
        [((experts, head_cols, depth), F32, (local, head_cols, depth), lambda b: (b, 0, 0))],
        "out_grad",
    )[0]
    gate_all, up_all, down_all = (whole_grad(p) for p in (gate_parts, up_parts, down_parts))
    own = tie(own, gate_all, up_all, down_all)
    dhidden_a = own[:, :seq_dev].astype(F32)
    dots_a = own[:, seq_dev:].reshape(seqs, -1)[:, :held].astype(F32)
    dots_a = dots_a.reshape(seqs, experts + 1, seq_dev).swapaxes(1, 2)

    def query_part(half):
        rows = depth // 2
        return cut_pieces(
            lambda n: lax.dynamic_slice_in_dim(grad_query_cat, n * depth + half * rows, rows, 0)
        )

    query_first = exchange_pieces(query_part(0), part)
    logits_a = logits_a.reshape(seqs, seq_len, experts)
    grad_in, small_a = sublayer_back(
        block_in, seq3(inverse_a), gain_attn, router_attn, gates_a, logits_a,
        dots_a[..., :experts], dots_a[..., experts], dhidden_a,
    )
    grad_in = grad_mid + grad_in
    block_out = (mid + come_home(home_f, down_home)).astype(BF16)

    smalls = jnp.concatenate([small_a, small_f], axis=0)
    high = smalls.astype(BF16)
    smalls = jnp.stack([high, (smalls - high.astype(F32)).astype(BF16)]).reshape(-1)
    held = smalls.shape[0]
    under = round_up(held, 16 * made_cols) // made_cols
    smalls = jnp.pad(smalls, (0, under * made_cols - held)).reshape(under, made_cols)
    query_second = exchange_pieces(
        [jnp.concatenate([piece, smalls], axis=0) for piece in query_part(1)]
    )
    smalls = sum(piece[depth // 2 :].astype(F32) for piece in query_second)
    smalls = jnp.sum(smalls.reshape(-1)[:held].reshape(2, -1, share), axis=0)
    smalls = lax.all_gather(smalls, "col", axis=1, tiled=True)
    def query_grad_body(m, ins, outs):
        for h in range(heads):
            columns = slice(h * HEAD_DIM, (h + 1) * HEAD_DIM)
            for p in range(parts):
                at = (h * parts + p) * HEAD_DIM
                for half in range(2):
                    rows = slice(half * (depth // 2), (half + 1) * (depth // 2))
                    piece = ins[half][: depth // 2, at : at + HEAD_DIM].astype(F32)
                    if p < local:
                        outs[0][p, rows, columns] = piece
                    elif m == 0:
                        outs[1 + p - local][rows, columns] = piece
                    else:
                        total = outs[1 + p - local][rows, columns] + piece
                        outs[1 + p - local][rows, columns] = total

    shared = ((depth, head_cols), F32, (depth, head_cols), lambda b: (0, 0))
    grad_query_own, grad_key_own, grad_value_own = assemble(
        list(zip(query_first, query_second)),
        query_grad_body,
        [
            ((experts, depth, head_cols), F32, (local, depth, head_cols), lambda b: (b, 0, 0)),
            shared,
            shared,
        ],
        "query_grad",
    )
    return (
        block_out,
        grad_in,
        smalls[experts],
        smalls[2 * experts + 1],
        smalls[:experts].T,
        smalls[experts + 1 : 2 * experts + 1].T,
        grad_query_own,
        grad_key_own,
        grad_value_own,
        grad_out_own,
        gate_all.swapaxes(1, 2),
        up_all.swapaxes(1, 2),
        down_all,
    )


def solution(mesh):
    in_specs = (
        P(None, "row", "col"),
        P(None, "row", "col"),
        P(),
        P(),
        P(),
        P(),
        P(None, "row", "col"),
        P("row", "col"),
        P("row", "col"),
        P(None, "col", "row"),
        P(None, "row", "col"),
        P(None, "row", "col"),
        P(None, "col", "row"),
        P(None, "row", None),
        P(None, "row", None),
        P(None, "row", None),
        P(None, "row", None),
        P(),
    )
    out_specs = (
        P(None, "row", "col"),
        P(None, "row", "col"),
        P(),
        P(),
        P(),
        P(),
        P(None, "row", "col"),
        P("row", "col"),
        P("row", "col"),
        P(None, "col", "row"),
        P(None, "row", "col"),
        P(None, "row", "col"),
        P(None, "col", "row"),
    )
    return jax.shard_map(
        per_device, mesh=mesh, in_specs=in_specs, out_specs=out_specs, check_vma=False
    )
```

```python
from functools import partial
import math

import jax
import jax.numpy as jnp
from jax import lax
from jax.experimental import pallas as pl
from jax.experimental.pallas import tpu as pltpu
from jax.sharding import PartitionSpec as P

HEAD_DIM = 128
EPSILON = 1e-05
ROPE_BASE = 10000.0
MASKED_SCORE = -1e30
BF16 = jnp.bfloat16
F32 = jnp.float32


def dot_f32(spec, left, right):
    return jnp.einsum(spec, left, right, preferred_element_type=F32)


def tie(value, *others):
    return lax.optimization_barrier((value, others))[0]


def rope_tables(length):
    half_width = HEAD_DIM // 2
    frequency = jnp.exp(
        -math.log(ROPE_BASE) * jnp.arange(half_width, dtype=F32) * (2.0 / HEAD_DIM)
    )
    angles = jnp.arange(length, dtype=jnp.int32).astype(F32)[:, None] * frequency
    cosine, sine = jnp.cos(angles), jnp.sin(angles)
    return (
        jnp.concatenate([cosine, cosine], axis=-1),
        jnp.concatenate([-sine, sine], axis=-1),
    )


def expert_ranks(pairs, order, expert):
    names, places = (jnp.concatenate([a[0], a[1]], axis=-1) for a in (pairs, order))
    ahead = jnp.logical_and(
        places[..., None, :] < places[..., :, None], names[..., None, :] == expert
    )
    rank = jnp.sum(ahead.astype(F32), axis=-1).astype(jnp.int32)
    chosen = jnp.where(names == expert, rank, -1)
    half = chosen.shape[-1] // 2
    return jnp.maximum(chosen[..., :half], chosen[..., half:])


def all_ranks(pairs, order):
    names, places = (jnp.concatenate([a[0], a[1]], axis=-1) for a in (pairs, order))
    ahead = jnp.logical_and(
        places[..., None, :] < places[..., :, None], names[..., None, :] == names[..., :, None]
    )
    rank = jnp.sum(ahead.astype(F32), axis=-1).astype(jnp.int32)
    half = rank.shape[-1] // 2
    return jnp.stack([rank[..., :half], rank[..., half:]])


def slot_match(pairs, ranks, expert, capacity):
    rank_here = jnp.max(jnp.where(pairs == expert, ranks, -1), axis=0)
    slots = jnp.arange(capacity, dtype=jnp.int32)[:, None]
    return rank_here[..., None, :] == slots


def gate_table(logits, routes):
    ids = jnp.arange(logits.shape[-1], dtype=jnp.int32)
    chosen = jnp.any(routes[..., None] == ids, axis=0)
    masked = jnp.where(chosen, logits, MASKED_SCORE)
    top = jnp.max(masked, axis=-1, keepdims=True)
    exps = jnp.where(chosen, jnp.exp(masked - top), 0.0)
    return exps / jnp.sum(exps, axis=-1, keepdims=True)


def normalize_rows(wide):
    inverse = lax.rsqrt(jnp.mean(wide * wide, axis=-1, keepdims=True) + EPSILON)
    return (wide * inverse, inverse)


def roll_half(values):
    return pltpu.roll(values, HEAD_DIM // 2, 1)


def project_kernel(
    rotated, x_ref, gain_ref, router_ref, weight_ref, cos_ref, sin_ref,
    hidden_ref, inverse_ref, logits_ref, out_ref,
):
    normed, inverse = normalize_rows(x_ref[...].astype(F32))
    hidden = (normed * gain_ref[...]).astype(BF16)
    hidden_ref[...] = hidden
    inverse_ref[...] = inverse
    logits_ref[...] = jnp.dot(hidden, router_ref[...], preferred_element_type=F32)
    made = jnp.dot(hidden, weight_ref[...], preferred_element_type=F32)
    cosine, sine = cos_ref[...], sin_ref[...]
    for at, turn in enumerate(rotated):
        columns = slice(at * HEAD_DIM, (at + 1) * HEAD_DIM)
        one = made[:, columns]
        if turn:
            one = one * cosine + roll_half(one) * sine
        out_ref[:, columns] = one.astype(BF16)


def project(x, gain, router, weight, cosine, sine, rotated):
    count, width = x.shape
    experts, cols = router.shape[1], weight.shape[1]
    length = cosine.shape[0]
    tile = 512
    row = lambda n: pl.BlockSpec((tile, n), lambda i: (i, 0))
    whole = lambda a: pl.BlockSpec(a.shape, lambda i: (0, 0))
    table = pl.BlockSpec((tile, HEAD_DIM), lambda i: (lax.rem(i, length // tile), 0))
    return pl.pallas_call(
        partial(project_kernel, rotated),
        grid=(count // tile,),
        in_specs=[row(width), pl.BlockSpec((1, width), lambda i: (0, 0)), whole(router),
                  whole(weight), table, table],
        out_specs=[row(width), row(1), row(experts), row(cols)],
        out_shape=[
            jax.ShapeDtypeStruct((count, width), BF16),
            jax.ShapeDtypeStruct((count, 1), F32),
            jax.ShapeDtypeStruct((count, experts), F32),
            jax.ShapeDtypeStruct((count, cols), BF16),
        ],
        compiler_params=pltpu.CompilerParams(vmem_limit_bytes=48 * 1024 * 1024),
        cost_estimate=pl.CostEstimate(
            flops=2 * count * width * cols,
            bytes_accessed=4 * count * width + 2 * count * cols,
            transcendentals=count,
        ),
        name="project",
    )(x, gain.reshape(1, width), router, weight, cosine, sine)


def scores_of(q, k, qblk, kblk):
    raw = lax.dot_general(q, k, (((1,), (1,)), ((), ())), preferred_element_type=F32)
    return jnp.where(kblk <= qblk, raw * HEAD_DIM ** (-0.5), MASKED_SCORE)


def head_part(ref, at):
    return ref[0, :, at * HEAD_DIM : (at + 1) * HEAD_DIM]


def pick_rows(match, tokens):
    return jnp.dot(match, tokens, preferred_element_type=F32).astype(BF16)


def put_rows(match, rows):
    first = (((0,), (0,)), ((), ()))
    return lax.dot_general(match, rows, first, preferred_element_type=F32)


def slot_rows_of(target_ref, kblk, rows):
    local, length = target_ref.shape[1:]
    at = lax.broadcasted_iota(jnp.int32, (rows, length), 0)
    found = [target_ref[0, j : j + 1] == at for j in range(local)]
    blocks = [
        jnp.sum(jnp.where(m, kblk.astype(F32), 0.0), axis=-1, keepdims=True) for m in found
    ]
    return found, [jnp.where(m, 1.0, 0.0).astype(BF16) for m in found], blocks


def attend_kernel(
    rows, qkv_ref, target_ref, gate_ref, kblk_ref, slot_ref, plain_ref, scaled_ref, lse_ref
):
    local = target_ref.shape[1]
    kblk = kblk_ref[0]
    found, match, blocks = slot_rows_of(target_ref, kblk, rows)
    q = jnp.concatenate([pick_rows(match[j], head_part(qkv_ref, j)) for j in range(local)], axis=0)
    k, v = head_part(qkv_ref, local), head_part(qkv_ref, local + 1)
    scores = scores_of(q, k, jnp.concatenate(blocks, axis=0), kblk.astype(F32))
    top = jnp.max(scores, axis=-1, keepdims=True)
    exps = jnp.exp(scores - top)
    total = jnp.sum(exps, axis=-1, keepdims=True)
    probs = (exps * (1.0 / total)).astype(BF16)
    out = jnp.dot(probs, v, preferred_element_type=F32).astype(BF16)
    lse_ref[0, 0] = top + jnp.log(total)
    for j in range(local):
        here = out[j * rows : (j + 1) * rows]
        gate = jnp.sum(jnp.where(found[j], gate_ref[0, j : j + 1], 0.0), axis=-1, keepdims=True)
        scaled = (here.astype(F32) * gate).astype(BF16)
        columns = slice(j * HEAD_DIM, (j + 1) * HEAD_DIM)
        slot_ref[j, 0] = scaled
        plain_ref[0, :, columns] = put_rows(match[j], here).astype(BF16)
        scaled_ref[0, :, columns] = put_rows(match[j], scaled).astype(BF16)


def attend(qkv, target, gates, kblk, rows, heads):
    seqs, length, cols = qkv.shape
    local = target.shape[1]
    token = lambda n: pl.BlockSpec((1, length, n * HEAD_DIM), lambda s, h: (s, 0, h))
    lane = lambda n: pl.BlockSpec((1, n, length), lambda s, h: (s, 0, 0))
    of_tokens = jax.ShapeDtypeStruct((seqs, length, heads * local * HEAD_DIM), BF16)
    total = local * rows
    return pl.pallas_call(
        partial(attend_kernel, rows),
        grid=(seqs, heads),
        in_specs=[token(local + 2), lane(local), lane(local), lane(1)],
        out_specs=[
            pl.BlockSpec((local, 1, rows, HEAD_DIM), lambda s, h: (0, s, 0, h)),
            token(local),
            token(local),
            pl.BlockSpec((1, 1, total, 1), lambda s, h: (s, h, 0, 0)),
        ],
        out_shape=[
            jax.ShapeDtypeStruct((local, seqs, rows, heads * HEAD_DIM), BF16),
            of_tokens,
            of_tokens,
            jax.ShapeDtypeStruct((seqs, heads, total, 1), F32),
        ],
        compiler_params=pltpu.CompilerParams(vmem_limit_bytes=56 * 1024 * 1024),
        cost_estimate=pl.CostEstimate(
            flops=12 * seqs * heads * total * length * HEAD_DIM,
            bytes_accessed=4 * qkv.size,
            transcendentals=seqs * heads * total * length,
        ),
        name="attend",
    )(qkv, target, gates, kblk)


def attend_back_kernel(
    rows, qkv_ref, target_ref, kblk_ref, lse_ref, plain_ref, raw_ref, gate_ref, cos_ref, sin_ref,
    out_ref, dots_ref,
):
    local = target_ref.shape[1]
    kblk = kblk_ref[0]
    _, match, blocks = slot_rows_of(target_ref, kblk, rows)
    q = jnp.concatenate([pick_rows(match[j], head_part(qkv_ref, j)) for j in range(local)], axis=0)
    k, v = head_part(qkv_ref, local), head_part(qkv_ref, local + 1)
    grads, dots = [], []
    for j in range(local):
        raw = head_part(raw_ref, j)
        gated = (raw * gate_ref[0, :, j : j + 1]).astype(BF16)
        grads.append(pick_rows(match[j], gated))
        dots.append(jnp.sum(raw * head_part(plain_ref, j).astype(F32), axis=-1, keepdims=True))
    g = jnp.concatenate(grads, axis=0)
    scores = scores_of(q, k, jnp.concatenate(blocks, axis=0), kblk.astype(F32))
    probs = jnp.exp(scores - lse_ref[0, 0])
    grad = lax.dot_general(g, v, (((1,), (1,)), ((), ())), preferred_element_type=F32)
    inner = jnp.sum(probs * grad, axis=-1, keepdims=True)
    grad_scores = (probs * (grad - inner) * HEAD_DIM ** (-0.5)).astype(BF16)
    dq = jnp.dot(grad_scores, k, preferred_element_type=F32)
    cosine, sine = cos_ref[...], sin_ref[...]
    inner_sum = 0.0
    turn = lambda value: (value * cosine - roll_half(value) * sine).astype(BF16)
    for j in range(local):
        here = dq[j * rows : (j + 1) * rows]
        high = here.astype(BF16)
        low = (here - high.astype(F32)).astype(BF16)
        placed = put_rows(match[j], high) + put_rows(match[j], low)
        out_ref[0, :, j * HEAD_DIM : (j + 1) * HEAD_DIM] = turn(placed)
        inner_sum = inner_sum + placed * head_part(qkv_ref, j).astype(F32)
    dk = put_rows(grad_scores, q)
    out_ref[0, :, local * HEAD_DIM : (local + 1) * HEAD_DIM] = turn(dk)
    dv = put_rows(probs.astype(BF16), g)
    out_ref[0, :, (local + 1) * HEAD_DIM : (local + 2) * HEAD_DIM] = dv.astype(BF16)
    inner_sum = inner_sum + dk * k.astype(F32) + dv * v.astype(F32)
    dots.append(jnp.sum(inner_sum, axis=-1, keepdims=True))
    for at in range(local + 1):

        @pl.when(pl.program_id(1) == 0)
        def _():
            dots_ref[0, :, at : at + 1] = dots[at]

        @pl.when(pl.program_id(1) > 0)
        def _():
            dots_ref[0, :, at : at + 1] = dots_ref[0, :, at : at + 1] + dots[at]


def attend_back(qkv, target, kblk, lse, plain, raw, gate_cols, cosine, sine, rows, heads):
    seqs, length, cols = qkv.shape
    local = target.shape[1]
    token = lambda n: pl.BlockSpec((1, length, n * HEAD_DIM), lambda s, h: (s, 0, h))
    lane = lambda n: pl.BlockSpec((1, n, length), lambda s, h: (s, 0, 0))
    total = local * rows
    column = pl.BlockSpec((1, length, local), lambda s, h: (s, 0, 0))
    table = pl.BlockSpec((length, HEAD_DIM), lambda s, h: (0, 0))
    return pl.pallas_call(
        partial(attend_back_kernel, rows),
        grid=(seqs, heads),
        in_specs=[
            token(local + 2),
            lane(local),
            lane(1),
            pl.BlockSpec((1, 1, total, 1), lambda s, h: (s, h, 0, 0)),
            token(local),
            token(local),
            column,
            table,
            table,
        ],
        out_specs=[
            token(local + 2),
            pl.BlockSpec((1, length, local + 1), lambda s, h: (s, 0, 0)),
        ],
        out_shape=[
            jax.ShapeDtypeStruct(qkv.shape, BF16),
            jax.ShapeDtypeStruct((seqs, length, local + 1), F32),
        ],
        compiler_params=pltpu.CompilerParams(vmem_limit_bytes=60 * 1024 * 1024),
        cost_estimate=pl.CostEstimate(
            flops=0,
            bytes_accessed=4 * qkv.size,
            transcendentals=0,
        ),
        name="attend_back",
    )(qkv, target, kblk, lse, plain, raw, gate_cols, cosine, sine)


def dispatch_body(target_ref, tokens, out_refs):
    rows = out_refs[0].shape[1]
    at = lax.broadcasted_iota(jnp.int32, (rows, tokens.shape[0]), 0)
    for j, out_ref in enumerate(out_refs):
        match = jnp.where(target_ref[0, j : j + 1] == at, 1.0, 0.0).astype(BF16)
        out_ref[0] = pick_rows(match, tokens[...])


def dispatch_kernel(x_ref, target_ref, *out_refs):
    dispatch_body(target_ref, x_ref.at[0], out_refs)


def norm_dispatch_kernel(step, x_ref, target_ref, gain_ref, router_ref, *refs):
    *out_refs, inverse_ref, logits_ref, hidden_ref = refs
    for first in range(0, x_ref.shape[1], step):
        rows = slice(first, first + step)
        normed, inverse = normalize_rows(x_ref[0, rows].astype(F32))
        hidden = (normed * gain_ref[...]).astype(BF16)
        hidden_ref[rows] = hidden
        inverse_ref[0, rows] = inverse
        logits_ref[0, rows] = jnp.dot(hidden, router_ref[...], preferred_element_type=F32)
    dispatch_body(target_ref, hidden_ref, out_refs)


def dispatch(x, target, rows, norm=None):
    seqs, length, width = x.shape
    local = target.shape[1]
    token = lambda n: pl.BlockSpec((1, length, n), lambda s: (s, 0, 0))
    in_specs = [token(width), pl.BlockSpec((1, local, length), lambda s: (s, 0, 0))]
    out_specs = [pl.BlockSpec((1, rows, width), lambda s: (s, 0, 0)) for _ in range(local)]
    out_shape = [jax.ShapeDtypeStruct((seqs, rows, width), BF16) for _ in range(local)]
    args, kernel, scratch = [x, target], dispatch_kernel, []
    if norm is not None:
        gain, router = norm
        experts = router.shape[1]
        in_specs += [
            pl.BlockSpec((1, width), lambda s: (0, 0)),
            pl.BlockSpec(router.shape, lambda s: (0, 0)),
        ]
        out_specs += [token(1), token(experts)]
        out_shape += [
            jax.ShapeDtypeStruct((seqs, length, 1), F32),
            jax.ShapeDtypeStruct((seqs, length, experts), F32),
        ]
        args += [gain.reshape(1, width), router]
        kernel = partial(norm_dispatch_kernel, 256)
        scratch = [pltpu.VMEM((length, width), BF16)]
    return pl.pallas_call(
        kernel,
        grid=(seqs,),
        in_specs=in_specs,
        out_specs=out_specs,
        out_shape=out_shape,
        scratch_shapes=scratch,
        compiler_params=pltpu.CompilerParams(vmem_limit_bytes=56 * 1024 * 1024),
        cost_estimate=pl.CostEstimate(
            flops=0,
            bytes_accessed=2 * x.size,
            transcendentals=0,
        ),
        name="dispatch",
    )(*args)


def expert_kernel(
    x_ref, grad_ref, weight_ref, gate_ref, up_ref, down_ref,
    scaled_ref, grad_gate_ref, grad_up_ref, back_ref, dots_ref,
):
    last = (((1,), (1,)), ((), ()))
    x, weight = x_ref[...], weight_ref[...]
    gate_pre = lax.dot_general(x, gate_ref[...], last, preferred_element_type=F32)
    up_pre = lax.dot_general(x, up_ref[...], last, preferred_element_type=F32)
    raw = lax.dot_general(grad_ref[...], down_ref[...], last, preferred_element_type=F32)
    gate_sig = jax.nn.sigmoid(gate_pre)
    gate_silu = gate_pre * gate_sig
    activated = gate_silu * up_pre
    scaled_ref[...] = (activated * weight).astype(BF16)
    grad_act = raw * weight
    grad_gate = grad_act * up_pre * (gate_sig * (1.0 + gate_pre * (1.0 - gate_sig)))
    grad_gate = grad_gate.astype(BF16)
    grad_up = (grad_act * gate_silu).astype(BF16)
    grad_gate_ref[...] = grad_gate
    grad_up_ref[...] = grad_up
    back = jnp.dot(grad_gate, gate_ref[...], preferred_element_type=F32)
    back = back + jnp.dot(grad_up, up_ref[...], preferred_element_type=F32)
    back_ref[...] = back.astype(BF16)
    inner = grad_gate.astype(F32) * gate_pre + grad_up.astype(F32) * up_pre
    dots_ref[:, 0:1] = jnp.sum(raw * activated, axis=-1, keepdims=True)
    dots_ref[:, 1:2] = jnp.sum(inner, axis=-1, keepdims=True)


def expert_step(x, grad, weight, gate_w, up_w, down_w, tile):
    count, width = x.shape
    units = gate_w.shape[0]
    row = lambda n: pl.BlockSpec((tile, n), lambda i: (i, 0))
    whole = pl.BlockSpec((units, width), lambda i: (0, 0))
    shape = lambda n, dtype=BF16: jax.ShapeDtypeStruct((count, n), dtype)
    return pl.pallas_call(
        expert_kernel,
        grid=(count // tile,),
        in_specs=[row(width), row(width), row(1), whole, whole, whole],
        out_specs=[row(units), row(units), row(units), row(width), row(2)],
        out_shape=[shape(units), shape(units), shape(units), shape(width), shape(2, F32)],
        compiler_params=pltpu.CompilerParams(vmem_limit_bytes=56 * 1024 * 1024),
        cost_estimate=pl.CostEstimate(
            flops=0,
            bytes_accessed=6 * width * units,
            transcendentals=0,
        ),
        name="expert_step",
    )(x, grad, weight, gate_w, up_w, down_w)


def gather_rows(own):
    return lax.all_gather(own, "row", axis=1, tiled=True)


def gather_cols(rows):
    return lax.all_gather(rows, "col", axis=2, tiled=True)


def exchange(parts):
    return lax.all_to_all(parts, "row", 0, 0)


def cut_pieces(piece_for):
    ranks, row = lax.axis_size("row"), lax.axis_index("row")
    return [piece_for(lax.rem(row + m, ranks)) for m in range(ranks)]


def exchange_pieces(pieces, *after):
    ranks = lax.axis_size("row")
    got = pieces[:1]
    for m in range(1, ranks):
        steps = [(i, (i + m) % ranks) for i in range(ranks)]
        got.append(lax.ppermute(tie(pieces[m], *after), "row", steps))
    return got


def cut_group(*parts):
    pieces = cut_pieces(lambda n: jnp.concatenate([piece_for(n) for piece_for, _ in parts], axis=0))
    return pieces, [rows for _, rows in parts]


def exchange_group(group, *after):
    pieces, counts = group
    got = exchange_pieces(pieces, *after)
    placed, first = [], 0
    for rows in counts:
        placed.append((got, first, rows))
        first += rows
    return got, placed


def assemble(pieces, body, outs, name):
    ranks, each = len(pieces), len(pieces[0])

    def kernel(row_ref, *refs):
        for m in range(ranks):

            @pl.when(pl.program_id(0) == m)
            def _():
                body(m, refs[m * each : (m + 1) * each], refs[ranks * each :])

    def at(index):
        return lambda m, row: index(lax.rem(row[0] - m + ranks, ranks))

    flat = [a for piece in pieces for a in piece]
    whole = lambda a: pl.BlockSpec(a.shape, lambda m, row: (0,) * a.ndim)
    return pl.pallas_call(
        kernel,
        grid_spec=pltpu.PrefetchScalarGridSpec(
            num_scalar_prefetch=1,
            grid=(ranks,),
            in_specs=[whole(a) for a in flat],
            out_specs=[pl.BlockSpec(block, at(index)) for _, _, block, index in outs],
        ),
        out_shape=[jax.ShapeDtypeStruct(shape, dtype) for shape, dtype, _, _ in outs],
        compiler_params=pltpu.CompilerParams(vmem_limit_bytes=48 * 1024 * 1024),
        cost_estimate=pl.CostEstimate(
            flops=0, bytes_accessed=4 * sum(a.size for a in flat), transcendentals=0
        ),
        name=name,
    )(lax.axis_index("row").astype(jnp.int32).reshape(1), *flat)


def place_rows(outs, at, refs, spans, dtype):
    to = 0
    for ref, (first, rows) in zip(refs, spans):
        piece = ref[first : first + rows].astype(dtype)
        if at is None:
            outs[to : to + rows] = piece
        else:
            outs[at, to : to + rows] = piece
        to += rows


def spread_kernel(into_ref, weight_ref, extra_ref, out_ref):
    last = (((1,), (1,)), ((), ()))
    tokens, copies = into_ref.shape[1], out_ref.shape[2] // extra_ref.shape[2]
    rows = lax.dot_general(into_ref[0], weight_ref[...], last, preferred_element_type=F32)
    out_ref[0, :tokens] = rows.astype(BF16)
    share = extra_ref.shape[2]
    for at in range(copies):
        out_ref[0, tokens:, at * share : (at + 1) * share] = extra_ref[0]


def spread(into, weight, extra):
    blocks, tokens, depth = into.shape
    width = weight.shape[0]
    rows = tokens + extra.shape[1]
    block = lambda a: pl.BlockSpec((1, *a.shape[1:]), lambda i: (i, 0, 0))
    return pl.pallas_call(
        spread_kernel,
        grid=(blocks,),
        in_specs=[block(into), pl.BlockSpec(weight.shape, lambda i: (0, 0)), block(extra)],
        out_specs=pl.BlockSpec((1, rows, width), lambda i: (i, 0, 0)),
        out_shape=jax.ShapeDtypeStruct((blocks, rows, width), BF16),
        compiler_params=pltpu.CompilerParams(vmem_limit_bytes=48 * 1024 * 1024),
        cost_estimate=pl.CostEstimate(
            flops=0,
            bytes_accessed=2 * blocks * rows * width,
            transcendentals=0,
        ),
        name="spread",
    )(into, weight, extra)


def sum_cols(rows):
    return lax.psum_scatter(rows, "col", scatter_dimension=1, tiled=True)


def round_up(count, unit):
    return -(-count // unit) * unit


def rows_home(own, seqs, capacity, extra=None):
    ranks, share = lax.axis_size("row"), own.shape[-1]
    rows = own.reshape(-1, seqs, ranks, capacity, share).transpose(2, 1, 0, 3, 4)
    rows = rows.reshape(ranks, -1, share)
    count = rows.shape[1]
    if extra is not None:
        rows = jnp.concatenate([rows, extra], axis=1)
    got = exchange(rows)
    home = got[:, :count].reshape(ranks, seqs, -1, share).swapaxes(0, 1)
    return home.reshape(seqs, -1, share), got[:, count:]


def per_device(
    block_in,
    grad_out,
    gain_attn,
    gain_ffn,
    router_attn,
    router_ffn,
    w_query,
    key_weight,
    value_weight,
    w_out,
    w_gate,
    w_up,
    w_down,
    routes_attn,
    routes_ffn,
    order_attn,
    order_ffn,
    block_ids,
):
    seqs, seq_dev, share = block_in.shape
    experts, depth, head_cols = w_query.shape
    capacity = 18 * seq_dev // (8 * experts)
    heads = head_cols // HEAD_DIM
    hidden_units = w_gate.shape[2]
    width = gain_attn.shape[0]
    seq_len = block_ids.shape[1]
    ranks = lax.axis_size("row")
    local = experts // ranks
    row_at, col_at = lax.axis_index("row"), lax.axis_index("col")
    slot_rows = seqs * ranks * capacity
    count = seqs * seq_len

    def own_features(whole):
        return lax.dynamic_slice_in_dim(whole, col_at * share, share, whole.ndim - 1)

    def own_tokens(whole):
        return lax.dynamic_slice_in_dim(whole, row_at * seq_dev, seq_dev, 1)

    def by_pair(table):
        return table.reshape(seqs, seq_dev, 2).transpose(2, 0, 1)

    small = jnp.stack([by_pair(t) for t in (routes_attn, order_attn, routes_ffn, order_ffn)])
    split = jnp.concatenate([small % 256, small[1::2] // 256]).astype(BF16)
    split = split.transpose(2, 0, 1, 3).reshape(seqs, -1)
    held = split.shape[1]
    table_rows = round_up(held, 16 * share) // share
    split = jnp.pad(split, ((0, 0), (0, table_rows * share - held)))
    in_rows = gather_rows(
        jnp.concatenate([block_in, split.reshape(seqs, table_rows, share)], axis=1)
    ).reshape(seqs, ranks, -1, share)
    split = in_rows[:, :, seq_dev:].reshape(seqs, ranks, -1)[..., :held].astype(jnp.int32)
    split = split.reshape(seqs, ranks, 6, 2, seq_dev).transpose(2, 3, 0, 1, 4)
    small_all = [split[0], split[1] + 256 * split[4], split[2], split[3] + 256 * split[5]]
    in_rows = in_rows[:, :, :seq_dev].reshape(seqs, seq_len, share)

    def halves(height, half):
        return (0, height) if half is None else (half * (height // 2), height // 2)

    def expert_part(weight, j, half=None):
        first, rows = halves(weight.shape[1], half)

        def piece_for(n):
            at = (n * local + j, first, 0)
            return lax.dynamic_slice(weight, at, (1, rows, weight.shape[2]))[0]

        return piece_for, rows

    def rows_in(placed):
        spans = [part[1:] for part in placed]
        pieces = [tuple(part[0][m] for part in placed) for m in range(ranks)]

        def body(m, ins, outs):
            place_rows(outs[0], None, ins, spans, BF16)

        out = ((hidden_units, width), BF16, (hidden_units, depth), lambda b: (0, b))
        return assemble(pieces, body, [out], "rows_in")[0]

    w_gate, w_up = w_gate.swapaxes(1, 2), w_up.swapaxes(1, 2)

    def group_in(weight):
        grouped = weight.reshape(ranks, local, *weight.shape[1:])
        return lambda n: lax.dynamic_index_in_dim(grouped, n, 0, keepdims=False)

    parts = local + 2
    key_value = jnp.stack([key_weight, value_weight])

    query_for = group_in(w_query)
    cosine, sine = rope_tables(seq_len)
    query_parts = cut_pieces(lambda n: jnp.concatenate([query_for(n), key_value]))
    out_parts = cut_pieces(group_in(w_out))
    group_a = cut_group(expert_part(w_gate, 0), expert_part(w_up, 0, 0))
    group_b = cut_group(expert_part(w_up, 0, 1), expert_part(w_down, 0))
    group_c = [cut_group(expert_part(w_gate, j), expert_part(w_up, j)) for j in range(1, local)]
    group_d = [cut_group(expert_part(w_down, j)) for j in range(1, local)]
    in_rows = tie(
        in_rows, cosine, sine, query_parts, out_parts, group_a, group_b, group_c, group_d
    )
    query_got = exchange_pieces(query_parts, in_rows)

    def query_body(m, ins, outs):
        for h in range(heads):
            for p in range(parts):
                at = (h * parts + p) * HEAD_DIM
                piece = ins[0][p, :, h * HEAD_DIM : (h + 1) * HEAD_DIM]
                outs[0][:, at : at + HEAD_DIM] = piece

    made_cols = heads * parts * HEAD_DIM
    query_w = assemble(
        [(p,) for p in query_got],
        query_body,
        [((width, made_cols), BF16, (depth, made_cols), lambda b: (b, 0))],
        "query_in",
    )[0]

    mine = [row_at * local + j for j in range(local)]

    def tokens_to_slots(pairs, order):
        first = jnp.arange(ranks, dtype=jnp.int32)[:, None] * capacity
        out = []
        for e in mine:
            rank = expert_ranks(pairs, order, e)
            kept = jnp.logical_and(rank >= 0, rank < capacity)
            out.append(jnp.where(kept, first + rank, -1).reshape(seqs, seq_len))
        return jnp.stack(out, axis=1)

    target_a = tokens_to_slots(small_all[0], small_all[1])
    target_f = tokens_to_slots(small_all[2], small_all[3])
    routes_a = small_all[0].reshape(2, seqs, seq_len)
    routes_f = small_all[2].reshape(2, seqs, seq_len)

    def home_match(pairs, order):
        ranks_here = all_ranks(pairs, order)
        every = [slot_match(pairs, ranks_here, e, capacity) for e in range(experts)]
        return jnp.concatenate(every, axis=1).astype(BF16)

    home_a = home_match(small[0], small[1])
    home_f = home_match(small[2], small[3])

    def come_home(match, rows):
        return dot_f32("sct,scf->stf", match, rows)

    def my_gates(gates):
        return jnp.stack(
            [lax.dynamic_index_in_dim(gates, e, 2, keepdims=False) for e in mine], axis=1
        )

    in_all = gather_cols(in_rows).reshape(count, width)
    grad_sent = jnp.einsum("sct,stf->scf", home_f, grad_out)
    grad_sent = grad_sent.reshape(seqs, ranks, local, capacity, share).transpose(1, 2, 0, 3, 4)
    in_all = tie(
        in_all, target_a, target_f, home_a, home_f, grad_sent
    )
    rotated = ([True] * (local + 1) + [False]) * heads
    hidden_a, inverse_a, logits_a, qkv = project(
        in_all, gain_attn, router_attn, query_w, cosine, sine, rotated
    )
    qkv = qkv.reshape(seqs, seq_len, -1)
    out_got = exchange_pieces(out_parts, in_all)
    qkv = tie(qkv, *out_got)
    grad_rows = exchange(tie(grad_sent, qkv))
    gates_a = gate_table(
        logits_a.reshape(seqs, seq_len, experts), routes_a
    )
    my_gates_a = my_gates(gates_a)
    kblk = block_ids.reshape(seqs, 1, seq_len)
    rows_each = ranks * capacity
    att_slot, att_plain, att_scaled, log_totals = attend(
        qkv, target_a, my_gates_a, kblk, rows_each, heads
    )
    def out_body(m, ins, outs):
        for j in range(local):
            outs[1][j] = ins[0][j]
            for h in range(heads):
                at = (h * local + j) * HEAD_DIM
                outs[0][at : at + HEAD_DIM] = ins[0][j, h * HEAD_DIM : (h + 1) * HEAD_DIM]

    rows_cat = heads * local * HEAD_DIM
    out_cat, out_w = assemble(
        [(p,) for p in tie(out_got, att_slot)],
        out_body,
        [
            ((rows_cat, width), BF16, (rows_cat, depth), lambda b: (0, b)),
            ((local, head_cols, width), BF16, (local, head_cols, depth), lambda b: (0, 0, b)),
        ],
        "out_in",
    )

    out_slots = dot_f32(
        "jrf,jfd->jrd", att_slot.reshape(local, slot_rows, head_cols), out_w
    ).astype(BF16)
    out_slots = tie(out_slots.reshape(-1, width), grad_rows)
    got, (gate_in, up_first) = exchange_group(group_a, *out_got)
    out_own = tie(sum_cols(out_slots), *got)
    out_home, _ = rows_home(out_own, seqs, capacity)
    mid = block_in.astype(F32) + come_home(home_a, out_home)

    mid_low = mid.astype(BF16)
    mid_rows = gather_rows(mid_low)
    mid_all = gather_cols(mid_rows).reshape(count, width)
    got, (up_second, down_in) = exchange_group(group_b, mid_rows)
    mid_all = tie(mid_all, *got)
    arrived = [([gate_in], [up_first, up_second], [down_in])]
    grad_rows = tie(grad_rows, mid_all).transpose(1, 2, 0, 3, 4)
    grad_rows = grad_rows.reshape(local, slot_rows, share)
    slot_grad_out = [
        lax.all_gather(grad_rows[j], "col", axis=1, tiled=True) for j in range(local)
    ]
    held_back = []
    for j in range(1, local):
        got, (gate_in, up_in) = exchange_group(group_c[j - 1], mid_all)
        held_back += got
        arrived.append(([gate_in], [up_in], []))
    seq3 = lambda a: a.reshape(seqs, seq_len, -1)
    *slot_in, inverse_f, logits_f = dispatch(
        seq3(mid_all), target_f, rows_each, (gain_ffn, router_ffn)
    )
    slot_in = [x.reshape(slot_rows, width) for x in slot_in]
    gates_f = gate_table(logits_f, routes_f)
    my_gates_f = my_gates(gates_f)
    blocked = lambda a: a.reshape(seqs, ranks, seq_dev)
    slots_at = jnp.arange(capacity, dtype=jnp.int32)[:, None]
    first_at = jnp.arange(ranks, dtype=jnp.int32)[:, None, None] * capacity
    match_f = [blocked(target_f[:, j])[:, :, None, :] == first_at + slots_at for j in range(local)]
    weights_f = [
        jnp.sum(
            jnp.where(match_f[j], blocked(my_gates_f[:, j])[:, :, None, :], 0.0), axis=-1
        ).reshape(slot_rows, 1)
        for j in range(local)
    ]

    slot_grads_f, dots_f = [], []
    grads_gate, grads_up, grads_down, down_slots = [], [], [], []
    pieces = tie([[part[0] for part in placed] for placed in arrived[0]], slot_in[0])
    arrived[0] = [
        [(got, *part[1:]) for got, part in zip(held, placed)]
        for held, placed in zip(pieces, arrived[0])
    ]
    next_w = rows_in(arrived[0][0]), rows_in(arrived[0][1])
    for j in range(local):
        x = slot_in[j]
        gate_w, up_w = next_w
        down_w = rows_in(arrived[j][2])
        scaled, grad_gate, grad_up, slot_grad, dots = expert_step(
            x, slot_grad_out[j], weights_f[j], gate_w, up_w, down_w, rows_each
        )
        dots = dots.reshape(seqs, ranks, capacity, 2).transpose(1, 3, 0, 2).reshape(ranks, -1)
        dots_f.append(dots.astype(BF16))
        if j + 1 < local:
            slot_grad = tie(slot_grad, *held_back)
            got, (down_in,) = exchange_group(group_d[j], *held_back)
            gate_in, up_in = arrived[j + 1][0][0], arrived[j + 1][1][0]
            next_w = rows_in([gate_in]), rows_in([up_in])
            made = tie((scaled, grad_gate, grad_up), *held_back)
            grads_down.append(dot_f32("rf,rd->fd", made[0], slot_grad_out[j]).astype(BF16))
            grads_gate.append(dot_f32("rf,rd->fd", made[1], slot_in[j]).astype(BF16))
            grads_up.append(dot_f32("rf,rd->fd", made[2], slot_in[j]).astype(BF16))
            down = jnp.dot(made[0], down_w, preferred_element_type=F32).astype(BF16)
            down_slots.append(down)
            done = (grads_down[-1], grads_gate[-1], grads_up[-1], down, next_w)
            arrived[j + 1][2].append((tie(got, done), *down_in[1:]))
        slot_grads_f.append(slot_grad)

    def grad_part(grad, half=None):
        first, rows = halves(grad.shape[0], half)

        def piece_for(n):
            return lax.dynamic_slice(grad, (first, n * depth), (rows, depth))

        return piece_for, rows

    def whole_grad(placed):
        flat = [part for parts in placed for part in parts]
        counts = [len(parts) for parts in placed]
        pieces = [tuple(part[0][m] for part in flat) for m in range(ranks)]

        def body(m, ins, outs):
            first = 0
            for j, held in enumerate(counts):
                spans = [part[1:] for part in placed[j]]
                place_rows(outs[0], j, ins[first : first + held], spans, F32)
                first += held

        rows = hidden_units
        out = ((experts, rows, depth), F32, (local, rows, depth), lambda b: (b, 0, 0))
        return assemble(pieces, body, [out], "whole_grad")[0]

    def sublayer_back(own_in, inverse_all, gain, router, gates_all, logits_all, dots, inner, dhidden):
        gates = own_tokens(gates_all)
        inverse = own_tokens(inverse_all)
        dlogits = gates * (dots - jnp.sum(gates * dots, axis=-1, keepdims=True))
        dlogits = dlogits.astype(BF16)
        gain_own = own_features(gain)
        router_own = lax.dynamic_slice_in_dim(router, col_at * share, share, 0)
        normed = own_in.astype(F32) * inverse
        hidden = (normed * gain_own).astype(BF16)
        dhidden = dhidden + dot_f32("ste,fe->stf", dlogits, router_own)
        grad_router = dot_f32("ste,stf->ef", dlogits, hidden)
        grad_gain = jnp.sum(dhidden * normed, axis=(0, 1))
        dn = dhidden * gain_own
        inner = inner + jnp.sum(dlogits.astype(F32) * own_tokens(logits_all), axis=-1)
        grad = inverse * (dn - normed * (inner / width)[..., None])
        return grad, jnp.concatenate([grad_router, grad_gain[None]], axis=0)

    first_grads = (grads_down, grads_gate, grads_up)
    if local == 1:
        first_grads = ([scaled], [grad_gate], [grad_up])
        for grads, rows in zip(first_grads, (slot_grad_out[0], slot_in[0], slot_in[0])):
            grads[0] = dot_f32("rf,rd->fd", grads[0], rows).astype(BF16)
    grads_down, grads_gate, grads_up = first_grads
    got, (down_first,) = exchange_group(
        cut_group(grad_part(grads_down[0], 0)), *[part[0][-1] for part in arrived[-1][2]]
    )
    slot_grads_f[-1] = tie(slot_grads_f[-1], *got)
    group_a = cut_group(grad_part(grads_down[0], 1), grad_part(grads_gate[0], 0))
    group_b = cut_group(grad_part(grads_gate[0], 1), grad_part(grads_up[0]))
    got, (down_second, gate_first) = exchange_group(group_a, slot_grads_f[-1])
    per_row = dots_f[0].shape[1]
    dot_rows = round_up(per_row, share) // share
    under = round_up(ranks * dot_rows, 16)
    own_rows, own_dots = [], []
    for rows, dots in zip(slot_grads_f, dots_f):
        dots = jnp.pad(dots, ((0, 0), (0, dot_rows * share - per_row)))
        dots = jnp.pad(dots.reshape(-1, share), ((0, under - ranks * dot_rows), (0, 0)))
        dots = jnp.tile(dots, (1, width // share))
        own = sum_cols(jnp.concatenate([rows, dots], axis=0))
        own_rows.append(own[:slot_rows])
        own_dots.append(own[slot_rows : slot_rows + ranks * dot_rows].reshape(ranks, -1, share))
    own_rows = tie(jnp.concatenate(own_rows, axis=0), *got)
    made = tie((scaled, grad_gate, grad_up), own_rows)
    if local > 1:
        grads_down.append(dot_f32("rf,rd->fd", made[0], slot_grad_out[-1]).astype(BF16))
        grads_gate.append(dot_f32("rf,rd->fd", made[1], slot_in[-1]).astype(BF16))
        grads_up.append(dot_f32("rf,rd->fd", made[2], slot_in[-1]).astype(BF16))
    down_slots.append(jnp.dot(made[0], down_w, preferred_element_type=F32).astype(BF16))
    grad_home, dots_home = rows_home(
        own_rows, seqs, capacity, jnp.concatenate(own_dots, axis=1)
    )
    dhidden_f = come_home(home_f, grad_home)
    dots_home = dots_home.reshape(ranks, local, -1)[..., :per_row].astype(F32)
    dots_home = dots_home.reshape(experts, 2, seqs, capacity, 1).transpose(1, 2, 0, 3, 4)
    match_home = home_f.reshape(seqs, experts, capacity, seq_dev).astype(F32)
    dots_home = jnp.sum(dots_home * match_home, axis=3).swapaxes(2, 3)
    grad_mid, small_f = sublayer_back(
        mid_low, inverse_f, gain_ffn, router_ffn, gates_f, logits_f,
        dots_home[0], jnp.sum(dots_home[1], axis=-1), dhidden_f,
    )
    grad_mid = grad_out.astype(F32) + grad_mid

    mid_grad_rows = gather_rows(grad_mid.astype(BF16))
    mid_grad_rows = tie(mid_grad_rows, group_b, *grads_down, *grads_gate, *grads_up, *down_slots)
    group_c = [
        cut_group(grad_part(grads_down[j]), grad_part(grads_gate[j], 0)) for j in range(1, local)
    ]
    group_d = [
        cut_group(grad_part(grads_gate[j], 1), grad_part(grads_up[j])) for j in range(1, local)
    ]
    mid_grad_all = gather_cols(mid_grad_rows).reshape(count, width)
    got, (gate_second, up_got) = exchange_group(group_b, mid_grad_rows)
    down_slots = jnp.concatenate(down_slots, axis=0)
    mid_grad_all = tie(mid_grad_all, down_slots, group_c, group_d, *got)
    down_parts, gate_parts = [[down_first, down_second]], [[gate_first, gate_second]]
    up_parts = [[up_got]]
    down_slots = tie(down_slots, mid_grad_all)
    down_own = sum_cols(down_slots)
    grad_raw = dot_f32("rd,fd->rf", mid_grad_all, out_cat)
    early = []
    for j in range(1, local):
        got, (down_got, gate_first) = exchange_group(group_c[j - 1], mid_grad_all)
        down_parts.append([down_got])
        gate_parts.append([gate_first])
        early += got
    into, dots_a = attend_back(
        qkv, target_a, kblk, log_totals, att_plain, seq3(grad_raw), my_gates_a.swapaxes(1, 2),
        cosine, sine, rows_each, heads,
    )
    placed = jnp.zeros((seqs, ranks, experts, seq_dev), F32)
    dots_a = dots_a.reshape(seqs, ranks, seq_dev, local + 1).swapaxes(2, 3)
    placed = lax.dynamic_update_slice_in_dim(placed, dots_a[:, :, :local], row_at * local, 2)
    extra = jnp.concatenate([placed, dots_a[:, :, local:]], axis=2).astype(BF16)
    extra = extra.reshape(seqs * ranks, -1)
    held = extra.shape[1]
    under = round_up(held, 16 * share) // share
    extra = jnp.pad(extra, ((0, 0), (0, under * share - held)))
    token_part = spread(
        into.reshape(seqs * ranks, seq_dev, -1), query_w, extra.reshape(-1, under, share)
    ).reshape(seqs, -1, width)
    token_part = tie(token_part, down_own, *early)
    last = []
    for j in range(1, local):
        got, (gate_second, up_got) = exchange_group(group_d[j - 1], token_part)
        gate_parts[j].append(gate_second)
        up_parts.append([up_got])
        last += got
    att_scaled = tie(att_scaled, *last[1:2]).reshape(count, -1)
    grad_out_cat = dot_f32("rf,rd->fd", att_scaled, mid_grad_all).astype(BF16)
    down_home, _ = rows_home(tie(down_own, token_part), seqs, capacity)
    part = lax.psum_scatter(token_part, "col", scatter_dimension=2, tiled=True)
    into = tie(into, *last[1:2]).reshape(count, -1)
    grad_query_cat = dot_f32("rd,rf->df", hidden_a, into).astype(BF16)
    out_pieces = exchange_pieces(cut_pieces(grad_part(grad_out_cat)[0]), *last[1:2])
    part = tie(part, *last, down_home, grad_query_cat, *out_pieces[1:])
    own = lax.psum_scatter(part, "row", scatter_dimension=1, tiled=True)
    def out_grad_body(m, ins, outs):
        for j in range(local):
            for h in range(heads):
                at = (h * local + j) * HEAD_DIM
                piece = ins[0][at : at + HEAD_DIM].astype(F32)
                outs[0][j, h * HEAD_DIM : (h + 1) * HEAD_DIM] = piece

    grad_out_own = assemble(
        [(p,) for p in out_pieces],
        out_grad_body,
        [((experts, head_cols, depth), F32, (local, head_cols, depth), lambda b: (b, 0, 0))],
        "out_grad",
    )[0]
    gate_all, up_all, down_all = (whole_grad(p) for p in (gate_parts, up_parts, down_parts))
    own = tie(own, gate_all, up_all, down_all)
    dhidden_a = own[:, :seq_dev].astype(F32)
    dots_a = own[:, seq_dev:].reshape(seqs, -1)[:, :held].astype(F32)
    dots_a = dots_a.reshape(seqs, experts + 1, seq_dev).swapaxes(1, 2)

    def query_part(half):
        rows = depth // 2
        return cut_pieces(
            lambda n: lax.dynamic_slice_in_dim(grad_query_cat, n * depth + half * rows, rows, 0)
        )

    query_first = exchange_pieces(query_part(0), part)
    logits_a = logits_a.reshape(seqs, seq_len, experts)
    grad_in, small_a = sublayer_back(
        block_in, seq3(inverse_a), gain_attn, router_attn, gates_a, logits_a,
        dots_a[..., :experts], dots_a[..., experts], dhidden_a,
    )
    grad_in = grad_mid + grad_in
    block_out = (mid + come_home(home_f, down_home)).astype(BF16)

    smalls = jnp.concatenate([small_a, small_f], axis=0)
    high = smalls.astype(BF16)
    smalls = jnp.stack([high, (smalls - high.astype(F32)).astype(BF16)]).reshape(-1)
    held = smalls.shape[0]
    under = round_up(held, 16 * made_cols) // made_cols
    smalls = jnp.pad(smalls, (0, under * made_cols - held)).reshape(under, made_cols)
    query_second = exchange_pieces(
        [jnp.concatenate([piece, smalls], axis=0) for piece in query_part(1)]
    )
    smalls = sum(piece[depth // 2 :].astype(F32) for piece in query_second)
    smalls = jnp.sum(smalls.reshape(-1)[:held].reshape(2, -1, share), axis=0)
    smalls = lax.all_gather(smalls, "col", axis=1, tiled=True)
    def query_grad_body(m, ins, outs):
        for h in range(heads):
            columns = slice(h * HEAD_DIM, (h + 1) * HEAD_DIM)
            for p in range(parts):
                at = (h * parts + p) * HEAD_DIM
                for half in range(2):
                    rows = slice(half * (depth // 2), (half + 1) * (depth // 2))
                    piece = ins[half][: depth // 2, at : at + HEAD_DIM].astype(F32)
                    if p < local:
                        outs[0][p, rows, columns] = piece
                    elif m == 0:
                        outs[1 + p - local][rows, columns] = piece
                    else:
                        total = outs[1 + p - local][rows, columns] + piece
                        outs[1 + p - local][rows, columns] = total

    shared = ((depth, head_cols), F32, (depth, head_cols), lambda b: (0, 0))
    grad_query_own, grad_key_own, grad_value_own = assemble(
        list(zip(query_first, query_second)),
        query_grad_body,
        [
            ((experts, depth, head_cols), F32, (local, depth, head_cols), lambda b: (b, 0, 0)),
            shared,
            shared,
        ],
        "query_grad",
    )
    return (
        block_out,
        grad_in,
        smalls[experts],
        smalls[2 * experts + 1],
        smalls[:experts].T,
        smalls[experts + 1 : 2 * experts + 1].T,
        grad_query_own,
        grad_key_own,
        grad_value_own,
        grad_out_own,
        gate_all.swapaxes(1, 2),
        up_all.swapaxes(1, 2),
        down_all,
    )


def solution(mesh):
    in_specs = (
        P(None, "row", "col"),
        P(None, "row", "col"),
        P(),
        P(),
        P(),
        P(),
        P(None, "row", "col"),
        P("row", "col"),
        P("row", "col"),
        P(None, "col", "row"),
        P(None, "row", "col"),
        P(None, "row", "col"),
        P(None, "col", "row"),
        P(None, "row", None),
        P(None, "row", None),
        P(None, "row", None),
        P(None, "row", None),
        P(),
    )
    out_specs = (
        P(None, "row", "col"),
        P(None, "row", "col"),
        P(),
        P(),
        P(),
        P(),
        P(None, "row", "col"),
        P("row", "col"),
        P("row", "col"),
        P(None, "col", "row"),
        P(None, "row", "col"),
        P(None, "row", "col"),
        P(None, "col", "row"),
    )
    return jax.shard_map(
        per_device, mesh=mesh, in_specs=in_specs, out_specs=out_specs, check_vma=False
    )
```
